256 devices in a mesh: samp: 16 (over y_lo, x, core), cpg: 16 (over z, y_hi).
Axes of the slice: x: 4, y: 4 (y_hi: 2, y_lo: 2; y = y_hi * 2 + y_lo), z: 8, core: 2. Of those that a mesh axis runs over, the one named last changes fastest.
Arguments:
- responses: bfloat16 [1024, 16384], P('samp', 'cpg'), may hold values from -5 to 5
- weights: bfloat16 [1024, 16384], P('samp', 'cpg'), may hold values from 1 to 8
- phenotype: float32 [16384], P('cpg'), may hold values from -6 to 6
- eigvecs: bfloat16 [16384, 16384], P('cpg', 'samp'), may hold values from -0.046875 to 0.046875
- eigvals: float32 [16384], P('samp'), may hold values from 0.0001 to 1
- positions: int32 [1024], replicated, may hold values from 1 to 307200, as said below
- reaches: int32 [1024], P('cpg'), may hold values from 1 to 8
Outputs:
- smoothed: float32 [1024], P('cpg')
- log_scale: float32 [1024], P('cpg')
The draws below stay inside these ranges and needn't reach their ends.
Inputs may be any that keep to these rules, and one draw needn't show every extreme that they name: CpG m (from 0) lies at 300 m plus an offset of 1 to 300, so positions strictly increase and consecutive CpGs lie 1 to 599 base pairs apart.
All inputs are finite; a program needn't handle non-finite values.
Results may differ from the reference program's by a relative error of at most 0.0041.
Values may be sent and summed in bfloat16 or wider, within the bound.
No kernel may reach another device: no remote copies, remote signals or barrier semaphores. Data moves between devices by JAX's collectives and lax.ppermute only.
A program may use at most 64 MiB of HBM per device.

```python
import math
import jax
import jax.numpy as jnp
from jax import lax

N = 16384
ITERS = 4
HALO = 8
M = 1024


def draw_positions(key, part):
    offsets = jax.random.randint(key, (M,), 1, 301)
    index = jnp.arange(M, dtype=jnp.int32)
    offsets = jnp.where(index == 0, 1, offsets)
    offsets = jnp.where(index == M - 1, 300, offsets)
    return (300 * index + offsets).astype(jnp.int32)


def draw_working(key):
    root_key = jax.random.fold_in(key, 4049)
    weight_key = jax.random.fold_in(root_key, 1)
    noise_key = jax.random.fold_in(root_key, 2)
    excess_key = jax.random.fold_in(root_key, 3)
    weight_draw = jnp.exp(jax.random.uniform(weight_key, (M, N), jnp.float32, 0.0, jnp.log(8.0)))
    noise_draw = jnp.clip(jax.random.normal(noise_key, (M, N), jnp.float32), -4.0, 4.0)
    weight_draw = jnp.clip(weight_draw, 1.0, 8.0).astype(jnp.bfloat16)
    excess = 0.04 * jnp.exp(jax.random.uniform(excess_key, (M, 1), jnp.float32, 0.0, jnp.log(5.0)))
    row_scale = jnp.sqrt((1.0 + excess) / weight_draw.astype(jnp.float32))
    response_draw = jnp.clip(row_scale * noise_draw, -5.0, 5.0).astype(jnp.bfloat16)
    return (weight_draw, response_draw)


def draw_weights(key, part):
    return draw_working(key)[0]


def draw_responses(key, part):
    return draw_working(key)[1]


def plant(array, stream_key, smallest, top_value):
    spot = [jax.random.randint(jax.random.fold_in(stream_key, axis), (), 0, length) for axis, length in enumerate(array.shape)]
    widest = array.shape.index(max(array.shape))
    neighbour = spot[:widest] + [(spot[widest] + 1) % array.shape[widest]] + spot[widest + 1:]
    return array.at[tuple(spot)].set(smallest).at[tuple(neighbour)].set(top_value)


def steps_of(key, extent, split, low, high):
    factor_of = 1.0
    for axis_at, blocks in split:
        draws = jax.random.uniform(jax.random.fold_in(jax.random.fold_in(key, 6), axis_at), (blocks,), jnp.float32, low / len(split), high / len(split))
        factor_of = factor_of * jnp.repeat(jnp.exp(draws), extent[axis_at] // blocks).reshape((-1,) + (1,) * (len(extent) - 1 - axis_at))
    return factor_of


def noise(stream_key, shape, scale, most, shards=(), kind=jnp.bfloat16):
    array = scale * jax.random.normal(stream_key, shape, jnp.float32)
    if shards:
        array = array * steps_of(stream_key, shape, shards, -0.22, 0.18)
    return jnp.clip(array, -most, most).astype(kind)


def setup_inputs(seed: int = 0) -> dict:
    key_of = jax.random.split(jax.random.key(seed), 8)
    return {
        "responses": draw_responses(jax.random.fold_in(key_of[7], 71), 0),
        "weights": draw_weights(jax.random.fold_in(key_of[7], 71), 0),
        "phenotype": noise(key_of[2], (N,), 1.0, 6.0, ((0, 16),), jnp.float32),
        "eigvecs": noise(key_of[3], (N, N), N ** -0.5, 0.046875, ((0, 16), (1, 16))),
        "eigvals": jnp.clip(jnp.exp(math.log(1.0) - 9.2103404 * jax.random.uniform(key_of[4], (N,), jnp.float32) ** steps_of(key_of[4], (N,), ((0, 16),), -0.2, 0.2)), 0.0001, 1.0),
        "positions": draw_positions(jax.random.fold_in(key_of[7], 71), 0),
        "reaches": plant(jax.random.randint(key_of[6], (M,), 1, HALO + 1), jax.random.fold_in(key_of[6], 1), 1, HALO).astype(jnp.int32),
    }


EPSILON = 1e-06
band_width = 1000.0

def smooth_block(widened, places, present, reaches):
    block_len = reaches.shape[0]
    centre = places[HALO:HALO + block_len]
    total_sum = jnp.zeros((block_len,), jnp.float32)
    norm_sum = jnp.zeros((block_len,), jnp.float32)
    for offset in range(2 * HALO + 1):
        near_scores = widened[offset:offset + block_len]
        near_places = places[offset:offset + block_len]
        within = (abs(offset - HALO) <= reaches).astype(jnp.float32)
        kernel = present[offset:offset + block_len] * within * jnp.exp(-jnp.abs(near_places - centre) / band_width)
        total_sum = total_sum + kernel * near_scores
        norm_sum = norm_sum + kernel
    return total_sum / norm_sum

def reference(responses, weights, phenotype, eigvecs, eigvals, positions, reaches):
    root_weight = jnp.sqrt(weights.astype(jnp.float32))
    weighted = (root_weight * responses.astype(jnp.float32)).astype(jnp.bfloat16)
    design = (root_weight * phenotype[None, :]).astype(jnp.bfloat16)
    rot_resp = jnp.dot(weighted, eigvecs, preferred_element_type=jnp.float32)
    rot_design = jnp.dot(design, eigvecs, preferred_element_type=jnp.float32)
    eigen_part = eigvals[None, :]
    log_scale = jnp.zeros((M,), jnp.float32)
    for repeat in range(ITERS):
        inverse = 1.0 / (jnp.exp(log_scale)[:, None] * eigen_part + 1.0)
        crossed = lax.optimization_barrier(jnp.sum(rot_design * rot_resp * inverse, axis=1))
        energy = lax.optimization_barrier(jnp.sum(rot_design * rot_design * inverse, axis=1)) + EPSILON
        effect = crossed / energy
        residual = rot_resp - effect[:, None] * rot_design
        spread = lax.optimization_barrier(jnp.sum(eigen_part * residual * residual * inverse * inverse, axis=1))
        traced = lax.optimization_barrier(jnp.sum(eigen_part * inverse, axis=1))
        fisher = 0.5 * lax.optimization_barrier(jnp.sum(eigen_part * eigen_part * inverse * inverse, axis=1))
        gradient = 0.5 * (spread - traced)
        log_scale = log_scale + jnp.tanh(gradient / (jnp.exp(log_scale) * fisher))
    inverse = 1.0 / (jnp.exp(log_scale)[:, None] * eigen_part + 1.0)
    crossed = lax.optimization_barrier(jnp.sum(rot_design * rot_resp * inverse, axis=1))
    energy = lax.optimization_barrier(jnp.sum(rot_design * rot_design * inverse, axis=1)) + EPSILON
    zscore = crossed / jnp.sqrt(energy)
    widened = jnp.pad(zscore, HALO)
    places = jnp.pad(positions.astype(jnp.float32), HALO)
    present = jnp.pad(jnp.ones((M,), jnp.float32), HALO)
    smoothed = smooth_block(widened, places, present, reaches)
    return (smoothed, log_scale)
```

```python
import functools

import jax
import jax.numpy as jnp
from jax import lax
from jax.experimental import pallas as pl
from jax.experimental.pallas import tpu as pltpu
from jax.sharding import Mesh
from jax.sharding import PartitionSpec as P

ITERS = 4
HALO = 8
SAMP = ("samp_0", "samp_1", "samp_2")
CPG = ("cpg_0", "cpg_1")
PLANE = ("cpg_1", "samp_0", "samp_1")
LAYER = ("cpg_1", "samp_0", "samp_1", "samp_2")

EPSILON = 1e-06
band_width = 1000.0


def shifted(value, axis, by):
    peers = lax.axis_size(axis)
    return lax.ppermute(value, axis, [(i, (i + by) % peers) for i in range(peers)])


def weigh_kernel(resp_ref, weight_ref, trait_ref, out_ref):
    rows = resp_ref.shape[0]
    trait = trait_ref[...]
    for at in range(0, rows, 16):
        root = jnp.sqrt(weight_ref[at : at + 16, :].astype(jnp.float32))
        weighted = root * resp_ref[at : at + 16, :].astype(jnp.float32)
        design = root * trait
        upper = lax.broadcasted_iota(jnp.int32, (8, root.shape[1]), 0) < 4
        tiles = []
        for half in (0, 8):
            a, b = weighted[half : half + 8], design[half : half + 8]
            tiles.append(jnp.where(upper, a, pltpu.roll(b, 4, 0)))
            tiles.append(jnp.where(upper, pltpu.roll(a, 4, 0), b))
        out_ref[2 * at : 2 * at + 32, :] = jnp.concatenate(tiles, axis=0).astype(jnp.bfloat16)


def weigh(responses, weights, phenotype):
    rows, width = responses.shape
    return pl.pallas_call(
        weigh_kernel,
        out_shape=jax.ShapeDtypeStruct((2 * rows, width), jnp.bfloat16),
    )(responses, weights, phenotype[None, :])


def fit_kernel(sums_ref, values_ref, out_ref, rows_ref, inv_ref):
    sources, width = values_ref.shape
    half = 8 * sources
    step = 512
    starts = [(i, j) for i in range(sources) for j in range(0, width, step)]
    for i in range(0, sources, 2):
        rows_ref[8 * i : 8 * i + 16, :] = sums_ref[8 * i : 8 * i + 16, :].astype(
            jnp.float32
        ) + sums_ref[half + 8 * i : half + 8 * i + 16, :].astype(jnp.float32)

    def total(acc):
        acc = acc.reshape(8, step // 128, 128)
        return jnp.sum(jnp.sum(acc, axis=1), axis=1, keepdims=True)

    def sweep(scale, fit):
        zero = jnp.zeros((8, step), jnp.float32)

        def body(i, accs):
            crossed, energy, traced, fisher = accs
            at = pl.multiple_of(8 * i, 8)
            for j in range(0, width, step):
                own = rows_ref[pl.ds(at, 8), j : j + step]
                lam = jnp.broadcast_to(values_ref[pl.ds(i, 1), j : j + step], (8, step))
                inv = 1.0 / (scale * lam + 1.0)
                over = own * inv
                crossed = crossed + over * pltpu.roll(own, 4, 0)
                energy = energy + over * own
                if fit:
                    lev = lam * inv
                    traced = traced + lev
                    fisher = fisher + lev * lev
                    inv_ref[pl.ds(at, 8), j : j + step] = lev * inv
            return crossed, energy, traced, fisher

        crossed, energy, traced, fisher = lax.fori_loop(0, sources, body, (zero,) * 4)
        crossed, energy = total(crossed), total(energy)
        upper = lax.broadcasted_iota(jnp.int32, (8, 128), 0) < 4
        energy = jnp.broadcast_to(energy, (8, 128))
        energy = jnp.where(upper, pltpu.roll(energy, 4, 0), energy)[:, :1]
        return crossed, energy + EPSILON, total(traced), total(fisher)

    log_scale = jnp.zeros((8, 1), jnp.float32)
    for _ in range(ITERS):
        scale = jnp.exp(log_scale)
        crossed, energy, traced, fisher = sweep(scale, True)
        effect = crossed / energy

        def spread_body(i, acc):
            at = pl.multiple_of(8 * i, 8)
            for j in range(0, width, step):
                own = rows_ref[pl.ds(at, 8), j : j + step]
                residual = own - effect * pltpu.roll(own, 4, 0)
                acc = acc + inv_ref[pl.ds(at, 8), j : j + step] * residual * residual
            return acc

        spread = total(lax.fori_loop(0, sources, spread_body, jnp.zeros((8, step), jnp.float32)))
        gradient = 0.5 * (spread - traced)
        moved = log_scale + jnp.tanh(gradient / (scale * (0.5 * fisher)))
        moved = jnp.broadcast_to(moved, (8, 128))
        upper = lax.broadcasted_iota(jnp.int32, (8, 128), 0) < 4
        log_scale = jnp.where(upper, moved, pltpu.roll(moved, 4, 0))[:, :1]
    crossed, energy, _, _ = sweep(jnp.exp(log_scale), False)
    score = jnp.broadcast_to(crossed / jnp.sqrt(energy), (8, 128))
    upper = lax.broadcasted_iota(jnp.int32, (8, 128), 0) < 4
    out_ref[...] = jnp.where(upper, score, jnp.broadcast_to(log_scale, (8, 128)))


def fit(sums, values):
    rows, width = sums.shape
    return pl.pallas_call(
        fit_kernel,
        out_shape=jax.ShapeDtypeStruct((8, 128), jnp.float32),
        scratch_shapes=[
            pltpu.VMEM((rows // 2, width), jnp.float32),
            pltpu.VMEM((rows // 2, width), jnp.float32),
        ],
    )(sums, values)


def gather_plane(own):
    x, y = "samp_1", "samp_0"
    left = shifted(own, x, 1)
    right = shifted(own, x, -1)
    over = shifted(own, y, 1)
    far = shifted(left, x, 1)
    over_right = shifted(over, x, -1)
    over_left = shifted(left, y, 1)
    over_far = jnp.concatenate(
        [
            shifted(over_left[:48], x, 1),
            shifted(over_right[48:96], x, -1),
            shifted(far[96:], y, 1),
        ],
        axis=0,
    )
    return jnp.stack([own, right, far, left, over, over_right, over_far, over_left])


def smooth_block(widened, places, present, reaches):
    block_len = reaches.shape[0]
    centre = places[HALO : HALO + block_len]
    total_sum = jnp.zeros((block_len,), jnp.float32)
    norm_sum = jnp.zeros((block_len,), jnp.float32)
    for offset in range(2 * HALO + 1):
        near_scores = widened[offset : offset + block_len]
        near_places = places[offset : offset + block_len]
        within = (abs(offset - HALO) <= reaches).astype(jnp.float32)
        kernel = (
            present[offset : offset + block_len]
            * within
            * jnp.exp(-jnp.abs(near_places - centre) / band_width)
        )
        total_sum = total_sum + kernel * near_scores
        norm_sum = norm_sum + kernel
    return total_sum / norm_sum


def shards(responses, weights, phenotype, eigvecs, eigvals, positions, reaches):
    z, x, y = lax.axis_index("cpg_0"), lax.axis_index("samp_1"), lax.axis_index("samp_0")
    layers = lax.axis_size("cpg_0")
    with jax.named_scope("swap_eigvecs"):
        vecs = (eigvecs, shifted(eigvecs, "samp_2", 1))
        values = jnp.concatenate([eigvals, shifted(eigvals, "samp_2", 1)])
    with jax.named_scope("weigh"):
        own = weigh(responses, weights, phenotype)
    with jax.named_scope("gather_rows"):
        blocks = gather_plane(own)
    with jax.named_scope("gather_values"):
        everywhere = lax.all_to_all(
            jnp.broadcast_to(values[None], (8, *values.shape)), ("samp_0", "samp_1"), 0, 0, tiled=True
        )

    def term(ahead, q, lo=0, hi=None):
        dest = lax.rem(z + ahead + layers, layers)
        across, along = dest // 4, lax.rem(dest, 4)
        place = 4 * (across ^ y) + lax.rem(along - x + 4, 4)
        rows = lax.dynamic_index_in_dim(blocks, place, 0, keepdims=False)[lo:hi]
        return jnp.dot(rows, vecs[q], preferred_element_type=jnp.float32)

    with jax.named_scope("sum_layers"):
        far = layers // 2
        rows = own.shape[0]
        cut = rows // 2
        sent = {}
        for q in (0, 1):
            sent[q, 1] = shifted(term(far, q, 0, cut).astype(jnp.bfloat16), "cpg_0", 1)
            sent[q, -1] = shifted(term(far, q, cut, rows).astype(jnp.bfloat16), "cpg_0", -1)
        for ahead in range(far - 1, 0, -1):
            for q in (0, 1):
                for way in (1, -1):
                    got = sent[q, way].astype(jnp.float32)
                    if got.shape[0] < rows:
                        rest = jnp.zeros_like(got)
                        got = jnp.concatenate([got, rest] if way == 1 else [rest, got], axis=0)
                    total = (term(way * ahead, q) + got).astype(jnp.bfloat16)
                    sent[q, way] = shifted(total, "cpg_0", way)
        summed = jnp.concatenate(
            [
                (
                    term(0, q)
                    + sent[q, 1].astype(jnp.float32)
                    + sent[q, -1].astype(jnp.float32)
                ).astype(jnp.bfloat16)
                for q in (0, 1)
            ],
            axis=1,
        )
    with jax.named_scope("to_components"):
        sums = lax.all_to_all(
            summed.reshape(16, rows // 16, -1), PLANE, 0, 0, tiled=True
        ).reshape(rows, -1)
    with jax.named_scope("fit"):
        fitted = fit(sums, everywhere)[:, 0]
    with jax.named_scope("gather_scores"):
        spread_out = lax.all_to_all(
            jnp.broadcast_to(fitted[None], (32, 8)), LAYER, 0, 0, tiled=True
        )
        layer = spread_out.reshape(16, 2, 2, 4).transpose(2, 1, 0, 3).reshape(2, -1)
        scores, scales = layer[0], layer[1]
        up = [(i, i + 1) for i in range(layers - 1)]
        down = [(j, i) for i, j in up]
        before = lax.ppermute(scores[-HALO:], "cpg_0", up)
        after = lax.ppermute(scores[:HALO], "cpg_0", down)
    with jax.named_scope("smooth"):
        block_len = reaches.shape[0]
        high = lax.axis_index("cpg_1")
        widened = lax.dynamic_slice_in_dim(
            jnp.concatenate([before, scores, after]), high * block_len, block_len + 2 * HALO, 0
        )
        log_scale = lax.dynamic_slice_in_dim(scales, high * block_len, block_len, 0)
        base = lax.axis_index(CPG) * block_len
        total_cpgs = block_len * lax.axis_size(CPG)
        places = lax.dynamic_slice_in_dim(
            jnp.pad(positions.astype(jnp.float32), HALO), base, block_len + 2 * HALO, 0
        )
        global_index = base - HALO + jnp.arange(block_len + 2 * HALO, dtype=jnp.int32)
        present = ((global_index >= 0) & (global_index < total_cpgs)).astype(jnp.float32)
        smoothed = smooth_block(widened, places, present, reaches)
    return (smoothed, log_scale)


def solution(mesh):
    split = Mesh(
        mesh.devices.reshape(2, 4, 2, 8, 2), ("samp_0", "samp_1", "samp_2", "cpg_0", "cpg_1")
    )
    return jax.shard_map(
        shards,
        mesh=split,
        in_specs=(P(SAMP, CPG), P(SAMP, CPG), P(CPG), P(CPG, SAMP), P(SAMP), P(), P(CPG)),
        out_specs=(P(CPG), P(CPG)),
        check_vma=False,
    )
```

```python
import functools

import jax
import jax.numpy as jnp
from jax import lax
from jax.experimental import pallas as pl
from jax.experimental.pallas import tpu as pltpu
from jax.sharding import Mesh
from jax.sharding import PartitionSpec as P

ITERS = 4
HALO = 8
SAMP = ("samp_0", "samp_1", "samp_2")
CPG = ("cpg_0", "cpg_1")
PLANE = ("cpg_1", "samp_0", "samp_1")
FLOOR = ("samp_0", "samp_1")
LAYER = ("cpg_1", "samp_0", "samp_1", "samp_2")

EPSILON = 1e-06
band_width = 1000.0


def shifted(value, axis, by):
    peers = lax.axis_size(axis)
    return lax.ppermute(value, axis, [(i, (i + by) % peers) for i in range(peers)])


def fit_kernel(slot_ref, resp_ref, design_ref, values_ref, out_ref, r_ref, d_ref, w_ref):
    half, width = values_ref.shape
    lanes = 512
    for i in range(0, half, 16):
        for given, kept in ((resp_ref, r_ref), (design_ref, d_ref)):
            kept[i : i + 16, :] = given[i : i + 16, :].astype(jnp.float32) + given[
                half + i : half + i + 16, :
            ].astype(jnp.float32)
    blocks = [(i, j) for i in range(0, half, 8) for j in range(0, width, lanes)]

    def total(acc):
        acc = functools.reduce(jnp.add, [acc[:, k : k + 128] for k in range(0, lanes, 128)])
        acc = acc + pltpu.roll(acc, 4, 0)
        return jnp.broadcast_to(jnp.sum(acc, axis=1, keepdims=True), (8, 128))

    def wide(value):
        return jnp.concatenate([value] * (lanes // 128), axis=1)

    def sweep(scale, last):
        zero = jnp.zeros((8, lanes), jnp.float32)
        crossed, energy, traced, fisher = zero, zero, zero, zero
        scale = wide(scale)
        for i, j in blocks:
            at = (slice(i, i + 8), slice(j, j + lanes))
            lam, resp, design = values_ref[at], r_ref[at], d_ref[at]
            v = scale * lam + 1.0
            inv = pl.reciprocal(v, approx=True)
            inv = inv * (2.0 - v * inv)
            over = design * inv
            crossed = crossed + over * resp
            energy = energy + over * design
            if not last:
                lev = lam * inv
                traced = traced + lev
                fisher = fisher + lev * lev
                w_ref[at] = lev * inv
        return total(crossed), total(energy) + EPSILON, traced, fisher

    log_scale = jnp.zeros((8, 128), jnp.float32)
    for _ in range(ITERS):
        scale = jnp.exp(log_scale)
        crossed, energy, traced, fisher = sweep(scale, False)
        effect = wide(crossed / energy)
        spread = jnp.zeros((8, lanes), jnp.float32)
        for i, j in blocks:
            at = (slice(i, i + 8), slice(j, j + lanes))
            residual = r_ref[at] - effect * d_ref[at]
            spread = spread + w_ref[at] * residual * residual
        gradient = 0.5 * (total(spread) - total(traced))
        log_scale = log_scale + jnp.tanh(gradient / (scale * (0.5 * total(fisher))))
    crossed, energy, _, _ = sweep(jnp.exp(log_scale), True)
    score = crossed / jnp.sqrt(energy)
    lane = lax.broadcasted_iota(jnp.int32, (8, 128), 1)
    row = lax.broadcasted_iota(jnp.int32, (8, 128), 0)
    here = (row < 4) & (lane == 4 * slot_ref[0] + row)
    both = [jnp.sum(jnp.where(here, v, 0.0), axis=0, keepdims=True) for v in (score, log_scale)]
    out_ref[...] = jnp.broadcast_to(
        jnp.concatenate(both, axis=1)[None], (out_ref.shape[0], 1, 256)
    )


def fit(slot, resp, design, values):
    rows, width = resp.shape
    vmem = pl.BlockSpec(memory_space=pltpu.VMEM)
    return pl.pallas_call(
        fit_kernel,
        out_shape=jax.ShapeDtypeStruct((32, 1, 256), jnp.float32),
        in_specs=[pl.BlockSpec(memory_space=pltpu.SMEM), vmem, vmem, vmem],
        out_specs=vmem,
        scratch_shapes=[pltpu.VMEM((rows // 2, width), jnp.float32)] * 3,
        compiler_params=pltpu.CompilerParams(vmem_limit_bytes=16 * 1024 * 1024),
    )(slot, resp, design, values)


def smooth_block(widened, places, present, reaches):
    block_len = reaches.shape[0]
    centre = places[HALO : HALO + block_len]
    total_sum = jnp.zeros((block_len,), jnp.float32)
    norm_sum = jnp.zeros((block_len,), jnp.float32)
    for offset in range(2 * HALO + 1):
        near_scores = widened[offset : offset + block_len]
        near_places = places[offset : offset + block_len]
        within = (abs(offset - HALO) <= reaches).astype(jnp.float32)
        kernel = (
            present[offset : offset + block_len]
            * within
            * jnp.exp(-jnp.abs(near_places - centre) / band_width)
        )
        total_sum = total_sum + kernel * near_scores
        norm_sum = norm_sum + kernel
    return total_sum / norm_sum


def copies(value, axes):
    peers = lax.axis_size(axes)
    return lax.all_to_all(
        jnp.broadcast_to(value[None], (peers, *value.shape)), axes, 0, 0, tiled=True
    )


def shards(responses, weights, phenotype, eigvecs, eigvals, positions, reaches):
    z = lax.axis_index("cpg_0")
    layers = lax.axis_size("cpg_0")
    rows = responses.shape[0]
    with jax.named_scope("weigh"):
        root = jnp.sqrt(weights.astype(jnp.float32))
        weighted = (root * responses.astype(jnp.float32)).astype(jnp.bfloat16)
        design = (root * phenotype[None, :]).astype(jnp.bfloat16)
    with jax.named_scope("gather_rows"):
        blocks = [copies(weighted, FLOOR), copies(design, FLOOR)]
    with jax.named_scope("swap_eigvecs"):
        vecs = jnp.concatenate([eigvecs, shifted(eigvecs, "samp_2", 1)], axis=1)
        values = jnp.concatenate([eigvals, shifted(eigvals, "samp_2", 1)])

    def term(t, ahead, lo, hi):
        dest = lax.rem(z + ahead + layers, layers)
        block = lax.dynamic_index_in_dim(blocks[t], dest, 0, keepdims=False)[lo:hi]
        return jnp.dot(block, vecs, preferred_element_type=jnp.float32)

    far = layers // 2
    cut = rows // 2
    sent = {}

    def first(t):
        sent[t, 1] = shifted(term(t, far, 0, cut).astype(jnp.bfloat16), "cpg_0", 1)
        sent[t, -1] = shifted(term(t, far, cut, rows).astype(jnp.bfloat16), "cpg_0", -1)

    def onward(t, ahead):
        for way in (1, -1):
            got = sent[t, way].astype(jnp.float32)
            if got.shape[0] < rows:
                rest = jnp.zeros_like(got)
                got = jnp.concatenate([got, rest] if way == 1 else [rest, got], axis=0)
            total = (term(t, way * ahead, 0, rows) + got).astype(jnp.bfloat16)
            sent[t, way] = shifted(total, "cpg_0", way)

    def exchanged(t):
        total = term(t, 0, 0, rows)
        for way in (1, -1):
            total = total + sent[t, way].astype(jnp.float32)
        return lax.all_to_all(total.astype(jnp.bfloat16), PLANE, 0, 0, tiled=True)

    with jax.named_scope("sum_layers"):
        first(0)
        onward(0, 3)
        first(1)
        onward(0, 2)
        onward(1, 3)
        onward(0, 1)
        onward(1, 2)
        sums = [exchanged(0)]
        onward(1, 1)
        sums.append(exchanged(1))
    with jax.named_scope("gather_values"):
        everywhere = jnp.repeat(copies(values, FLOOR), 4, axis=0)
    with jax.named_scope("fit"):
        slot = lax.axis_index("samp_2") * 16 + lax.axis_index(PLANE)
        fitted = fit(slot.astype(jnp.int32)[None], *sums, everywhere)
    with jax.named_scope("gather_scores"):
        layer = jnp.sum(lax.all_to_all(fitted, LAYER, 0, 0, tiled=True), axis=(0, 1))
        up = [(i, i + 1) for i in range(layers - 1)]
        down = [(j, i) for i, j in up]
        before = lax.ppermute(layer, "cpg_0", up)[2 * rows - HALO : 2 * rows]
        after = lax.ppermute(layer, "cpg_0", down)[:HALO]
        scores, scales = layer[: 2 * rows], layer[2 * rows :]
    with jax.named_scope("smooth"):
        block_len = reaches.shape[0]
        high = lax.axis_index("cpg_1")
        widened = lax.dynamic_slice_in_dim(
            jnp.concatenate([before, scores, after]), high * block_len, block_len + 2 * HALO, 0
        )
        log_scale = lax.dynamic_slice_in_dim(scales, high * block_len, block_len, 0)
        base = lax.axis_index(CPG) * block_len
        total_cpgs = block_len * lax.axis_size(CPG)
        places = lax.dynamic_slice_in_dim(
            jnp.pad(positions.astype(jnp.float32), HALO), base, block_len + 2 * HALO, 0
        )
        global_index = base - HALO + jnp.arange(block_len + 2 * HALO, dtype=jnp.int32)
        present = ((global_index >= 0) & (global_index < total_cpgs)).astype(jnp.float32)
        smoothed = smooth_block(widened, places, present, reaches)
    return (smoothed, log_scale)


def solution(mesh):
    split = Mesh(
        mesh.devices.reshape(2, 4, 2, 8, 2), ("samp_0", "samp_1", "samp_2", "cpg_0", "cpg_1")
    )
    return jax.shard_map(
        shards,
        mesh=split,
        in_specs=(P(SAMP, CPG), P(SAMP, CPG), P(CPG), P(CPG, SAMP), P(SAMP), P(), P(CPG)),
        out_specs=(P(CPG), P(CPG)),
        check_vma=False,
    )
```

```python
import functools

import jax
import jax.numpy as jnp
from jax import lax
from jax.experimental import pallas as pl
from jax.experimental.pallas import tpu as pltpu
from jax.sharding import Mesh
from jax.sharding import PartitionSpec as P

ITERS = 4
HALO = 8
SAMP = ("samp_0", "samp_1", "samp_2")
CPG = ("cpg_0", "cpg_1")
PLANE = ("cpg_1", "samp_0", "samp_1")
FLOOR = ("samp_0", "samp_1")
LAYER = ("cpg_1", "samp_0", "samp_1", "samp_2")

EPSILON = 1e-06
band_width = 1000.0


def shifted(value, axis, by):
    peers = lax.axis_size(axis)
    return lax.ppermute(value, axis, [(i, (i + by) % peers) for i in range(peers)])


def weigh_kernel(resp_ref, weight_ref, trait_ref, out_ref):
    rows = resp_ref.shape[0]
    trait = trait_ref[...]
    for at in range(0, rows, 16):
        root = jnp.sqrt(weight_ref[at : at + 16, :].astype(jnp.float32))
        weighted = root * resp_ref[at : at + 16, :].astype(jnp.float32)
        design = root * trait
        upper = lax.broadcasted_iota(jnp.int32, (8, root.shape[1]), 0) < 4
        tiles = []
        for half in (0, 8):
            a, b = weighted[half : half + 8], design[half : half + 8]
            tiles.append(jnp.where(upper, a, pltpu.roll(b, 4, 0)))
            tiles.append(jnp.where(upper, pltpu.roll(a, 4, 0), b))
        out_ref[2 * at : 2 * at + 32, :] = jnp.concatenate(tiles, axis=0).astype(jnp.bfloat16)


def weigh(responses, weights, phenotype):
    rows, width = responses.shape
    return pl.pallas_call(
        weigh_kernel,
        out_shape=jax.ShapeDtypeStruct((2 * rows, width), jnp.bfloat16),
    )(responses, weights, phenotype[None, :])


def fit_kernel(slot_ref, sums_ref, values_ref, out_ref, r_ref, d_ref, w_ref):
    half, width = values_ref.shape
    lanes = 512
    upper = lax.broadcasted_iota(jnp.int32, (8, width), 0) < 4
    for i in range(0, half, 8):
        pair = sums_ref[2 * i : 2 * i + 16, :].astype(jnp.float32) + sums_ref[
            2 * (half + i) : 2 * (half + i) + 16, :
        ].astype(jnp.float32)
        a, b = pair[:8], pair[8:]
        r_ref[i : i + 8, :] = jnp.where(upper, a, pltpu.roll(b, 4, 0))
        d_ref[i : i + 8, :] = jnp.where(upper, pltpu.roll(a, 4, 0), b)
    blocks = [(i, j) for i in range(0, half, 8) for j in range(0, width, lanes)]

    def total(acc):
        acc = functools.reduce(jnp.add, [acc[:, k : k + 128] for k in range(0, lanes, 128)])
        acc = acc + pltpu.roll(acc, 4, 0)
        return jnp.broadcast_to(jnp.sum(acc, axis=1, keepdims=True), (8, 128))

    def wide(value):
        return jnp.concatenate([value] * (lanes // 128), axis=1)

    def sweep(scale, last):
        zero = jnp.zeros((8, lanes), jnp.float32)
        crossed, energy, traced, fisher = zero, zero, zero, zero
        scale = wide(scale)
        for i, j in blocks:
            at = (slice(i, i + 8), slice(j, j + lanes))
            lam, resp, design = values_ref[at], r_ref[at], d_ref[at]
            v = scale * lam + 1.0
            inv = pl.reciprocal(v, approx=True)
            inv = inv * (2.0 - v * inv)
            over = design * inv
            crossed = crossed + over * resp
            energy = energy + over * design
            if not last:
                lev = lam * inv
                traced = traced + lev
                fisher = fisher + lev * lev
                w_ref[at] = lev * inv
        return total(crossed), total(energy) + EPSILON, traced, fisher

    log_scale = jnp.zeros((8, 128), jnp.float32)
    for _ in range(ITERS):
        scale = jnp.exp(log_scale)
        crossed, energy, traced, fisher = sweep(scale, False)
        effect = wide(crossed / energy)
        spread = jnp.zeros((8, lanes), jnp.float32)
        for i, j in blocks:
            at = (slice(i, i + 8), slice(j, j + lanes))
            residual = r_ref[at] - effect * d_ref[at]
            spread = spread + w_ref[at] * residual * residual
        gradient = 0.5 * (total(spread) - total(traced))
        log_scale = log_scale + jnp.tanh(gradient / (scale * (0.5 * total(fisher))))
    crossed, energy, _, _ = sweep(jnp.exp(log_scale), True)
    score = crossed / jnp.sqrt(energy)
    lane = lax.broadcasted_iota(jnp.int32, (8, 128), 1)
    row = lax.broadcasted_iota(jnp.int32, (8, 128), 0)
    here = (row < 4) & (lane == 4 * slot_ref[0] + row)
    both = [jnp.sum(jnp.where(here, v, 0.0), axis=0, keepdims=True) for v in (score, log_scale)]
    out_ref[...] = jnp.broadcast_to(
        jnp.concatenate(both, axis=1)[None], (out_ref.shape[0], 1, 256)
    )


def fit(slot, sums, values):
    rows, width = values.shape
    vmem = pl.BlockSpec(memory_space=pltpu.VMEM)
    return pl.pallas_call(
        fit_kernel,
        out_shape=jax.ShapeDtypeStruct((32, 1, 256), jnp.float32),
        in_specs=[pl.BlockSpec(memory_space=pltpu.SMEM), vmem, vmem],
        out_specs=vmem,
        scratch_shapes=[pltpu.VMEM((rows, width), jnp.float32)] * 3,
        compiler_params=pltpu.CompilerParams(vmem_limit_bytes=16 * 1024 * 1024),
    )(slot, sums, values)


def gather_plane(own):
    x, y = "samp_1", "samp_0"
    left = shifted(own, x, 1)
    right = shifted(own, x, -1)
    over = shifted(own, y, 1)
    far = shifted(left, x, 1)
    over_right = shifted(over, x, -1)
    over_left = shifted(left, y, 1)
    over_far = jnp.concatenate(
        [
            shifted(over_left[:48], x, 1),
            shifted(over_right[48:96], x, -1),
            shifted(far[96:], y, 1),
        ],
        axis=0,
    )
    return jnp.stack([own, right, far, left, over, over_right, over_far, over_left])


def smooth_block(widened, places, present, reaches):
    block_len = reaches.shape[0]
    centre = places[HALO : HALO + block_len]
    total_sum = jnp.zeros((block_len,), jnp.float32)
    norm_sum = jnp.zeros((block_len,), jnp.float32)
    for offset in range(2 * HALO + 1):
        near_scores = widened[offset : offset + block_len]
        near_places = places[offset : offset + block_len]
        within = (abs(offset - HALO) <= reaches).astype(jnp.float32)
        kernel = (
            present[offset : offset + block_len]
            * within
            * jnp.exp(-jnp.abs(near_places - centre) / band_width)
        )
        total_sum = total_sum + kernel * near_scores
        norm_sum = norm_sum + kernel
    return total_sum / norm_sum


def copies(value, axes):
    peers = lax.axis_size(axes)
    return lax.all_to_all(
        jnp.broadcast_to(value[None], (peers, *value.shape)), axes, 0, 0, tiled=True
    )


def shards(responses, weights, phenotype, eigvecs, eigvals, positions, reaches):
    z, x, y = lax.axis_index("cpg_0"), lax.axis_index("samp_1"), lax.axis_index("samp_0")
    layers = lax.axis_size("cpg_0")
    with jax.named_scope("weigh"):
        own = weigh(responses, weights, phenotype)
    with jax.named_scope("gather_rows"):
        blocks = gather_plane(own)
    with jax.named_scope("swap_eigvecs"):
        low = lax.axis_index("samp_2") == 0
        other = shifted(eigvecs, "samp_2", 1)
        vecs = (jnp.where(low, eigvecs, other), jnp.where(low, other, eigvecs))
        other = shifted(eigvals, "samp_2", 1)
        values = jnp.where(low, jnp.concatenate([eigvals, other]), jnp.concatenate([other, eigvals]))
    rows = own.shape[0]

    def term(q, ahead, lo, hi):
        dest = lax.rem(z + ahead + layers, layers)
        across, along = dest // 4, lax.rem(dest, 4)
        place = 4 * (across ^ y) + lax.rem(along - x + 4, 4)
        block = lax.dynamic_index_in_dim(blocks, place, 0, keepdims=False)[lo:hi]
        return jnp.dot(block, vecs[q], preferred_element_type=jnp.float32)

    far = layers // 2
    cut = rows // 2
    sent = {}

    def first(q):
        sent[q, 1] = shifted(term(q, far, 0, cut).astype(jnp.bfloat16), "cpg_0", 1)
        sent[q, -1] = shifted(term(q, far, cut, rows).astype(jnp.bfloat16), "cpg_0", -1)

    def onward(q, ahead):
        for way in (1, -1):
            got = sent[q, way].astype(jnp.float32)
            if got.shape[0] < rows:
                rest = jnp.zeros_like(got)
                got = jnp.concatenate([got, rest] if way == 1 else [rest, got], axis=0)
            total = (term(q, way * ahead, 0, rows) + got).astype(jnp.bfloat16)
            sent[q, way] = shifted(total, "cpg_0", way)

    def summed(q):
        total = term(q, 0, 0, rows)
        for way in (1, -1):
            total = total + sent[q, way].astype(jnp.float32)
        return total.astype(jnp.bfloat16)

    with jax.named_scope("sum_layers"):
        first(0)
        first(1)
        for ahead in range(far - 1, 0, -1):
            onward(0, ahead)
            onward(1, ahead)
        whole = jnp.concatenate([summed(0), summed(1)], axis=1)
    with jax.named_scope("to_components"):
        sums = lax.all_to_all(whole, PLANE, 0, 0, tiled=True)
    with jax.named_scope("gather_values"):
        values = values + 0.0 * whole[0, 0].astype(jnp.float32)
        everywhere = jnp.repeat(copies(values, FLOOR), 4, axis=0)
    with jax.named_scope("fit"):
        slot = lax.axis_index("samp_2") * 16 + lax.axis_index(PLANE)
        fitted = fit(slot.astype(jnp.int32)[None], sums, everywhere)
    with jax.named_scope("gather_scores"):
        layer = jnp.sum(lax.all_to_all(fitted, LAYER, 0, 0, tiled=True), axis=(0, 1))
        beside = [(2 * i, 2 * i + 2) for i in range(layers - 1)]
        beside += [(2 * i + 3, 2 * i + 1) for i in range(layers - 1)]
        other = lax.ppermute(layer, CPG, beside)
        scores, scales = layer[:rows], layer[rows:]
        before, after = other[rows - HALO : rows], other[:HALO]
    with jax.named_scope("smooth"):
        block_len = reaches.shape[0]
        high = lax.axis_index("cpg_1")
        widened = lax.dynamic_slice_in_dim(
            jnp.concatenate([before, scores, after]), high * block_len, block_len + 2 * HALO, 0
        )
        log_scale = lax.dynamic_slice_in_dim(scales, high * block_len, block_len, 0)
        base = lax.axis_index(CPG) * block_len
        total_cpgs = block_len * lax.axis_size(CPG)
        places = lax.dynamic_slice_in_dim(
            jnp.pad(positions.astype(jnp.float32), HALO), base, block_len + 2 * HALO, 0
        )
        global_index = base - HALO + jnp.arange(block_len + 2 * HALO, dtype=jnp.int32)
        present = ((global_index >= 0) & (global_index < total_cpgs)).astype(jnp.float32)
        smoothed = smooth_block(widened, places, present, reaches)
    return (smoothed, log_scale)


def solution(mesh):
    split = Mesh(
        mesh.devices.reshape(2, 4, 2, 8, 2), ("samp_0", "samp_1", "samp_2", "cpg_0", "cpg_1")
    )
    return jax.shard_map(
        shards,
        mesh=split,
        in_specs=(P(SAMP, CPG), P(SAMP, CPG), P(CPG), P(CPG, SAMP), P(SAMP), P(), P(CPG)),
        out_specs=(P(CPG), P(CPG)),
        check_vma=False,
    )
```

```python
import functools

import jax
import jax.numpy as jnp
from jax import lax
from jax.experimental import pallas as pl
from jax.experimental.pallas import tpu as pltpu
from jax.sharding import Mesh
from jax.sharding import PartitionSpec as P

ITERS = 4
HALO = 8
SAMP = ("samp_0", "samp_1", "samp_2")
CPG = ("cpg_0", "cpg_1")
PLANE = ("cpg_1", "samp_0", "samp_1")
FLOOR = ("samp_0", "samp_1")
LAYER = ("cpg_1", "samp_0", "samp_1", "samp_2")

EPSILON = 1e-06
band_width = 1000.0


def shifted(value, axis, by):
    peers = lax.axis_size(axis)
    return lax.ppermute(value, axis, [(i, (i + by) % peers) for i in range(peers)])


def weigh_kernel(resp_ref, weight_ref, trait_ref, out_ref):
    rows = resp_ref.shape[0]
    trait = trait_ref[...]
    for at in range(0, rows, 16):
        root = jnp.sqrt(weight_ref[at : at + 16, :].astype(jnp.float32))
        weighted = root * resp_ref[at : at + 16, :].astype(jnp.float32)
        design = root * trait
        upper = lax.broadcasted_iota(jnp.int32, (8, root.shape[1]), 0) < 4
        tiles = []
        for half in (0, 8):
            a, b = weighted[half : half + 8], design[half : half + 8]
            tiles.append(jnp.where(upper, a, pltpu.roll(b, 4, 0)))
            tiles.append(jnp.where(upper, pltpu.roll(a, 4, 0), b))
        out_ref[2 * at : 2 * at + 32, :] = jnp.concatenate(tiles, axis=0).astype(jnp.bfloat16)


def weigh(responses, weights, phenotype):
    rows, width = responses.shape
    return pl.pallas_call(
        weigh_kernel,
        out_shape=jax.ShapeDtypeStruct((2 * rows, width), jnp.bfloat16),
    )(responses, weights, phenotype[None, :])


def fit_kernel(slot_ref, sums_ref, values_ref, out_ref, r_ref, d_ref, w_ref):
    half, width = values_ref.shape
    lanes = 512
    upper = lax.broadcasted_iota(jnp.int32, (8, width), 0) < 4
    for i in range(0, half, 8):
        pair = sums_ref[2 * i : 2 * i + 16, :].astype(jnp.float32) + sums_ref[
            2 * (half + i) : 2 * (half + i) + 16, :
        ].astype(jnp.float32)
        a, b = pair[:8], pair[8:]
        r_ref[i : i + 8, :] = jnp.where(upper, a, pltpu.roll(b, 4, 0))
        d_ref[i : i + 8, :] = jnp.where(upper, pltpu.roll(a, 4, 0), b)
    blocks = [(i, j) for i in range(0, half, 8) for j in range(0, width, lanes)]

    def total(acc):
        acc = functools.reduce(jnp.add, [acc[:, k : k + 128] for k in range(0, lanes, 128)])
        acc = acc + pltpu.roll(acc, 4, 0)
        return jnp.broadcast_to(jnp.sum(acc, axis=1, keepdims=True), (8, 128))

    def wide(value):
        return jnp.concatenate([value] * (lanes // 128), axis=1)

    def sweep(scale, last):
        zero = jnp.zeros((8, lanes), jnp.float32)
        crossed, energy, traced, fisher = zero, zero, zero, zero
        scale = wide(scale)
        for i, j in blocks:
            at = (slice(i, i + 8), slice(j, j + lanes))
            lam, resp, design = values_ref[at], r_ref[at], d_ref[at]
            v = scale * lam + 1.0
            inv = pl.reciprocal(v, approx=True)
            inv = inv * (2.0 - v * inv)
            over = design * inv
            crossed = crossed + over * resp
            energy = energy + over * design
            if not last:
                lev = lam * inv
                traced = traced + lev
                fisher = fisher + lev * lev
                w_ref[at] = lev * inv
        return total(crossed), total(energy) + EPSILON, traced, fisher

    log_scale = jnp.zeros((8, 128), jnp.float32)
    for _ in range(ITERS):
        scale = jnp.exp(log_scale)
        crossed, energy, traced, fisher = sweep(scale, False)
        effect = wide(crossed / energy)
        spread = jnp.zeros((8, lanes), jnp.float32)
        for i, j in blocks:
            at = (slice(i, i + 8), slice(j, j + lanes))
            residual = r_ref[at] - effect * d_ref[at]
            spread = spread + w_ref[at] * residual * residual
        gradient = 0.5 * (total(spread) - total(traced))
        log_scale = log_scale + jnp.tanh(gradient / (scale * (0.5 * total(fisher))))
    crossed, energy, _, _ = sweep(jnp.exp(log_scale), True)
    score = crossed / jnp.sqrt(energy)
    lane = lax.broadcasted_iota(jnp.int32, (8, 128), 1)
    row = lax.broadcasted_iota(jnp.int32, (8, 128), 0)
    here = (row < 4) & (lane == 4 * slot_ref[0] + row)
    both = [jnp.sum(jnp.where(here, v, 0.0), axis=0, keepdims=True) for v in (score, log_scale)]
    out_ref[...] = jnp.broadcast_to(
        jnp.concatenate(both, axis=1)[None], (out_ref.shape[0], 1, 256)
    )


def fit(slot, sums, values):
    rows, width = values.shape
    vmem = pl.BlockSpec(memory_space=pltpu.VMEM)
    return pl.pallas_call(
        fit_kernel,
        out_shape=jax.ShapeDtypeStruct((32, 1, 256), jnp.float32),
        in_specs=[pl.BlockSpec(memory_space=pltpu.SMEM), vmem, vmem],
        out_specs=vmem,
        scratch_shapes=[pltpu.VMEM((rows, width), jnp.float32)] * 3,
        compiler_params=pltpu.CompilerParams(vmem_limit_bytes=16 * 1024 * 1024),
    )(slot, sums, values)


def gather_plane(own):
    x, y = "samp_1", "samp_0"
    left = shifted(own, x, 1)
    right = shifted(own, x, -1)
    over = shifted(own, y, 1)
    far = shifted(left, x, 1)
    over_right = shifted(over, x, -1)
    over_left = shifted(left, y, 1)
    over_far = jnp.concatenate(
        [
            shifted(over_left[:48], x, 1),
            shifted(over_right[48:96], x, -1),
            shifted(far[96:], y, 1),
        ],
        axis=0,
    )
    return jnp.stack([own, right, far, left, over, over_right, over_far, over_left])


def smooth_block(widened, places, present, reaches):
    block_len = reaches.shape[0]
    centre = places[HALO : HALO + block_len]
    total_sum = jnp.zeros((block_len,), jnp.float32)
    norm_sum = jnp.zeros((block_len,), jnp.float32)
    for offset in range(2 * HALO + 1):
        near_scores = widened[offset : offset + block_len]
        near_places = places[offset : offset + block_len]
        within = (abs(offset - HALO) <= reaches).astype(jnp.float32)
        kernel = (
            present[offset : offset + block_len]
            * within
            * jnp.exp(-jnp.abs(near_places - centre) / band_width)
        )
        total_sum = total_sum + kernel * near_scores
        norm_sum = norm_sum + kernel
    return total_sum / norm_sum


def copies(value, axes):
    peers = lax.axis_size(axes)
    return lax.all_to_all(
        jnp.broadcast_to(value[None], (peers, *value.shape)), axes, 0, 0, tiled=True
    )


def shards(responses, weights, phenotype, eigvecs, eigvals, positions, reaches):
    z, x, y = lax.axis_index("cpg_0"), lax.axis_index("samp_1"), lax.axis_index("samp_0")
    layers = lax.axis_size("cpg_0")
    with jax.named_scope("weigh"):
        own = weigh(responses, weights, phenotype)
    with jax.named_scope("gather_rows"):
        blocks = gather_plane(own)
    with jax.named_scope("swap_eigvecs"):
        other = shifted(eigvecs, "samp_2", 1)
        vecs = (eigvecs, other)
        ready = (0.0 * other[0, 0].astype(jnp.float32)).astype(jnp.int32)
    with jax.named_scope("gather_values"):
        everywhere = copies(eigvals, SAMP).reshape(-1, 2, eigvals.shape[0])
        everywhere = jnp.where(lax.axis_index("samp_2") == 0, everywhere, everywhere[:, ::-1])
        everywhere = jnp.repeat(everywhere.reshape(everywhere.shape[0], -1), 4, axis=0)
    rows = own.shape[0]

    def term(q, ahead, lo, hi):
        dest = lax.rem(z + ahead + layers, layers)
        across, along = dest // 4, lax.rem(dest, 4)
        place = 4 * (across ^ y) + lax.rem(along - x + 4, 4) + ready
        block = lax.dynamic_index_in_dim(blocks, place, 0, keepdims=False)[lo:hi]
        return jnp.dot(block, vecs[q], preferred_element_type=jnp.float32)

    far = layers // 2
    cut = rows // 2
    sent = {}

    def first(q):
        sent[q, 1] = shifted(term(q, far, 0, cut).astype(jnp.bfloat16), "cpg_0", 1)
        sent[q, -1] = shifted(term(q, far, cut, rows).astype(jnp.bfloat16), "cpg_0", -1)

    def onward(q, ahead):
        for way in (1, -1):
            got = sent[q, way].astype(jnp.float32)
            if got.shape[0] < rows:
                rest = jnp.zeros_like(got)
                got = jnp.concatenate([got, rest] if way == 1 else [rest, got], axis=0)
            total = (term(q, way * ahead, 0, rows) + got).astype(jnp.bfloat16)
            sent[q, way] = shifted(total, "cpg_0", way)

    def summed(q):
        total = term(q, 0, 0, rows)
        for way in (1, -1):
            total = total + sent[q, way].astype(jnp.float32)
        return total.astype(jnp.bfloat16)

    with jax.named_scope("sum_layers"):
        first(0)
        first(1)
        for ahead in range(far - 1, 0, -1):
            onward(0, ahead)
            onward(1, ahead)
        whole = jnp.concatenate([summed(0), summed(1)], axis=1)
    with jax.named_scope("to_components"):
        sums = lax.all_to_all(whole, PLANE, 0, 0, tiled=True)
    with jax.named_scope("fit"):
        slot = lax.axis_index("samp_2") * 16 + lax.axis_index(PLANE)
        fitted = fit(slot.astype(jnp.int32)[None], sums, everywhere)
    with jax.named_scope("gather_scores"):
        layer = jnp.sum(lax.all_to_all(fitted, LAYER, 0, 0, tiled=True), axis=(0, 1))
        beside = [(2 * i, 2 * i + 2) for i in range(layers - 1)]
        beside += [(2 * i + 3, 2 * i + 1) for i in range(layers - 1)]
        other = lax.ppermute(layer, CPG, beside)
        scores, scales = layer[:rows], layer[rows:]
        before, after = other[rows - HALO : rows], other[:HALO]
    with jax.named_scope("smooth"):
        block_len = reaches.shape[0]
        high = lax.axis_index("cpg_1")
        widened = lax.dynamic_slice_in_dim(
            jnp.concatenate([before, scores, after]), high * block_len, block_len + 2 * HALO, 0
        )
        log_scale = lax.dynamic_slice_in_dim(scales, high * block_len, block_len, 0)
        base = lax.axis_index(CPG) * block_len
        total_cpgs = block_len * lax.axis_size(CPG)
        places = lax.dynamic_slice_in_dim(
            jnp.pad(positions.astype(jnp.float32), HALO), base, block_len + 2 * HALO, 0
        )
        global_index = base - HALO + jnp.arange(block_len + 2 * HALO, dtype=jnp.int32)
        present = ((global_index >= 0) & (global_index < total_cpgs)).astype(jnp.float32)
        smoothed = smooth_block(widened, places, present, reaches)
    return (smoothed, log_scale)


def solution(mesh):
    split = Mesh(
        mesh.devices.reshape(2, 4, 2, 8, 2), ("samp_0", "samp_1", "samp_2", "cpg_0", "cpg_1")
    )
    return jax.shard_map(
        shards,
        mesh=split,
        in_specs=(P(SAMP, CPG), P(SAMP, CPG), P(CPG), P(CPG, SAMP), P(SAMP), P(), P(CPG)),
        out_specs=(P(CPG), P(CPG)),
        check_vma=False,
    )
```

```python
import functools

import jax
import jax.numpy as jnp
from jax import lax
from jax.experimental import pallas as pl
from jax.experimental.pallas import tpu as pltpu
from jax.sharding import Mesh
from jax.sharding import PartitionSpec as P

ITERS = 4
HALO = 8
SAMP = ("samp_0", "samp_1", "samp_2")
CPG = ("cpg_0", "cpg_1")
PLANE = ("cpg_1", "samp_0", "samp_1")
FLOOR = ("samp_0", "samp_1")
LAYER = ("cpg_1", "samp_0", "samp_1", "samp_2")

EPSILON = 1e-06
band_width = 1000.0


def shifted(value, axis, by):
    peers = lax.axis_size(axis)
    return lax.ppermute(value, axis, [(i, (i + by) % peers) for i in range(peers)])


def weigh_kernel(resp_ref, weight_ref, trait_ref, out_ref):
    rows = resp_ref.shape[0]
    trait = trait_ref[...]
    for at in range(0, rows, 16):
        root = jnp.sqrt(weight_ref[at : at + 16, :].astype(jnp.float32))
        weighted = root * resp_ref[at : at + 16, :].astype(jnp.float32)
        design = root * trait
        upper = lax.broadcasted_iota(jnp.int32, (8, root.shape[1]), 0) < 4
        tiles = []
        for half in (0, 8):
            a, b = weighted[half : half + 8], design[half : half + 8]
            tiles.append(jnp.where(upper, a, pltpu.roll(b, 4, 0)))
            tiles.append(jnp.where(upper, pltpu.roll(a, 4, 0), b))
        out_ref[2 * at : 2 * at + 32, :] = jnp.concatenate(tiles, axis=0).astype(jnp.bfloat16)


def weigh(responses, weights, phenotype):
    rows, width = responses.shape
    return pl.pallas_call(
        weigh_kernel,
        out_shape=jax.ShapeDtypeStruct((2 * rows, width), jnp.bfloat16),
    )(responses, weights, phenotype[None, :])


def fit_kernel(slot_ref, sums_ref, values_ref, out_ref, r_ref, d_ref, w_ref):
    half, width = values_ref.shape
    lanes = 512
    upper = lax.broadcasted_iota(jnp.int32, (8, width), 0) < 4
    for i in range(0, half, 8):
        pair = sums_ref[2 * i : 2 * i + 16, :].astype(jnp.float32) + sums_ref[
            2 * (half + i) : 2 * (half + i) + 16, :
        ].astype(jnp.float32)
        a, b = pair[:8], pair[8:]
        r_ref[i : i + 8, :] = jnp.where(upper, a, pltpu.roll(b, 4, 0))
        d_ref[i : i + 8, :] = jnp.where(upper, pltpu.roll(a, 4, 0), b)
    blocks = [(i, j) for i in range(0, half, 8) for j in range(0, width, lanes)]

    def total(acc):
        acc = functools.reduce(jnp.add, [acc[:, k : k + 128] for k in range(0, lanes, 128)])
        acc = acc + pltpu.roll(acc, 4, 0)
        return jnp.broadcast_to(jnp.sum(acc, axis=1, keepdims=True), (8, 128))

    def wide(value):
        return jnp.concatenate([value] * (lanes // 128), axis=1)

    def sweep(scale, last):
        zero = jnp.zeros((8, lanes), jnp.float32)
        crossed, energy, traced, fisher = zero, zero, zero, zero
        scale = wide(scale)
        for i, j in blocks:
            at = (slice(i, i + 8), slice(j, j + lanes))
            lam, resp, design = values_ref[at], r_ref[at], d_ref[at]
            v = scale * lam + 1.0
            inv = pl.reciprocal(v, approx=True)
            inv = inv * (2.0 - v * inv)
            over = design * inv
            crossed = crossed + over * resp
            energy = energy + over * design
            if not last:
                lev = lam * inv
                traced = traced + lev
                fisher = fisher + lev * lev
                w_ref[at] = lev * inv
        return total(crossed), total(energy) + EPSILON, traced, fisher

    log_scale = jnp.zeros((8, 128), jnp.float32)
    for _ in range(ITERS):
        scale = jnp.exp(log_scale)
        crossed, energy, traced, fisher = sweep(scale, False)
        effect = wide(crossed / energy)
        spread = jnp.zeros((8, lanes), jnp.float32)
        for i, j in blocks:
            at = (slice(i, i + 8), slice(j, j + lanes))
            residual = r_ref[at] - effect * d_ref[at]
            spread = spread + w_ref[at] * residual * residual
        gradient = 0.5 * (total(spread) - total(traced))
        log_scale = log_scale + jnp.tanh(gradient / (scale * (0.5 * total(fisher))))
    crossed, energy, _, _ = sweep(jnp.exp(log_scale), True)
    score = crossed / jnp.sqrt(energy)
    lane = lax.broadcasted_iota(jnp.int32, (8, 128), 1)
    row = lax.broadcasted_iota(jnp.int32, (8, 128), 0)
    here = (row < 4) & (lane == 4 * slot_ref[0] + row)
    both = [jnp.sum(jnp.where(here, v, 0.0), axis=0, keepdims=True) for v in (score, log_scale)]
    out_ref[...] = jnp.broadcast_to(
        jnp.concatenate(both, axis=1)[None], (out_ref.shape[0], 1, 256)
    )


def fit(slot, sums, values):
    rows, width = values.shape
    vmem = pl.BlockSpec(memory_space=pltpu.VMEM)
    return pl.pallas_call(
        fit_kernel,
        out_shape=jax.ShapeDtypeStruct((32, 1, 256), jnp.float32),
        in_specs=[pl.BlockSpec(memory_space=pltpu.SMEM), vmem, vmem],
        out_specs=vmem,
        scratch_shapes=[pltpu.VMEM((rows, width), jnp.float32)] * 3,
        compiler_params=pltpu.CompilerParams(vmem_limit_bytes=16 * 1024 * 1024),
    )(slot, sums, values)


def gather_plane(own, other):
    x, y = "samp_1", "samp_0"
    left = shifted(own, x, 1)
    right = shifted(own, x, -1)
    over = shifted(own, y, 1)
    far = shifted(left, x, 1)
    over_right = shifted(over, x, -1)
    over_left = shifted(left, y, 1)
    over_far = jnp.concatenate(
        [
            shifted(over_left[:48], x, 1),
            shifted(over_right[48:96], x, -1),
            shifted(far[96:], y, 1),
        ],
        axis=0,
    )
    over_far = over_far + 0 * other[: own.shape[0]]
    return jnp.stack([own, right, far, left, over, over_right, over_far, over_left])


def smooth_block(widened, places, present, reaches):
    block_len = reaches.shape[0]
    centre = places[HALO : HALO + block_len]
    total_sum = jnp.zeros((block_len,), jnp.float32)
    norm_sum = jnp.zeros((block_len,), jnp.float32)
    for offset in range(2 * HALO + 1):
        near_scores = widened[offset : offset + block_len]
        near_places = places[offset : offset + block_len]
        within = (abs(offset - HALO) <= reaches).astype(jnp.float32)
        kernel = (
            present[offset : offset + block_len]
            * within
            * jnp.exp(-jnp.abs(near_places - centre) / band_width)
        )
        total_sum = total_sum + kernel * near_scores
        norm_sum = norm_sum + kernel
    return total_sum / norm_sum


def copies(value, axes):
    peers = lax.axis_size(axes)
    return lax.all_to_all(
        jnp.broadcast_to(value[None], (peers, *value.shape)), axes, 0, 0, tiled=True
    )


def shards(responses, weights, phenotype, eigvecs, eigvals, positions, reaches):
    z, x, y = lax.axis_index("cpg_0"), lax.axis_index("samp_1"), lax.axis_index("samp_0")
    layers = lax.axis_size("cpg_0")
    with jax.named_scope("swap_eigvecs"):
        other = shifted(eigvecs, "samp_2", 1)
    with jax.named_scope("weigh"):
        own = weigh(responses, weights, phenotype)
    with jax.named_scope("gather_rows"):
        blocks = gather_plane(own, other)
    with jax.named_scope("gather_values"):
        everywhere = copies(eigvals, SAMP).reshape(-1, 2, eigvals.shape[0])
        everywhere = jnp.where(lax.axis_index("samp_2") == 0, everywhere, everywhere[:, ::-1])
        everywhere = jnp.repeat(everywhere.reshape(everywhere.shape[0], -1), 4, axis=0)
    other = other + 0 * (blocks[6, :1] + everywhere[:1, : other.shape[1]].astype(other.dtype))
    vecs = (eigvecs, other)
    rows = own.shape[0]

    def term(q, ahead, lo, hi):
        dest = lax.rem(z + ahead + layers, layers)
        across, along = dest // 4, lax.rem(dest, 4)
        place = 4 * (across ^ y) + lax.rem(along - x + 4, 4)
        block = lax.dynamic_index_in_dim(blocks, place, 0, keepdims=False)[lo:hi]
        return jnp.dot(block, vecs[q], preferred_element_type=jnp.float32)

    far = layers // 2
    cut = rows // 2
    sent = {}

    def first(q):
        sent[q, 1] = shifted(term(q, far, 0, cut).astype(jnp.bfloat16), "cpg_0", 1)
        sent[q, -1] = shifted(term(q, far, cut, rows).astype(jnp.bfloat16), "cpg_0", -1)

    def onward(q, ahead):
        for way in (1, -1):
            got = sent[q, way].astype(jnp.float32)
            if got.shape[0] < rows:
                rest = jnp.zeros_like(got)
                got = jnp.concatenate([got, rest] if way == 1 else [rest, got], axis=0)
            total = (term(q, way * ahead, 0, rows) + got).astype(jnp.bfloat16)
            sent[q, way] = shifted(total, "cpg_0", way)

    def summed(q):
        total = term(q, 0, 0, rows)
        for way in (1, -1):
            total = total + sent[q, way].astype(jnp.float32)
        return total.astype(jnp.bfloat16)

    with jax.named_scope("sum_layers"):
        first(0)
        first(1)
        for ahead in range(far - 1, 0, -1):
            onward(0, ahead)
            onward(1, ahead)
        whole = jnp.concatenate([summed(0), summed(1)], axis=1)
    with jax.named_scope("to_components"):
        sums = lax.all_to_all(whole, PLANE, 0, 0, tiled=True)
    with jax.named_scope("fit"):
        slot = lax.axis_index("samp_2") * 16 + lax.axis_index(PLANE)
        fitted = fit(slot.astype(jnp.int32)[None], sums, everywhere)
    with jax.named_scope("gather_scores"):
        layer = jnp.sum(lax.all_to_all(fitted, LAYER, 0, 0, tiled=True), axis=(0, 1))
        beside = [(2 * i, 2 * i + 2) for i in range(layers - 1)]
        beside += [(2 * i + 3, 2 * i + 1) for i in range(layers - 1)]
        other = lax.ppermute(layer, CPG, beside)
        scores, scales = layer[:rows], layer[rows:]
        before, after = other[rows - HALO : rows], other[:HALO]
    with jax.named_scope("smooth"):
        block_len = reaches.shape[0]
        high = lax.axis_index("cpg_1")
        widened = lax.dynamic_slice_in_dim(
            jnp.concatenate([before, scores, after]), high * block_len, block_len + 2 * HALO, 0
        )
        log_scale = lax.dynamic_slice_in_dim(scales, high * block_len, block_len, 0)
        base = lax.axis_index(CPG) * block_len
        total_cpgs = block_len * lax.axis_size(CPG)
        places = lax.dynamic_slice_in_dim(
            jnp.pad(positions.astype(jnp.float32), HALO), base, block_len + 2 * HALO, 0
        )
        global_index = base - HALO + jnp.arange(block_len + 2 * HALO, dtype=jnp.int32)
        present = ((global_index >= 0) & (global_index < total_cpgs)).astype(jnp.float32)
        smoothed = smooth_block(widened, places, present, reaches)
    return (smoothed, log_scale)


def solution(mesh):
    split = Mesh(
        mesh.devices.reshape(2, 4, 2, 8, 2), ("samp_0", "samp_1", "samp_2", "cpg_0", "cpg_1")
    )
    return jax.shard_map(
        shards,
        mesh=split,
        in_specs=(P(SAMP, CPG), P(SAMP, CPG), P(CPG), P(CPG, SAMP), P(SAMP), P(), P(CPG)),
        out_specs=(P(CPG), P(CPG)),
        check_vma=False,
    )
```

```python
import functools

import jax
import jax.numpy as jnp
from jax import lax
from jax.experimental import pallas as pl
from jax.experimental.pallas import tpu as pltpu
from jax.sharding import Mesh
from jax.sharding import PartitionSpec as P

ITERS = 4
HALO = 8
SAMP = ("samp_0", "samp_1", "samp_2")
CPG = ("cpg_0", "cpg_1")
PLANE = ("cpg_1", "samp_0", "samp_1")
FLOOR = ("samp_0", "samp_1")
LAYER = ("cpg_1", "samp_0", "samp_1", "samp_2")

EPSILON = 1e-06
band_width = 1000.0


def shifted(value, axis, by):
    peers = lax.axis_size(axis)
    return lax.ppermute(value, axis, [(i, (i + by) % peers) for i in range(peers)])


def weigh_kernel(resp_ref, weight_ref, trait_ref, out_ref):
    rows = resp_ref.shape[0]
    trait = trait_ref[...]
    for at in range(0, rows, 16):
        root = jnp.sqrt(weight_ref[at : at + 16, :].astype(jnp.float32))
        weighted = root * resp_ref[at : at + 16, :].astype(jnp.float32)
        design = root * trait
        upper = lax.broadcasted_iota(jnp.int32, (8, root.shape[1]), 0) < 4
        tiles = []
        for half in (0, 8):
            a, b = weighted[half : half + 8], design[half : half + 8]
            tiles.append(jnp.where(upper, a, pltpu.roll(b, 4, 0)))
            tiles.append(jnp.where(upper, pltpu.roll(a, 4, 0), b))
        out_ref[2 * at : 2 * at + 32, :] = jnp.concatenate(tiles, axis=0).astype(jnp.bfloat16)


def weigh(responses, weights, phenotype):
    rows, width = responses.shape
    return pl.pallas_call(
        weigh_kernel,
        out_shape=jax.ShapeDtypeStruct((2 * rows, width), jnp.bfloat16),
    )(responses, weights, phenotype[None, :])


def open_kernel(place_ref, blocks_ref, own_ref, other_ref, *refs):
    outs, nears, (block_ref, block_sem, near_sems) = refs[:4], refs[4:6], refs[6:]
    fetch = pltpu.make_async_copy(blocks_ref.at[place_ref[0]], block_ref, block_sem)
    copies = [
        pltpu.make_async_copy(given, near, near_sems.at[q])
        for q, (given, near) in enumerate(zip((own_ref, other_ref), nears))
    ]
    fetch.start()
    for copy in copies:
        copy.start()
    fetch.wait()
    cut = outs[0].shape[0]
    for q, copy in enumerate(copies):
        copy.wait()
        total = jnp.dot(block_ref[...], nears[q][...], preferred_element_type=jnp.float32)
        outs[2 * q][...] = total[:cut].astype(jnp.bfloat16)
        outs[2 * q + 1][...] = total[cut:].astype(jnp.bfloat16)


def open_sums(place, blocks, own, other):
    _, rows, width = blocks.shape
    columns = own.shape[1]
    anywhere = pl.BlockSpec(memory_space=pl.ANY)
    vmem = pl.BlockSpec(memory_space=pltpu.VMEM)
    return pl.pallas_call(
        open_kernel,
        out_shape=[jax.ShapeDtypeStruct((rows // 2, columns), jnp.bfloat16)] * 4
        + [pltpu.VMEM(own.shape, own.dtype)] * 2,
        in_specs=[pl.BlockSpec(memory_space=pltpu.SMEM), anywhere, anywhere, anywhere],
        out_specs=[vmem] * 6,
        scratch_shapes=[
            pltpu.VMEM((rows, width), jnp.bfloat16),
            pltpu.SemaphoreType.DMA,
            pltpu.SemaphoreType.DMA((2,)),
        ],
        compiler_params=pltpu.CompilerParams(vmem_limit_bytes=24 * 1024 * 1024),
    )(place, blocks, own, other)


def fit_kernel(slot_ref, sums_ref, values_ref, out_ref, r_ref, d_ref, w_ref):
    half, width = values_ref.shape
    lanes = 512
    upper = lax.broadcasted_iota(jnp.int32, (8, width), 0) < 4
    for i in range(0, half, 8):
        pair = sums_ref[2 * i : 2 * i + 16, :].astype(jnp.float32) + sums_ref[
            2 * (half + i) : 2 * (half + i) + 16, :
        ].astype(jnp.float32)
        a, b = pair[:8], pair[8:]
        r_ref[i : i + 8, :] = jnp.where(upper, a, pltpu.roll(b, 4, 0))
        d_ref[i : i + 8, :] = jnp.where(upper, pltpu.roll(a, 4, 0), b)
    blocks = [(i, j) for i in range(0, half, 8) for j in range(0, width, lanes)]

    def total(acc):
        acc = functools.reduce(jnp.add, [acc[:, k : k + 128] for k in range(0, lanes, 128)])
        acc = acc + pltpu.roll(acc, 4, 0)
        return jnp.broadcast_to(jnp.sum(acc, axis=1, keepdims=True), (8, 128))

    def wide(value):
        return jnp.concatenate([value] * (lanes // 128), axis=1)

    def sweep(scale, last):
        zero = jnp.zeros((8, lanes), jnp.float32)
        crossed, energy, traced, fisher = zero, zero, zero, zero
        scale = wide(scale)
        for i, j in blocks:
            at = (slice(i, i + 8), slice(j, j + lanes))
            lam, resp, design = values_ref[at], r_ref[at], d_ref[at]
            v = scale * lam + 1.0
            inv = pl.reciprocal(v, approx=True)
            inv = inv * (2.0 - v * inv)
            over = design * inv
            crossed = crossed + over * resp
            energy = energy + over * design
            if not last:
                lev = lam * inv
                traced = traced + lev
                fisher = fisher + lev * lev
                w_ref[at] = lev * inv
        return total(crossed), total(energy) + EPSILON, traced, fisher

    log_scale = jnp.zeros((8, 128), jnp.float32)
    for _ in range(ITERS):
        scale = jnp.exp(log_scale)
        crossed, energy, traced, fisher = sweep(scale, False)
        effect = wide(crossed / energy)
        spread = jnp.zeros((8, lanes), jnp.float32)
        for i, j in blocks:
            at = (slice(i, i + 8), slice(j, j + lanes))
            residual = r_ref[at] - effect * d_ref[at]
            spread = spread + w_ref[at] * residual * residual
        gradient = 0.5 * (total(spread) - total(traced))
        log_scale = log_scale + jnp.tanh(gradient / (scale * (0.5 * total(fisher))))
    crossed, energy, _, _ = sweep(jnp.exp(log_scale), True)
    score = crossed / jnp.sqrt(energy)
    lane = lax.broadcasted_iota(jnp.int32, (8, 128), 1)
    row = lax.broadcasted_iota(jnp.int32, (8, 128), 0)
    here = (row < 4) & (lane == 4 * slot_ref[0] + row)
    both = [jnp.sum(jnp.where(here, v, 0.0), axis=0, keepdims=True) for v in (score, log_scale)]
    out_ref[...] = jnp.broadcast_to(
        jnp.concatenate(both, axis=1)[None], (out_ref.shape[0], 1, 256)
    )


def fit(slot, sums, values):
    rows, width = values.shape
    vmem = pl.BlockSpec(memory_space=pltpu.VMEM)
    return pl.pallas_call(
        fit_kernel,
        out_shape=jax.ShapeDtypeStruct((32, 1, 256), jnp.float32),
        in_specs=[pl.BlockSpec(memory_space=pltpu.SMEM), vmem, vmem],
        out_specs=vmem,
        scratch_shapes=[pltpu.VMEM((rows, width), jnp.float32)] * 3,
        compiler_params=pltpu.CompilerParams(vmem_limit_bytes=16 * 1024 * 1024),
    )(slot, sums, values)


def gather_plane(own):
    x, y = "samp_1", "samp_0"
    left = shifted(own, x, 1)
    right = shifted(own, x, -1)
    over = shifted(own, y, 1)
    far = shifted(left, x, 1)
    over_right = shifted(over, x, -1)
    over_left = shifted(left, y, 1)
    over_far = jnp.concatenate(
        [
            shifted(over_left[:48], x, 1),
            shifted(over_right[48:96], x, -1),
            shifted(far[96:], y, 1),
        ],
        axis=0,
    )
    return jnp.stack([own, right, far, left, over, over_right, over_far, over_left])


def smooth_block(widened, places, present, reaches):
    block_len = reaches.shape[0]
    centre = places[HALO : HALO + block_len]
    total_sum = jnp.zeros((block_len,), jnp.float32)
    norm_sum = jnp.zeros((block_len,), jnp.float32)
    for offset in range(2 * HALO + 1):
        near_scores = widened[offset : offset + block_len]
        near_places = places[offset : offset + block_len]
        within = (abs(offset - HALO) <= reaches).astype(jnp.float32)
        kernel = (
            present[offset : offset + block_len]
            * within
            * jnp.exp(-jnp.abs(near_places - centre) / band_width)
        )
        total_sum = total_sum + kernel * near_scores
        norm_sum = norm_sum + kernel
    return total_sum / norm_sum


def copies(value, axes):
    peers = lax.axis_size(axes)
    return lax.all_to_all(
        jnp.broadcast_to(value[None], (peers, *value.shape)), axes, 0, 0, tiled=True
    )


def shards(responses, weights, phenotype, eigvecs, eigvals, positions, reaches):
    z, x, y = lax.axis_index("cpg_0"), lax.axis_index("samp_1"), lax.axis_index("samp_0")
    layers = lax.axis_size("cpg_0")
    with jax.named_scope("weigh"):
        own = weigh(responses, weights, phenotype)
    with jax.named_scope("gather_rows"):
        blocks = gather_plane(own)
    with jax.named_scope("swap_eigvecs"):
        other = shifted(eigvecs, "samp_2", 1)
    with jax.named_scope("gather_values"):
        everywhere = copies(eigvals, SAMP).reshape(-1, 2, eigvals.shape[0])
        everywhere = jnp.where(lax.axis_index("samp_2") == 0, everywhere, everywhere[:, ::-1])
        everywhere = jnp.repeat(everywhere.reshape(everywhere.shape[0], -1), 4, axis=0)
    rows = own.shape[0]

    def place(ahead):
        dest = lax.rem(z + ahead + layers, layers)
        across, along = dest // 4, lax.rem(dest, 4)
        return 4 * (across ^ y) + lax.rem(along - x + 4, 4)

    def term(q, ahead):
        block = lax.dynamic_index_in_dim(blocks, place(ahead), 0, keepdims=False)
        return jnp.dot(block, vecs[q], preferred_element_type=jnp.float32)

    far = layers // 2
    sent = {}

    def onward(q, ahead):
        for way in (1, -1):
            got = sent[q, way].astype(jnp.float32)
            if got.shape[0] < rows:
                rest = jnp.zeros_like(got)
                got = jnp.concatenate([got, rest] if way == 1 else [rest, got], axis=0)
            total = (term(q, way * ahead) + got).astype(jnp.bfloat16)
            sent[q, way] = shifted(total, "cpg_0", way)

    def summed(q):
        total = term(q, 0)
        for way in (1, -1):
            total = total + sent[q, way].astype(jnp.float32)
        return total.astype(jnp.bfloat16)

    with jax.named_scope("sum_layers"):
        *halves, near_own, near_other = open_sums(place(far)[None], blocks, eigvecs, other)
        vecs = (near_own, near_other)
        for q in (0, 1):
            for at, way in enumerate((1, -1)):
                sent[q, way] = shifted(halves[2 * q + at], "cpg_0", way)
        for ahead in range(far - 1, 0, -1):
            onward(0, ahead)
            onward(1, ahead)
        whole = jnp.concatenate([summed(0), summed(1)], axis=1)
    with jax.named_scope("to_components"):
        sums = lax.all_to_all(whole, PLANE, 0, 0, tiled=True)
    with jax.named_scope("fit"):
        slot = lax.axis_index("samp_2") * 16 + lax.axis_index(PLANE)
        fitted = fit(slot.astype(jnp.int32)[None], sums, everywhere)
    with jax.named_scope("gather_scores"):
        layer = jnp.sum(lax.all_to_all(fitted, LAYER, 0, 0, tiled=True), axis=(0, 1))
        beside = [(2 * i, 2 * i + 2) for i in range(layers - 1)]
        beside += [(2 * i + 3, 2 * i + 1) for i in range(layers - 1)]
        other = lax.ppermute(layer, CPG, beside)
        scores, scales = layer[:rows], layer[rows:]
        before, after = other[rows - HALO : rows], other[:HALO]
    with jax.named_scope("smooth"):
        block_len = reaches.shape[0]
        high = lax.axis_index("cpg_1")
        widened = lax.dynamic_slice_in_dim(
            jnp.concatenate([before, scores, after]), high * block_len, block_len + 2 * HALO, 0
        )
        log_scale = lax.dynamic_slice_in_dim(scales, high * block_len, block_len, 0)
        base = lax.axis_index(CPG) * block_len
        total_cpgs = block_len * lax.axis_size(CPG)
        places = lax.dynamic_slice_in_dim(
            jnp.pad(positions.astype(jnp.float32), HALO), base, block_len + 2 * HALO, 0
        )
        global_index = base - HALO + jnp.arange(block_len + 2 * HALO, dtype=jnp.int32)
        present = ((global_index >= 0) & (global_index < total_cpgs)).astype(jnp.float32)
        smoothed = smooth_block(widened, places, present, reaches)
    return (smoothed, log_scale)


def solution(mesh):
    split = Mesh(
        mesh.devices.reshape(2, 4, 2, 8, 2), ("samp_0", "samp_1", "samp_2", "cpg_0", "cpg_1")
    )
    return jax.shard_map(
        shards,
        mesh=split,
        in_specs=(P(SAMP, CPG), P(SAMP, CPG), P(CPG), P(CPG, SAMP), P(SAMP), P(), P(CPG)),
        out_specs=(P(CPG), P(CPG)),
        check_vma=False,
    )
```

```python
import functools

import jax
import jax.numpy as jnp
from jax import lax
from jax.experimental import pallas as pl
from jax.experimental.pallas import tpu as pltpu
from jax.sharding import Mesh
from jax.sharding import PartitionSpec as P

ITERS = 4
HALO = 8
SAMP = ("samp_0", "samp_1", "samp_2")
CPG = ("cpg_0", "cpg_1")
PLANE = ("cpg_1", "samp_0", "samp_1")
FLOOR = ("samp_0", "samp_1")
LAYER = ("cpg_1", "samp_0", "samp_1", "samp_2")

EPSILON = 1e-06
band_width = 1000.0


def shifted(value, axis, by):
    peers = lax.axis_size(axis)
    return lax.ppermute(value, axis, [(i, (i + by) % peers) for i in range(peers)])


def weigh_kernel(resp_ref, weight_ref, trait_ref, out_ref):
    rows = resp_ref.shape[0]
    trait = trait_ref[...]
    for at in range(0, rows, 16):
        root = jnp.sqrt(weight_ref[at : at + 16, :].astype(jnp.float32))
        weighted = root * resp_ref[at : at + 16, :].astype(jnp.float32)
        design = root * trait
        upper = lax.broadcasted_iota(jnp.int32, (8, root.shape[1]), 0) < 4
        tiles = []
        for half in (0, 8):
            a, b = weighted[half : half + 8], design[half : half + 8]
            tiles.append(jnp.where(upper, a, pltpu.roll(b, 4, 0)))
            tiles.append(jnp.where(upper, pltpu.roll(a, 4, 0), b))
        out_ref[2 * at : 2 * at + 32, :] = jnp.concatenate(tiles, axis=0).astype(jnp.bfloat16)


def weigh(responses, weights, phenotype):
    rows, width = responses.shape
    return pl.pallas_call(
        weigh_kernel,
        out_shape=jax.ShapeDtypeStruct((2 * rows, width), jnp.bfloat16),
    )(responses, weights, phenotype[None, :])


def open_kernel(place_ref, blocks_ref, own_ref, other_ref, done_ref, *refs):
    outs, nears, (block_ref, block_sem, near_sems) = refs[:4], refs[4:6], refs[6:]
    fetch = pltpu.make_async_copy(blocks_ref.at[place_ref[0]], block_ref, block_sem)
    copies = [
        pltpu.make_async_copy(given, near, near_sems.at[q])
        for q, (given, near) in enumerate(zip((own_ref, other_ref), nears))
    ]
    fetch.start()
    for copy in copies:
        copy.start()
    fetch.wait()
    cut = outs[0].shape[0]
    for q, copy in enumerate(copies):
        copy.wait()
        total = jnp.dot(block_ref[...], nears[q][...], preferred_element_type=jnp.float32)
        outs[2 * q][...] = total[:cut].astype(jnp.bfloat16)
        outs[2 * q + 1][...] = total[cut:].astype(jnp.bfloat16)


def open_sums(place, blocks, own, other, done):
    _, rows, width = blocks.shape
    columns = own.shape[1]
    anywhere = pl.BlockSpec(memory_space=pl.ANY)
    vmem = pl.BlockSpec(memory_space=pltpu.VMEM)
    return pl.pallas_call(
        open_kernel,
        out_shape=[jax.ShapeDtypeStruct((rows // 2, columns), jnp.bfloat16)] * 4
        + [pltpu.VMEM(own.shape, own.dtype)] * 2,
        in_specs=[pl.BlockSpec(memory_space=pltpu.SMEM), anywhere, anywhere, anywhere, anywhere],
        out_specs=[vmem] * 6,
        scratch_shapes=[
            pltpu.VMEM((rows, width), jnp.bfloat16),
            pltpu.SemaphoreType.DMA,
            pltpu.SemaphoreType.DMA((2,)),
        ],
        compiler_params=pltpu.CompilerParams(vmem_limit_bytes=24 * 1024 * 1024),
    )(place, blocks, pltpu.with_memory_space_constraint(own, pltpu.HBM), other, done)


def fit_kernel(slot_ref, sums_ref, values_ref, out_ref, r_ref, d_ref, w_ref):
    half, width = values_ref.shape
    lanes = 512
    upper = lax.broadcasted_iota(jnp.int32, (8, width), 0) < 4
    for i in range(0, half, 8):
        pair = sums_ref[2 * i : 2 * i + 16, :].astype(jnp.float32) + sums_ref[
            2 * (half + i) : 2 * (half + i) + 16, :
        ].astype(jnp.float32)
        a, b = pair[:8], pair[8:]
        r_ref[i : i + 8, :] = jnp.where(upper, a, pltpu.roll(b, 4, 0))
        d_ref[i : i + 8, :] = jnp.where(upper, pltpu.roll(a, 4, 0), b)
    blocks = [(i, j) for i in range(0, half, 8) for j in range(0, width, lanes)]

    def total(acc):
        acc = functools.reduce(jnp.add, [acc[:, k : k + 128] for k in range(0, lanes, 128)])
        acc = acc + pltpu.roll(acc, 4, 0)
        return jnp.broadcast_to(jnp.sum(acc, axis=1, keepdims=True), (8, 128))

    def wide(value):
        return jnp.concatenate([value] * (lanes // 128), axis=1)

    def sweep(scale, last):
        zero = jnp.zeros((8, lanes), jnp.float32)
        crossed, energy, traced, fisher = zero, zero, zero, zero
        scale = wide(scale)
        for i, j in blocks:
            at = (slice(i, i + 8), slice(j, j + lanes))
            lam, resp, design = values_ref[at], r_ref[at], d_ref[at]
            v = scale * lam + 1.0
            inv = pl.reciprocal(v, approx=True)
            inv = inv * (2.0 - v * inv)
            over = design * inv
            crossed = crossed + over * resp
            energy = energy + over * design
            if not last:
                lev = lam * inv
                traced = traced + lev
                fisher = fisher + lev * lev
                w_ref[at] = lev * inv
        return total(crossed), total(energy) + EPSILON, traced, fisher

    log_scale = jnp.zeros((8, 128), jnp.float32)
    for _ in range(ITERS):
        scale = jnp.exp(log_scale)
        crossed, energy, traced, fisher = sweep(scale, False)
        effect = wide(crossed / energy)
        spread = jnp.zeros((8, lanes), jnp.float32)
        for i, j in blocks:
            at = (slice(i, i + 8), slice(j, j + lanes))
            residual = r_ref[at] - effect * d_ref[at]
            spread = spread + w_ref[at] * residual * residual
        gradient = 0.5 * (total(spread) - total(traced))
        log_scale = log_scale + jnp.tanh(gradient / (scale * (0.5 * total(fisher))))
    crossed, energy, _, _ = sweep(jnp.exp(log_scale), True)
    score = crossed / jnp.sqrt(energy)
    lane = lax.broadcasted_iota(jnp.int32, (8, 128), 1)
    row = lax.broadcasted_iota(jnp.int32, (8, 128), 0)
    here = (row < 4) & (lane == 4 * slot_ref[0] + row)
    both = [jnp.sum(jnp.where(here, v, 0.0), axis=0, keepdims=True) for v in (score, log_scale)]
    out_ref[...] = jnp.broadcast_to(
        jnp.concatenate(both, axis=1)[None], (out_ref.shape[0], 1, 256)
    )


def fit(slot, sums, values):
    rows, width = values.shape
    vmem = pl.BlockSpec(memory_space=pltpu.VMEM)
    return pl.pallas_call(
        fit_kernel,
        out_shape=jax.ShapeDtypeStruct((32, 1, 256), jnp.float32),
        in_specs=[pl.BlockSpec(memory_space=pltpu.SMEM), vmem, vmem],
        out_specs=vmem,
        scratch_shapes=[pltpu.VMEM((rows, width), jnp.float32)] * 3,
        compiler_params=pltpu.CompilerParams(vmem_limit_bytes=16 * 1024 * 1024),
    )(slot, sums, values)


def gather_plane(own):
    x, y = "samp_1", "samp_0"
    left = shifted(own, x, 1)
    right = shifted(own, x, -1)
    over = shifted(own, y, 1)
    far = shifted(left, x, 1)
    over_right = shifted(over, x, -1)
    over_left = shifted(left, y, 1)
    over_far = jnp.concatenate(
        [
            shifted(over_left[:48], x, 1),
            shifted(over_right[48:96], x, -1),
            shifted(far[96:], y, 1),
        ],
        axis=0,
    )
    return jnp.stack([own, right, far, left, over, over_right, over_far, over_left])


def smooth_block(widened, places, present, reaches):
    block_len = reaches.shape[0]
    centre = places[HALO : HALO + block_len]
    total_sum = jnp.zeros((block_len,), jnp.float32)
    norm_sum = jnp.zeros((block_len,), jnp.float32)
    for offset in range(2 * HALO + 1):
        near_scores = widened[offset : offset + block_len]
        near_places = places[offset : offset + block_len]
        within = (abs(offset - HALO) <= reaches).astype(jnp.float32)
        kernel = (
            present[offset : offset + block_len]
            * within
            * jnp.exp(-jnp.abs(near_places - centre) / band_width)
        )
        total_sum = total_sum + kernel * near_scores
        norm_sum = norm_sum + kernel
    return total_sum / norm_sum


def copies(value, axes):
    peers = lax.axis_size(axes)
    return lax.all_to_all(
        jnp.broadcast_to(value[None], (peers, *value.shape)), axes, 0, 0, tiled=True
    )


def shards(responses, weights, phenotype, eigvecs, eigvals, positions, reaches):
    z, x, y = lax.axis_index("cpg_0"), lax.axis_index("samp_1"), lax.axis_index("samp_0")
    layers = lax.axis_size("cpg_0")
    with jax.named_scope("weigh"):
        own = weigh(responses, weights, phenotype)
    with jax.named_scope("gather_rows"):
        blocks = gather_plane(own)
    with jax.named_scope("swap_eigvecs"):
        other = shifted(eigvecs, "samp_2", 1)
    with jax.named_scope("gather_values"):
        raw = copies(eigvals, SAMP)
        everywhere = raw.reshape(-1, 2, eigvals.shape[0])
        everywhere = jnp.where(lax.axis_index("samp_2") == 0, everywhere, everywhere[:, ::-1])
        everywhere = jnp.repeat(everywhere.reshape(everywhere.shape[0], -1), 4, axis=0)
    rows = own.shape[0]

    def place(ahead):
        dest = lax.rem(z + ahead + layers, layers)
        across, along = dest // 4, lax.rem(dest, 4)
        return 4 * (across ^ y) + lax.rem(along - x + 4, 4)

    def term(q, ahead):
        block = lax.dynamic_index_in_dim(blocks, place(ahead), 0, keepdims=False)
        return jnp.dot(block, vecs[q], preferred_element_type=jnp.float32)

    far = layers // 2
    sent = {}

    def onward(q, ahead):
        for way in (1, -1):
            got = sent[q, way].astype(jnp.float32)
            if got.shape[0] < rows:
                rest = jnp.zeros_like(got)
                got = jnp.concatenate([got, rest] if way == 1 else [rest, got], axis=0)
            total = (term(q, way * ahead) + got).astype(jnp.bfloat16)
            sent[q, way] = shifted(total, "cpg_0", way)

    def summed(q):
        total = term(q, 0)
        for way in (1, -1):
            total = total + sent[q, way].astype(jnp.float32)
        return total.astype(jnp.bfloat16)

    with jax.named_scope("sum_layers"):
        *halves, near_own, near_other = open_sums(
            place(far)[None], blocks, eigvecs, other, raw
        )
        vecs = (near_own, near_other)
        for q in (0, 1):
            for at, way in enumerate((1, -1)):
                sent[q, way] = shifted(halves[2 * q + at], "cpg_0", way)
        for ahead in range(far - 1, 0, -1):
            onward(0, ahead)
            onward(1, ahead)
        whole = jnp.concatenate([summed(0), summed(1)], axis=1)
    with jax.named_scope("to_components"):
        sums = lax.all_to_all(whole, PLANE, 0, 0, tiled=True)
    with jax.named_scope("fit"):
        slot = lax.axis_index("samp_2") * 16 + lax.axis_index(PLANE)
        fitted = fit(slot.astype(jnp.int32)[None], sums, everywhere)
    with jax.named_scope("gather_scores"):
        layer = jnp.sum(lax.all_to_all(fitted, LAYER, 0, 0, tiled=True), axis=(0, 1))
        beside = [(2 * i, 2 * i + 2) for i in range(layers - 1)]
        beside += [(2 * i + 3, 2 * i + 1) for i in range(layers - 1)]
        other = lax.ppermute(layer, CPG, beside)
        scores, scales = layer[:rows], layer[rows:]
        before, after = other[rows - HALO : rows], other[:HALO]
    with jax.named_scope("smooth"):
        block_len = reaches.shape[0]
        high = lax.axis_index("cpg_1")
        widened = lax.dynamic_slice_in_dim(
            jnp.concatenate([before, scores, after]), high * block_len, block_len + 2 * HALO, 0
        )
        log_scale = lax.dynamic_slice_in_dim(scales, high * block_len, block_len, 0)
        base = lax.axis_index(CPG) * block_len
        total_cpgs = block_len * lax.axis_size(CPG)
        places = lax.dynamic_slice_in_dim(
            jnp.pad(positions.astype(jnp.float32), HALO), base, block_len + 2 * HALO, 0
        )
        global_index = base - HALO + jnp.arange(block_len + 2 * HALO, dtype=jnp.int32)
        present = ((global_index >= 0) & (global_index < total_cpgs)).astype(jnp.float32)
        smoothed = smooth_block(widened, places, present, reaches)
    return (smoothed, log_scale)


def solution(mesh):
    split = Mesh(
        mesh.devices.reshape(2, 4, 2, 8, 2), ("samp_0", "samp_1", "samp_2", "cpg_0", "cpg_1")
    )
    return jax.shard_map(
        shards,
        mesh=split,
        in_specs=(P(SAMP, CPG), P(SAMP, CPG), P(CPG), P(CPG, SAMP), P(SAMP), P(), P(CPG)),
        out_specs=(P(CPG), P(CPG)),
        check_vma=False,
    )
```

```python
import functools

import jax
import jax.numpy as jnp
from jax import lax
from jax.experimental import pallas as pl
from jax.experimental.pallas import tpu as pltpu
from jax.sharding import Mesh
from jax.sharding import PartitionSpec as P

ITERS = 4
HALO = 8
SAMP = ("samp_0", "samp_1", "samp_2")
CPG = ("cpg_0", "cpg_1")
PLANE = ("cpg_1", "samp_0", "samp_1")
FLOOR = ("samp_0", "samp_1")
LAYER = ("cpg_1", "samp_0", "samp_1", "samp_2")

EPSILON = 1e-06
band_width = 1000.0


def shifted(value, axis, by):
    peers = lax.axis_size(axis)
    return lax.ppermute(value, axis, [(i, (i + by) % peers) for i in range(peers)])


def weigh_kernel(resp_ref, weight_ref, trait_ref, out_ref):
    rows = resp_ref.shape[0]
    trait = trait_ref[...]
    for at in range(0, rows, 16):
        root = jnp.sqrt(weight_ref[at : at + 16, :].astype(jnp.float32))
        weighted = root * resp_ref[at : at + 16, :].astype(jnp.float32)
        design = root * trait
        upper = lax.broadcasted_iota(jnp.int32, (8, root.shape[1]), 0) < 4
        tiles = []
        for half in (0, 8):
            a, b = weighted[half : half + 8], design[half : half + 8]
            tiles.append(jnp.where(upper, a, pltpu.roll(b, 4, 0)))
            tiles.append(jnp.where(upper, pltpu.roll(a, 4, 0), b))
        out_ref[2 * at : 2 * at + 32, :] = jnp.concatenate(tiles, axis=0).astype(jnp.bfloat16)


def weigh(responses, weights, phenotype):
    rows, width = responses.shape
    return pl.pallas_call(
        weigh_kernel,
        out_shape=jax.ShapeDtypeStruct((2 * rows, width), jnp.bfloat16),
    )(responses, weights, phenotype[None, :])


def fit_kernel(slot_ref, sums_ref, values_ref, out_ref, r_ref, d_ref, w_ref):
    half, width = values_ref.shape
    lanes = 512
    upper = lax.broadcasted_iota(jnp.int32, (8, width), 0) < 4
    for i in range(0, half, 8):
        pair = sums_ref[2 * i : 2 * i + 16, :].astype(jnp.float32) + sums_ref[
            2 * (half + i) : 2 * (half + i) + 16, :
        ].astype(jnp.float32)
        a, b = pair[:8], pair[8:]
        r_ref[i : i + 8, :] = jnp.where(upper, a, pltpu.roll(b, 4, 0))
        d_ref[i : i + 8, :] = jnp.where(upper, pltpu.roll(a, 4, 0), b)
    blocks = [(i, j) for i in range(0, half, 8) for j in range(0, width, lanes)]

    def total(acc):
        acc = functools.reduce(jnp.add, [acc[:, k : k + 128] for k in range(0, lanes, 128)])
        acc = acc + pltpu.roll(acc, 4, 0)
        return jnp.broadcast_to(jnp.sum(acc, axis=1, keepdims=True), (8, 128))

    def wide(value):
        return jnp.concatenate([value] * (lanes // 128), axis=1)

    def sweep(scale, last):
        zero = jnp.zeros((8, lanes), jnp.float32)
        crossed, energy, traced, fisher = zero, zero, zero, zero
        scale = wide(scale)
        for i, j in blocks:
            at = (slice(i, i + 8), slice(j, j + lanes))
            lam, resp, design = values_ref[at], r_ref[at], d_ref[at]
            v = scale * lam + 1.0
            inv = pl.reciprocal(v, approx=True)
            inv = inv * (2.0 - v * inv)
            over = design * inv
            crossed = crossed + over * resp
            energy = energy + over * design
            if not last:
                lev = lam * inv
                traced = traced + lev
                fisher = fisher + lev * lev
                w_ref[at] = lev * inv
        return total(crossed), total(energy) + EPSILON, traced, fisher

    log_scale = jnp.zeros((8, 128), jnp.float32)
    for _ in range(ITERS):
        scale = jnp.exp(log_scale)
        crossed, energy, traced, fisher = sweep(scale, False)
        effect = wide(crossed / energy)
        spread = jnp.zeros((8, lanes), jnp.float32)
        for i, j in blocks:
            at = (slice(i, i + 8), slice(j, j + lanes))
            residual = r_ref[at] - effect * d_ref[at]
            spread = spread + w_ref[at] * residual * residual
        gradient = 0.5 * (total(spread) - total(traced))
        log_scale = log_scale + jnp.tanh(gradient / (scale * (0.5 * total(fisher))))
    crossed, energy, _, _ = sweep(jnp.exp(log_scale), True)
    score = crossed / jnp.sqrt(energy)
    lane = lax.broadcasted_iota(jnp.int32, (8, 128), 1)
    row = lax.broadcasted_iota(jnp.int32, (8, 128), 0)
    here = (row < 4) & (lane == 4 * slot_ref[0] + row)
    both = [jnp.sum(jnp.where(here, v, 0.0), axis=0, keepdims=True) for v in (score, log_scale)]
    out_ref[...] = jnp.broadcast_to(
        jnp.concatenate(both, axis=1)[None], (out_ref.shape[0], 1, 256)
    )


def fit(slot, sums, values):
    rows, width = values.shape
    vmem = pl.BlockSpec(memory_space=pltpu.VMEM)
    return pl.pallas_call(
        fit_kernel,
        out_shape=jax.ShapeDtypeStruct((32, 1, 256), jnp.float32),
        in_specs=[pl.BlockSpec(memory_space=pltpu.SMEM), vmem, vmem],
        out_specs=vmem,
        scratch_shapes=[pltpu.VMEM((rows, width), jnp.float32)] * 3,
        compiler_params=pltpu.CompilerParams(vmem_limit_bytes=16 * 1024 * 1024),
    )(slot, sums, values)


def gather_plane(own, other):
    x, y = "samp_1", "samp_0"
    left = shifted(own, x, 1)
    right = shifted(own, x, -1)
    over = shifted(own, y, 1)
    far = shifted(left, x, 1)
    over_right = shifted(over, x, -1)
    over_left = shifted(left, y, 1)
    over_far = jnp.concatenate(
        [
            shifted(over_left[:48], x, 1),
            shifted(over_right[48:96], x, -1),
            shifted(far[96:], y, 1),
        ],
        axis=0,
    )
    over_far = over_far + 0 * other[: own.shape[0]]
    return jnp.stack([own, right, far, left, over, over_right, over_far, over_left])


def smooth_block(widened, places, present, reaches):
    block_len = reaches.shape[0]
    centre = places[HALO : HALO + block_len]
    total_sum = jnp.zeros((block_len,), jnp.float32)
    norm_sum = jnp.zeros((block_len,), jnp.float32)
    for offset in range(2 * HALO + 1):
        near_scores = widened[offset : offset + block_len]
        near_places = places[offset : offset + block_len]
        within = (abs(offset - HALO) <= reaches).astype(jnp.float32)
        kernel = (
            present[offset : offset + block_len]
            * within
            * jnp.exp(-jnp.abs(near_places - centre) / band_width)
        )
        total_sum = total_sum + kernel * near_scores
        norm_sum = norm_sum + kernel
    return total_sum / norm_sum


def copies(value, axes):
    peers = lax.axis_size(axes)
    return lax.all_to_all(
        jnp.broadcast_to(value[None], (peers, *value.shape)), axes, 0, 0, tiled=True
    )


def shards(responses, weights, phenotype, eigvecs, eigvals, positions, reaches):
    z, x, y = lax.axis_index("cpg_0"), lax.axis_index("samp_1"), lax.axis_index("samp_0")
    layers = lax.axis_size("cpg_0")
    with jax.named_scope("swap_eigvecs"):
        other = shifted(eigvecs, "samp_2", 1)
        vecs = (eigvecs, other)
    with jax.named_scope("weigh"):
        own = weigh(responses, weights, phenotype)
    with jax.named_scope("gather_rows"):
        blocks = gather_plane(own, other)
    with jax.named_scope("gather_values"):
        everywhere = copies(eigvals, SAMP).reshape(-1, 2, eigvals.shape[0])
        everywhere = jnp.where(lax.axis_index("samp_2") == 0, everywhere, everywhere[:, ::-1])
        everywhere = jnp.repeat(everywhere.reshape(everywhere.shape[0], -1), 4, axis=0)
    rows = own.shape[0]

    def term(q, ahead, lo, hi):
        dest = lax.rem(z + ahead + layers, layers)
        across, along = dest // 4, lax.rem(dest, 4)
        place = 4 * (across ^ y) + lax.rem(along - x + 4, 4)
        block = lax.dynamic_index_in_dim(blocks, place, 0, keepdims=False)[lo:hi]
        return jnp.dot(block, vecs[q], preferred_element_type=jnp.float32)

    far = layers // 2
    cut = rows // 2
    sent = {}

    def first(q):
        sent[q, 1] = shifted(term(q, far, 0, cut).astype(jnp.bfloat16), "cpg_0", 1)
        sent[q, -1] = shifted(term(q, far, cut, rows).astype(jnp.bfloat16), "cpg_0", -1)

    def onward(q, ahead):
        for way in (1, -1):
            got = sent[q, way].astype(jnp.float32)
            if got.shape[0] < rows:
                rest = jnp.zeros_like(got)
                got = jnp.concatenate([got, rest] if way == 1 else [rest, got], axis=0)
            total = (term(q, way * ahead, 0, rows) + got).astype(jnp.bfloat16)
            sent[q, way] = shifted(total, "cpg_0", way)

    def summed(q):
        total = term(q, 0, 0, rows)
        for way in (1, -1):
            total = total + sent[q, way].astype(jnp.float32)
        return total.astype(jnp.bfloat16)

    with jax.named_scope("sum_layers"):
        first(0)
        first(1)
        for ahead in range(far - 1, 0, -1):
            onward(0, ahead)
            onward(1, ahead)
        whole = jnp.concatenate([summed(0), summed(1)], axis=1)
    with jax.named_scope("to_components"):
        sums = lax.all_to_all(whole, PLANE, 0, 0, tiled=True)
    with jax.named_scope("fit"):
        slot = lax.axis_index("samp_2") * 16 + lax.axis_index(PLANE)
        fitted = fit(slot.astype(jnp.int32)[None], sums, everywhere)
    with jax.named_scope("gather_scores"):
        layer = jnp.sum(lax.all_to_all(fitted, LAYER, 0, 0, tiled=True), axis=(0, 1))
        beside = [(2 * i, 2 * i + 2) for i in range(layers - 1)]
        beside += [(2 * i + 3, 2 * i + 1) for i in range(layers - 1)]
        other = lax.ppermute(layer, CPG, beside)
        scores, scales = layer[:rows], layer[rows:]
        before, after = other[rows - HALO : rows], other[:HALO]
    with jax.named_scope("smooth"):
        block_len = reaches.shape[0]
        high = lax.axis_index("cpg_1")
        widened = lax.dynamic_slice_in_dim(
            jnp.concatenate([before, scores, after]), high * block_len, block_len + 2 * HALO, 0
        )
        log_scale = lax.dynamic_slice_in_dim(scales, high * block_len, block_len, 0)
        base = lax.axis_index(CPG) * block_len
        total_cpgs = block_len * lax.axis_size(CPG)
        places = lax.dynamic_slice_in_dim(
            jnp.pad(positions.astype(jnp.float32), HALO), base, block_len + 2 * HALO, 0
        )
        global_index = base - HALO + jnp.arange(block_len + 2 * HALO, dtype=jnp.int32)
        present = ((global_index >= 0) & (global_index < total_cpgs)).astype(jnp.float32)
        smoothed = smooth_block(widened, places, present, reaches)
    return (smoothed, log_scale)


def solution(mesh):
    split = Mesh(
        mesh.devices.reshape(2, 4, 2, 8, 2), ("samp_0", "samp_1", "samp_2", "cpg_0", "cpg_1")
    )
    return jax.shard_map(
        shards,
        mesh=split,
        in_specs=(P(SAMP, CPG), P(SAMP, CPG), P(CPG), P(CPG, SAMP), P(SAMP), P(), P(CPG)),
        out_specs=(P(CPG), P(CPG)),
        check_vma=False,
    )
```

```python
import functools

import jax
import jax.numpy as jnp
from jax import lax
from jax.experimental import pallas as pl
from jax.experimental.pallas import tpu as pltpu
from jax.sharding import Mesh
from jax.sharding import PartitionSpec as P

ITERS = 4
HALO = 8
SAMP = ("samp_0", "samp_1", "samp_2")
CPG = ("cpg_0", "cpg_1")
PLANE = ("cpg_1", "samp_0", "samp_1")
FLOOR = ("samp_0", "samp_1")
LAYER = ("cpg_1", "samp_0", "samp_1", "samp_2")

EPSILON = 1e-06
band_width = 1000.0


def shifted(value, axis, by):
    peers = lax.axis_size(axis)
    return lax.ppermute(value, axis, [(i, (i + by) % peers) for i in range(peers)])


CUT = 64
EXTRA = 16


def weigh_kernel(resp_ref, weight_ref, trait_ref, values_ref, first_ref, second_ref):
    trait = trait_ref[...]
    width = trait.shape[1]
    upper = lax.broadcasted_iota(jnp.int32, (8, width), 0) < 4
    for at in range(0, resp_ref.shape[0], 16):
        root = jnp.sqrt(weight_ref[at : at + 16, :].astype(jnp.float32))
        weighted = root * resp_ref[at : at + 16, :].astype(jnp.float32)
        design = root * trait
        tiles = []
        for half in (0, 8):
            a, b = weighted[half : half + 8], design[half : half + 8]
            tiles.append(jnp.where(upper, a, pltpu.roll(b, 4, 0)))
            tiles.append(jnp.where(upper, pltpu.roll(a, 4, 0), b))
        out_ref, base = (first_ref, 0) if 2 * at < CUT else (second_ref, CUT)
        out_ref[2 * at - base : 2 * at - base + 32, :] = jnp.concatenate(tiles, axis=0).astype(
            jnp.bfloat16
        )
    rest = values_ref[...]
    row = lax.broadcasted_iota(jnp.int32, (EXTRA, width), 0)
    parts = jnp.zeros((EXTRA, width), jnp.float32)
    for k in range(3):
        part = rest.astype(jnp.bfloat16).astype(jnp.float32)
        parts = jnp.where(row == k, part, parts)
        rest = rest - part
    bottom = second_ref.shape[0] - EXTRA
    second_ref[bottom:, :] = parts.astype(jnp.bfloat16)


def weigh(responses, weights, phenotype, eigvals):
    rows, width = responses.shape
    return pl.pallas_call(
        weigh_kernel,
        out_shape=[
            jax.ShapeDtypeStruct((CUT, width), jnp.bfloat16),
            jax.ShapeDtypeStruct((2 * rows - CUT + EXTRA, width), jnp.bfloat16),
        ],
    )(responses, weights, phenotype[None, :], eigvals[None, :])


def stack_kernel(ahead_ref, chip_ref, *refs):
    *pieces, _, blocks_ref, values_ref, parts_ref, sems = refs
    rows = blocks_ref.shape[1]
    copies = []
    for place in range(8):
        at, given = 0, pieces[place * 2 : place * 2 + 2] if place < 7 else pieces[14:]
        for piece in given:
            count = min(piece.shape[0], rows - at)
            sem = sems.at[len(copies)]
            copies.append(
                pltpu.make_async_copy(
                    piece.at[pl.ds(0, count)],
                    blocks_ref.at[ahead_ref[place], pl.ds(at, count)],
                    sem,
                )
            )
            at += count
        sem = sems.at[len(copies)]
        copies.append(
            pltpu.make_async_copy(
                given[-1].at[pl.ds(given[-1].shape[0] - EXTRA, EXTRA)],
                parts_ref.at[chip_ref[place]],
                sem,
            )
        )
    for copy in copies:
        copy.start()
    for copy in copies:
        copy.wait()
    for chip in range(8):
        parts = parts_ref[chip].astype(jnp.float32)
        values_ref[chip : chip + 1, :] = parts[0:1] + parts[1:2] + parts[2:3]


def stack(ahead, chip, pieces, last, rows):
    width = pieces[0].shape[1]
    smem = pl.BlockSpec(memory_space=pltpu.SMEM)
    anywhere = pl.BlockSpec(memory_space=pl.ANY)
    return pl.pallas_call(
        stack_kernel,
        out_shape=[
            jax.ShapeDtypeStruct((8, rows, width), jnp.bfloat16),
            jax.ShapeDtypeStruct((8, width), jnp.float32),
        ],
        in_specs=[smem, smem] + [anywhere] * (len(pieces) + 1),
        out_specs=[anywhere, pl.BlockSpec(memory_space=pltpu.VMEM)],
        scratch_shapes=[
            pltpu.VMEM((8, EXTRA, width), jnp.bfloat16),
            pltpu.SemaphoreType.DMA((len(pieces) + 8,)),
        ],
        compiler_params=pltpu.CompilerParams(vmem_limit_bytes=4 * 1024 * 1024),
    )(ahead, chip, *pieces, last)


def fit_kernel(slot_ref, sums_ref, values_ref, out_ref, r_ref, d_ref, w_ref):
    half, width = values_ref.shape
    lanes = 512
    upper = lax.broadcasted_iota(jnp.int32, (8, width), 0) < 4
    for i in range(0, half, 8):
        pair = sums_ref[2 * i : 2 * i + 16, :].astype(jnp.float32) + sums_ref[
            2 * (half + i) : 2 * (half + i) + 16, :
        ].astype(jnp.float32)
        a, b = pair[:8], pair[8:]
        r_ref[i : i + 8, :] = jnp.where(upper, a, pltpu.roll(b, 4, 0))
        d_ref[i : i + 8, :] = jnp.where(upper, pltpu.roll(a, 4, 0), b)
    blocks = [(i, j) for i in range(0, half, 8) for j in range(0, width, lanes)]

    def total(acc):
        acc = functools.reduce(jnp.add, [acc[:, k : k + 128] for k in range(0, lanes, 128)])
        acc = acc + pltpu.roll(acc, 4, 0)
        return jnp.broadcast_to(jnp.sum(acc, axis=1, keepdims=True), (8, 128))

    def wide(value):
        return jnp.concatenate([value] * (lanes // 128), axis=1)

    def sweep(scale, last):
        zero = jnp.zeros((8, lanes), jnp.float32)
        crossed, energy, traced, fisher = zero, zero, zero, zero
        scale = wide(scale)
        for i, j in blocks:
            at = (slice(i, i + 8), slice(j, j + lanes))
            lam, resp, design = values_ref[at], r_ref[at], d_ref[at]
            v = scale * lam + 1.0
            inv = pl.reciprocal(v, approx=True)
            inv = inv * (2.0 - v * inv)
            over = design * inv
            crossed = crossed + over * resp
            energy = energy + over * design
            if not last:
                lev = lam * inv
                traced = traced + lev
                fisher = fisher + lev * lev
                w_ref[at] = lev * inv
        return total(crossed), total(energy) + EPSILON, traced, fisher

    log_scale = jnp.zeros((8, 128), jnp.float32)
    for _ in range(ITERS):
        scale = jnp.exp(log_scale)
        crossed, energy, traced, fisher = sweep(scale, False)
        effect = wide(crossed / energy)
        spread = jnp.zeros((8, lanes), jnp.float32)
        for i, j in blocks:
            at = (slice(i, i + 8), slice(j, j + lanes))
            residual = r_ref[at] - effect * d_ref[at]
            spread = spread + w_ref[at] * residual * residual
        gradient = 0.5 * (total(spread) - total(traced))
        log_scale = log_scale + jnp.tanh(gradient / (scale * (0.5 * total(fisher))))
    crossed, energy, _, _ = sweep(jnp.exp(log_scale), True)
    score = crossed / jnp.sqrt(energy)
    lane = lax.broadcasted_iota(jnp.int32, (8, 128), 1)
    row = lax.broadcasted_iota(jnp.int32, (8, 128), 0)
    here = (row < 4) & (lane == 4 * slot_ref[0] + row)
    both = [jnp.sum(jnp.where(here, v, 0.0), axis=0, keepdims=True) for v in (score, log_scale)]
    out_ref[...] = jnp.broadcast_to(
        jnp.concatenate(both, axis=1)[None], (out_ref.shape[0], 1, 256)
    )


def fit(slot, sums, values):
    rows, width = values.shape
    vmem = pl.BlockSpec(memory_space=pltpu.VMEM)
    return pl.pallas_call(
        fit_kernel,
        out_shape=jax.ShapeDtypeStruct((32, 1, 256), jnp.float32),
        in_specs=[pl.BlockSpec(memory_space=pltpu.SMEM), vmem, vmem],
        out_specs=vmem,
        scratch_shapes=[pltpu.VMEM((rows, width), jnp.float32)] * 3,
        compiler_params=pltpu.CompilerParams(vmem_limit_bytes=16 * 1024 * 1024),
    )(slot, sums, values)


def gather_plane(halves):
    x, y = "samp_1", "samp_0"
    got = []
    for own in halves:
        left = shifted(own, x, 1)
        right = shifted(own, x, -1)
        over = shifted(own, y, 1)
        got.append([own, right, None, left, over, None, None])
    for each in got:
        _, _, _, left, over, _, _ = each
        each[2] = shifted(left, x, 1)
        each[5] = shifted(over, x, -1)
        each[6] = shifted(left, y, 1)
    first, second = got
    farthest = [
        shifted(first[6], x, 1),
        shifted(second[5][:48], x, -1),
        shifted(second[2][48:], y, 1),
    ]
    return [piece for place in zip(first, second) for piece in place] + farthest


def smooth_block(widened, places, present, reaches):
    block_len = reaches.shape[0]
    centre = places[HALO : HALO + block_len]
    total_sum = jnp.zeros((block_len,), jnp.float32)
    norm_sum = jnp.zeros((block_len,), jnp.float32)
    for offset in range(2 * HALO + 1):
        near_scores = widened[offset : offset + block_len]
        near_places = places[offset : offset + block_len]
        within = (abs(offset - HALO) <= reaches).astype(jnp.float32)
        kernel = (
            present[offset : offset + block_len]
            * within
            * jnp.exp(-jnp.abs(near_places - centre) / band_width)
        )
        total_sum = total_sum + kernel * near_scores
        norm_sum = norm_sum + kernel
    return total_sum / norm_sum


def copies(value, axes):
    peers = lax.axis_size(axes)
    return lax.all_to_all(
        jnp.broadcast_to(value[None], (peers, *value.shape)), axes, 0, 0, tiled=True
    )


def shards(responses, weights, phenotype, eigvecs, eigvals, positions, reaches):
    z, x, y = lax.axis_index("cpg_0"), lax.axis_index("samp_1"), lax.axis_index("samp_0")
    layers = lax.axis_size("cpg_0")
    with jax.named_scope("swap_eigvecs"):
        other = shifted(eigvecs, "samp_2", 1)
        vecs = (eigvecs, other)
    with jax.named_scope("weigh"):
        halves = weigh(responses, weights, phenotype, eigvals)
    rows = 2 * responses.shape[0]
    with jax.named_scope("gather_rows"):
        place = jnp.array([0, 1, 2, 3, 4, 5, 7, 6], jnp.int32)
        chip = (4 * (y ^ (place // 4)) + (x + place) % 4).astype(jnp.int32)
        ahead = ((chip - z) % layers).astype(jnp.int32)
        blocks, values = stack(ahead, chip, gather_plane(halves), other, rows)
    with jax.named_scope("gather_values"):
        values = jnp.concatenate([values, shifted(values, "samp_2", 1)], axis=1)
        everywhere = jnp.repeat(values, 4, axis=0)

    def term(q, ahead, lo, hi):
        block = blocks[ahead % layers, lo:hi]
        return jnp.dot(block, vecs[q], preferred_element_type=jnp.float32)

    far = layers // 2
    cut = rows // 2
    sent = {}

    def first(q):
        sent[q, 1] = shifted(term(q, far, 0, cut).astype(jnp.bfloat16), "cpg_0", 1)
        sent[q, -1] = shifted(term(q, far, cut, rows).astype(jnp.bfloat16), "cpg_0", -1)

    def onward(q, ahead):
        for way in (1, -1):
            got = sent[q, way].astype(jnp.float32)
            if got.shape[0] < rows:
                rest = jnp.zeros_like(got)
                got = jnp.concatenate([got, rest] if way == 1 else [rest, got], axis=0)
            total = (term(q, way * ahead, 0, rows) + got).astype(jnp.bfloat16)
            sent[q, way] = shifted(total, "cpg_0", way)

    def summed(q):
        total = term(q, 0, 0, rows)
        for way in (1, -1):
            total = total + sent[q, way].astype(jnp.float32)
        return total.astype(jnp.bfloat16)

    with jax.named_scope("sum_layers"):
        first(0)
        first(1)
        for ahead in range(far - 1, 0, -1):
            onward(0, ahead)
            onward(1, ahead)
        whole = jnp.concatenate([summed(0), summed(1)], axis=1)
    with jax.named_scope("to_components"):
        sums = lax.all_to_all(whole, PLANE, 0, 0, tiled=True)
    with jax.named_scope("fit"):
        slot = lax.axis_index("samp_2") * 16 + lax.axis_index(PLANE)
        fitted = fit(slot.astype(jnp.int32)[None], sums, everywhere)
    with jax.named_scope("gather_scores"):
        layer = jnp.sum(lax.all_to_all(fitted, LAYER, 0, 0, tiled=True), axis=(0, 1))
        beside = [(2 * i, 2 * i + 2) for i in range(layers - 1)]
        beside += [(2 * i + 3, 2 * i + 1) for i in range(layers - 1)]
        other = lax.ppermute(layer, CPG, beside)
        scores, scales = layer[:rows], layer[rows:]
        before, after = other[rows - HALO : rows], other[:HALO]
    with jax.named_scope("smooth"):
        block_len = reaches.shape[0]
        high = lax.axis_index("cpg_1")
        widened = lax.dynamic_slice_in_dim(
            jnp.concatenate([before, scores, after]), high * block_len, block_len + 2 * HALO, 0
        )
        log_scale = lax.dynamic_slice_in_dim(scales, high * block_len, block_len, 0)
        base = lax.axis_index(CPG) * block_len
        total_cpgs = block_len * lax.axis_size(CPG)
        places = lax.dynamic_slice_in_dim(
            jnp.pad(positions.astype(jnp.float32), HALO), base, block_len + 2 * HALO, 0
        )
        global_index = base - HALO + jnp.arange(block_len + 2 * HALO, dtype=jnp.int32)
        present = ((global_index >= 0) & (global_index < total_cpgs)).astype(jnp.float32)
        smoothed = smooth_block(widened, places, present, reaches)
    return (smoothed, log_scale)


def solution(mesh):
    split = Mesh(
        mesh.devices.reshape(2, 4, 2, 8, 2), ("samp_0", "samp_1", "samp_2", "cpg_0", "cpg_1")
    )
    return jax.shard_map(
        shards,
        mesh=split,
        in_specs=(P(SAMP, CPG), P(SAMP, CPG), P(CPG), P(CPG, SAMP), P(SAMP), P(), P(CPG)),
        out_specs=(P(CPG), P(CPG)),
        check_vma=False,
    )
```

```python
import functools

import jax
import jax.numpy as jnp
from jax import lax
from jax.experimental import pallas as pl
from jax.experimental.pallas import tpu as pltpu
from jax.sharding import Mesh
from jax.sharding import PartitionSpec as P

ITERS = 4
HALO = 8
SAMP = ("samp_0", "samp_1", "samp_2")
CPG = ("cpg_0", "cpg_1")
PLANE = ("cpg_1", "samp_0", "samp_1")
FLOOR = ("samp_0", "samp_1")
LAYER = ("cpg_1", "samp_0", "samp_1", "samp_2")

EPSILON = 1e-06
band_width = 1000.0


def shifted(value, axis, by):
    peers = lax.axis_size(axis)
    return lax.ppermute(value, axis, [(i, (i + by) % peers) for i in range(peers)])


def weigh_kernel(resp_ref, weight_ref, trait_ref, out_ref):
    rows = resp_ref.shape[0]
    trait = trait_ref[...]
    for at in range(0, rows, 16):
        root = jnp.sqrt(weight_ref[at : at + 16, :].astype(jnp.float32))
        weighted = root * resp_ref[at : at + 16, :].astype(jnp.float32)
        design = root * trait
        upper = lax.broadcasted_iota(jnp.int32, (8, root.shape[1]), 0) < 4
        tiles = []
        for half in (0, 8):
            a, b = weighted[half : half + 8], design[half : half + 8]
            tiles.append(jnp.where(upper, a, pltpu.roll(b, 4, 0)))
            tiles.append(jnp.where(upper, pltpu.roll(a, 4, 0), b))
        out_ref[2 * at : 2 * at + 32, :] = jnp.concatenate(tiles, axis=0).astype(jnp.bfloat16)


def weigh(responses, weights, phenotype):
    rows, width = responses.shape
    return pl.pallas_call(
        weigh_kernel,
        out_shape=jax.ShapeDtypeStruct((2 * rows, width), jnp.bfloat16),
    )(responses, weights, phenotype[None, :])


def fit_kernel(slot_ref, sums_ref, values_ref, out_ref, r_ref, d_ref, w_ref):
    half, width = values_ref.shape
    lanes = 512
    upper = lax.broadcasted_iota(jnp.int32, (8, width), 0) < 4
    for i in range(0, half, 8):
        pair = sums_ref[2 * i : 2 * i + 16, :].astype(jnp.float32) + sums_ref[
            2 * (half + i) : 2 * (half + i) + 16, :
        ].astype(jnp.float32)
        a, b = pair[:8], pair[8:]
        r_ref[i : i + 8, :] = jnp.where(upper, a, pltpu.roll(b, 4, 0))
        d_ref[i : i + 8, :] = jnp.where(upper, pltpu.roll(a, 4, 0), b)
    blocks = [(i, j) for i in range(0, half, 8) for j in range(0, width, lanes)]

    def total(acc):
        acc = functools.reduce(jnp.add, [acc[:, k : k + 128] for k in range(0, lanes, 128)])
        acc = acc + pltpu.roll(acc, 4, 0)
        return jnp.broadcast_to(jnp.sum(acc, axis=1, keepdims=True), (8, 128))

    def wide(value):
        return jnp.concatenate([value] * (lanes // 128), axis=1)

    def sweep(scale, last):
        zero = jnp.zeros((8, lanes), jnp.float32)
        crossed, energy, traced, fisher = zero, zero, zero, zero
        scale = wide(scale)
        for i, j in blocks:
            at = (slice(i, i + 8), slice(j, j + lanes))
            lam, resp, design = values_ref[at], r_ref[at], d_ref[at]
            v = scale * lam + 1.0
            inv = pl.reciprocal(v, approx=True)
            inv = inv * (2.0 - v * inv)
            over = design * inv
            crossed = crossed + over * resp
            energy = energy + over * design
            if not last:
                lev = lam * inv
                traced = traced + lev
                fisher = fisher + lev * lev
                w_ref[at] = lev * inv
        return total(crossed), total(energy) + EPSILON, traced, fisher

    log_scale = jnp.zeros((8, 128), jnp.float32)
    for _ in range(ITERS):
        scale = jnp.exp(log_scale)
        crossed, energy, traced, fisher = sweep(scale, False)
        effect = wide(crossed / energy)
        spread = jnp.zeros((8, lanes), jnp.float32)
        for i, j in blocks:
            at = (slice(i, i + 8), slice(j, j + lanes))
            residual = r_ref[at] - effect * d_ref[at]
            spread = spread + w_ref[at] * residual * residual
        gradient = 0.5 * (total(spread) - total(traced))
        log_scale = log_scale + jnp.tanh(gradient / (scale * (0.5 * total(fisher))))
    crossed, energy, _, _ = sweep(jnp.exp(log_scale), True)
    score = crossed / jnp.sqrt(energy)
    lane = lax.broadcasted_iota(jnp.int32, (8, 128), 1)
    row = lax.broadcasted_iota(jnp.int32, (8, 128), 0)
    here = (row < 4) & (lane == 4 * slot_ref[0] + row)
    both = [jnp.sum(jnp.where(here, v, 0.0), axis=0, keepdims=True) for v in (score, log_scale)]
    out_ref[...] = jnp.broadcast_to(
        jnp.concatenate(both, axis=1)[None], (out_ref.shape[0], 1, 256)
    )


def fit(slot, sums, values):
    rows, width = values.shape
    vmem = pl.BlockSpec(memory_space=pltpu.VMEM)
    return pl.pallas_call(
        fit_kernel,
        out_shape=jax.ShapeDtypeStruct((32, 1, 256), jnp.float32),
        in_specs=[pl.BlockSpec(memory_space=pltpu.SMEM), vmem, vmem],
        out_specs=vmem,
        scratch_shapes=[pltpu.VMEM((rows, width), jnp.float32)] * 3,
        compiler_params=pltpu.CompilerParams(vmem_limit_bytes=16 * 1024 * 1024),
    )(slot, sums, values)


def gather_plane(own, other):
    x, y = "samp_1", "samp_0"
    left = shifted(own, x, 1)
    right = shifted(own, x, -1)
    over = shifted(own, y, 1)
    floor = lax.axis_size(x)

    def across(value, by):
        pairs = [
            (floor * v + u, floor * (1 - v) + (u + by) % floor) for v in (0, 1) for u in range(floor)
        ]
        return lax.ppermute(value, (y, x), pairs)

    over_left = shifted(left, y, 1)
    over_far = across(right, -1)
    over_right = shifted(over, x, -1)
    far = shifted(left, x, 1)
    over_far = over_far + 0 * other[: own.shape[0]]
    return jnp.stack([over_left, own, right, far, left, over, over_right, over_far])


def smooth_block(widened, places, present, reaches):
    block_len = reaches.shape[0]
    centre = places[HALO : HALO + block_len]
    total_sum = jnp.zeros((block_len,), jnp.float32)
    norm_sum = jnp.zeros((block_len,), jnp.float32)
    for offset in range(2 * HALO + 1):
        near_scores = widened[offset : offset + block_len]
        near_places = places[offset : offset + block_len]
        within = (abs(offset - HALO) <= reaches).astype(jnp.float32)
        kernel = (
            present[offset : offset + block_len]
            * within
            * jnp.exp(-jnp.abs(near_places - centre) / band_width)
        )
        total_sum = total_sum + kernel * near_scores
        norm_sum = norm_sum + kernel
    return total_sum / norm_sum


def copies(value, axes):
    peers = lax.axis_size(axes)
    return lax.all_to_all(
        jnp.broadcast_to(value[None], (peers, *value.shape)), axes, 0, 0, tiled=True
    )


def shards(responses, weights, phenotype, eigvecs, eigvals, positions, reaches):
    z, x, y = lax.axis_index("cpg_0"), lax.axis_index("samp_1"), lax.axis_index("samp_0")
    layers = lax.axis_size("cpg_0")
    with jax.named_scope("swap_eigvecs"):
        other = shifted(eigvecs, "samp_2", 1)
        vecs = (eigvecs, other)
    with jax.named_scope("weigh"):
        own = weigh(responses, weights, phenotype)
    with jax.named_scope("gather_rows"):
        blocks = gather_plane(own, other)
    with jax.named_scope("gather_values"):
        everywhere = copies(eigvals, SAMP).reshape(-1, 2, eigvals.shape[0])
        everywhere = jnp.where(lax.axis_index("samp_2") == 0, everywhere, everywhere[:, ::-1])
        everywhere = jnp.repeat(everywhere.reshape(everywhere.shape[0], -1), 4, axis=0)
    rows = own.shape[0]

    def term(q, ahead, lo, hi):
        dest = lax.rem(z + ahead + layers, layers)
        across, along = dest // 4, lax.rem(dest, 4)
        place = (4 * (across ^ y) + lax.rem(along - x + 4, 4) + 1) & 7
        block = lax.dynamic_index_in_dim(blocks, place, 0, keepdims=False)[lo:hi]
        return jnp.dot(block, vecs[q], preferred_element_type=jnp.float32)

    far = layers // 2
    cut = rows // 2
    sent = {}

    def first(q):
        sent[q, 1] = shifted(term(q, far, 0, cut).astype(jnp.bfloat16), "cpg_0", 1)
        sent[q, -1] = shifted(term(q, far, cut, rows).astype(jnp.bfloat16), "cpg_0", -1)

    def onward(q, ahead):
        for way in (1, -1):
            got = sent[q, way].astype(jnp.float32)
            if got.shape[0] < rows:
                rest = jnp.zeros_like(got)
                got = jnp.concatenate([got, rest] if way == 1 else [rest, got], axis=0)
            total = (term(q, way * ahead, 0, rows) + got).astype(jnp.bfloat16)
            sent[q, way] = shifted(total, "cpg_0", way)

    def summed(q):
        total = term(q, 0, 0, rows)
        for way in (1, -1):
            total = total + sent[q, way].astype(jnp.float32)
        return total.astype(jnp.bfloat16)

    with jax.named_scope("sum_layers"):
        first(0)
        first(1)
        for ahead in range(far - 1, 0, -1):
            onward(0, ahead)
            onward(1, ahead)
        whole = jnp.concatenate([summed(0), summed(1)], axis=1)
    with jax.named_scope("to_components"):
        sums = lax.all_to_all(whole, PLANE, 0, 0, tiled=True)
    with jax.named_scope("fit"):
        slot = lax.axis_index("samp_2") * 16 + lax.axis_index(PLANE)
        fitted = fit(slot.astype(jnp.int32)[None], sums, everywhere)
    with jax.named_scope("gather_scores"):
        layer = jnp.sum(lax.all_to_all(fitted, LAYER, 0, 0, tiled=True), axis=(0, 1))
        beside = [(2 * i, 2 * i + 2) for i in range(layers - 1)]
        beside += [(2 * i + 3, 2 * i + 1) for i in range(layers - 1)]
        other = lax.ppermute(layer, CPG, beside)
        scores, scales = layer[:rows], layer[rows:]
        before, after = other[rows - HALO : rows], other[:HALO]
    with jax.named_scope("smooth"):
        block_len = reaches.shape[0]
        high = lax.axis_index("cpg_1")
        widened = lax.dynamic_slice_in_dim(
            jnp.concatenate([before, scores, after]), high * block_len, block_len + 2 * HALO, 0
        )
        log_scale = lax.dynamic_slice_in_dim(scales, high * block_len, block_len, 0)
        base = lax.axis_index(CPG) * block_len
        total_cpgs = block_len * lax.axis_size(CPG)
        places = lax.dynamic_slice_in_dim(
            jnp.pad(positions.astype(jnp.float32), HALO), base, block_len + 2 * HALO, 0
        )
        global_index = base - HALO + jnp.arange(block_len + 2 * HALO, dtype=jnp.int32)
        present = ((global_index >= 0) & (global_index < total_cpgs)).astype(jnp.float32)
        smoothed = smooth_block(widened, places, present, reaches)
    return (smoothed, log_scale)


def solution(mesh):
    split = Mesh(
        mesh.devices.reshape(2, 4, 2, 8, 2), ("samp_0", "samp_1", "samp_2", "cpg_0", "cpg_1")
    )
    return jax.shard_map(
        shards,
        mesh=split,
        in_specs=(P(SAMP, CPG), P(SAMP, CPG), P(CPG), P(CPG, SAMP), P(SAMP), P(), P(CPG)),
        out_specs=(P(CPG), P(CPG)),
        check_vma=False,
    )
```

```python
import functools

import jax
import jax.numpy as jnp
from jax import lax
from jax.experimental import pallas as pl
from jax.experimental.pallas import tpu as pltpu
from jax.sharding import Mesh
from jax.sharding import PartitionSpec as P

ITERS = 4
HALO = 8
SAMP = ("samp_0", "samp_1", "samp_2")
CPG = ("cpg_0", "cpg_1")
PLANE = ("cpg_1", "samp_0", "samp_1")
FLOOR = ("samp_0", "samp_1")
LAYER = ("cpg_1", "samp_0", "samp_1", "samp_2")

EPSILON = 1e-06
band_width = 1000.0


def shifted(value, axis, by):
    peers = lax.axis_size(axis)
    return lax.ppermute(value, axis, [(i, (i + by) % peers) for i in range(peers)])


EXTRA = 16


def weigh_kernel(resp_ref, weight_ref, trait_ref, values_ref, out_ref):
    trait = trait_ref[...]
    width = trait.shape[1]
    upper = lax.broadcasted_iota(jnp.int32, (8, width), 0) < 4
    for at in range(0, resp_ref.shape[0], 16):
        root = jnp.sqrt(weight_ref[at : at + 16, :].astype(jnp.float32))
        weighted = root * resp_ref[at : at + 16, :].astype(jnp.float32)
        design = root * trait
        tiles = []
        for half in (0, 8):
            a, b = weighted[half : half + 8], design[half : half + 8]
            tiles.append(jnp.where(upper, a, pltpu.roll(b, 4, 0)))
            tiles.append(jnp.where(upper, pltpu.roll(a, 4, 0), b))
        out_ref[2 * at : 2 * at + 32, :] = jnp.concatenate(tiles, axis=0).astype(jnp.bfloat16)
    rest = values_ref[...]
    row = lax.broadcasted_iota(jnp.int32, (EXTRA, width), 0)
    parts = jnp.zeros((EXTRA, width), jnp.float32)
    for k in range(3):
        part = rest.astype(jnp.bfloat16).astype(jnp.float32)
        parts = jnp.where(row == k, part, parts)
        rest = rest - part
    out_ref[out_ref.shape[0] - EXTRA :, :] = parts.astype(jnp.bfloat16)


def weigh(responses, weights, phenotype, eigvals):
    rows, width = responses.shape
    return pl.pallas_call(
        weigh_kernel,
        out_shape=jax.ShapeDtypeStruct((2 * rows + EXTRA, width), jnp.bfloat16),
    )(responses, weights, phenotype[None, :], eigvals[None, :])


def fit_kernel(slot_ref, sums_ref, values_ref, out_ref, r_ref, d_ref, w_ref):
    half, width = values_ref.shape
    lanes = 512
    upper = lax.broadcasted_iota(jnp.int32, (8, width), 0) < 4
    for i in range(0, half, 8):
        pair = sums_ref[2 * i : 2 * i + 16, :].astype(jnp.float32) + sums_ref[
            2 * (half + i) : 2 * (half + i) + 16, :
        ].astype(jnp.float32)
        a, b = pair[:8], pair[8:]
        r_ref[i : i + 8, :] = jnp.where(upper, a, pltpu.roll(b, 4, 0))
        d_ref[i : i + 8, :] = jnp.where(upper, pltpu.roll(a, 4, 0), b)
    blocks = [(i, j) for i in range(0, half, 8) for j in range(0, width, lanes)]

    def total(acc):
        acc = functools.reduce(jnp.add, [acc[:, k : k + 128] for k in range(0, lanes, 128)])
        acc = acc + pltpu.roll(acc, 4, 0)
        return jnp.broadcast_to(jnp.sum(acc, axis=1, keepdims=True), (8, 128))

    def wide(value):
        return jnp.concatenate([value] * (lanes // 128), axis=1)

    def sweep(scale, last):
        zero = jnp.zeros((8, lanes), jnp.float32)
        crossed, energy, traced, fisher = zero, zero, zero, zero
        scale = wide(scale)
        for i, j in blocks:
            at = (slice(i, i + 8), slice(j, j + lanes))
            lam, resp, design = values_ref[at], r_ref[at], d_ref[at]
            v = scale * lam + 1.0
            inv = pl.reciprocal(v, approx=True)
            inv = inv * (2.0 - v * inv)
            over = design * inv
            crossed = crossed + over * resp
            energy = energy + over * design
            if not last:
                lev = lam * inv
                traced = traced + lev
                fisher = fisher + lev * lev
                w_ref[at] = lev * inv
        return total(crossed), total(energy) + EPSILON, traced, fisher

    log_scale = jnp.zeros((8, 128), jnp.float32)
    for _ in range(ITERS):
        scale = jnp.exp(log_scale)
        crossed, energy, traced, fisher = sweep(scale, False)
        effect = wide(crossed / energy)
        spread = jnp.zeros((8, lanes), jnp.float32)
        for i, j in blocks:
            at = (slice(i, i + 8), slice(j, j + lanes))
            residual = r_ref[at] - effect * d_ref[at]
            spread = spread + w_ref[at] * residual * residual
        gradient = 0.5 * (total(spread) - total(traced))
        log_scale = log_scale + jnp.tanh(gradient / (scale * (0.5 * total(fisher))))
    crossed, energy, _, _ = sweep(jnp.exp(log_scale), True)
    score = crossed / jnp.sqrt(energy)
    lane = lax.broadcasted_iota(jnp.int32, (8, 128), 1)
    row = lax.broadcasted_iota(jnp.int32, (8, 128), 0)
    here = (row < 4) & (lane == 4 * slot_ref[0] + row)
    both = [jnp.sum(jnp.where(here, v, 0.0), axis=0, keepdims=True) for v in (score, log_scale)]
    out_ref[...] = jnp.broadcast_to(
        jnp.concatenate(both, axis=1)[None], (out_ref.shape[0], 1, 256)
    )


def fit(slot, sums, values):
    rows, width = values.shape
    vmem = pl.BlockSpec(memory_space=pltpu.VMEM)
    return pl.pallas_call(
        fit_kernel,
        out_shape=jax.ShapeDtypeStruct((32, 1, 256), jnp.float32),
        in_specs=[pl.BlockSpec(memory_space=pltpu.SMEM), vmem, vmem],
        out_specs=vmem,
        scratch_shapes=[pltpu.VMEM((rows, width), jnp.float32)] * 3,
        compiler_params=pltpu.CompilerParams(vmem_limit_bytes=16 * 1024 * 1024),
    )(slot, sums, values)


def gather_plane(own, other):
    x, y = "samp_1", "samp_0"
    left = shifted(own, x, 1)
    right = shifted(own, x, -1)
    over = shifted(own, y, 1)
    floor = lax.axis_size(x)

    def across(value, by):
        pairs = [
            (floor * v + u, floor * (1 - v) + (u + by) % floor) for v in (0, 1) for u in range(floor)
        ]
        return lax.ppermute(value, (y, x), pairs)

    over_left = shifted(left, y, 1)
    over_far = across(right, -1)
    over_right = shifted(over, x, -1)
    far = shifted(left, x, 1)
    over_far = over_far + 0 * other[: own.shape[0]]
    return jnp.stack([over_left, own, right, far, left, over, over_right, over_far])


def smooth_block(widened, places, present, reaches):
    block_len = reaches.shape[0]
    centre = places[HALO : HALO + block_len]
    total_sum = jnp.zeros((block_len,), jnp.float32)
    norm_sum = jnp.zeros((block_len,), jnp.float32)
    for offset in range(2 * HALO + 1):
        near_scores = widened[offset : offset + block_len]
        near_places = places[offset : offset + block_len]
        within = (abs(offset - HALO) <= reaches).astype(jnp.float32)
        kernel = (
            present[offset : offset + block_len]
            * within
            * jnp.exp(-jnp.abs(near_places - centre) / band_width)
        )
        total_sum = total_sum + kernel * near_scores
        norm_sum = norm_sum + kernel
    return total_sum / norm_sum


def copies(value, axes):
    peers = lax.axis_size(axes)
    return lax.all_to_all(
        jnp.broadcast_to(value[None], (peers, *value.shape)), axes, 0, 0, tiled=True
    )


def shards(responses, weights, phenotype, eigvecs, eigvals, positions, reaches):
    z, x, y = lax.axis_index("cpg_0"), lax.axis_index("samp_1"), lax.axis_index("samp_0")
    layers = lax.axis_size("cpg_0")
    with jax.named_scope("swap_eigvecs"):
        other = shifted(eigvecs, "samp_2", 1)
        vecs = (eigvecs, other)
    with jax.named_scope("weigh"):
        own = weigh(responses, weights, phenotype, eigvals)
    with jax.named_scope("gather_rows"):
        blocks = gather_plane(own, other)
    rows = own.shape[0] - EXTRA

    def place(across, along):
        return (4 * (across ^ y) + (along - x) % 4 + 1) % 8

    with jax.named_scope("gather_values"):
        here = jnp.arange(8, dtype=jnp.int32)
        kept = place(here // 4, here % 4)[:, None] == here[None, :]
        parts = blocks[:, rows : rows + 3].astype(jnp.float32)
        parts = parts[:, 0] + parts[:, 1] + parts[:, 2]
        values = jnp.sum(jnp.where(kept[:, :, None], parts[None], 0.0), axis=1)
        values = jnp.concatenate([values, shifted(values, "samp_2", 1)], axis=1)
        everywhere = jnp.repeat(values, 4, axis=0)

    def term(q, ahead, lo, hi):
        dest = lax.rem(z + ahead + layers, layers)
        at = place(dest // 4, lax.rem(dest, 4))
        block = lax.dynamic_index_in_dim(blocks, at, 0, keepdims=False)[lo:hi]
        return jnp.dot(block, vecs[q], preferred_element_type=jnp.float32)

    far = layers // 2
    cut = rows // 2
    sent = {}

    def first(q):
        sent[q, 1] = shifted(term(q, far, 0, cut).astype(jnp.bfloat16), "cpg_0", 1)
        sent[q, -1] = shifted(term(q, far, cut, rows).astype(jnp.bfloat16), "cpg_0", -1)

    def onward(q, ahead):
        for way in (1, -1):
            got = sent[q, way].astype(jnp.float32)
            if got.shape[0] < rows:
                rest = jnp.zeros_like(got)
                got = jnp.concatenate([got, rest] if way == 1 else [rest, got], axis=0)
            total = (term(q, way * ahead, 0, rows) + got).astype(jnp.bfloat16)
            sent[q, way] = shifted(total, "cpg_0", way)

    def summed(q):
        total = term(q, 0, 0, rows)
        for way in (1, -1):
            total = total + sent[q, way].astype(jnp.float32)
        return total.astype(jnp.bfloat16)

    with jax.named_scope("sum_layers"):
        first(0)
        first(1)
        for ahead in range(far - 1, 0, -1):
            onward(0, ahead)
            onward(1, ahead)
        whole = jnp.concatenate([summed(0), summed(1)], axis=1)
    with jax.named_scope("to_components"):
        sums = lax.all_to_all(whole, PLANE, 0, 0, tiled=True)
    with jax.named_scope("fit"):
        slot = lax.axis_index("samp_2") * 16 + lax.axis_index(PLANE)
        fitted = fit(slot.astype(jnp.int32)[None], sums, everywhere)
    with jax.named_scope("gather_scores"):
        layer = jnp.sum(lax.all_to_all(fitted, LAYER, 0, 0, tiled=True), axis=(0, 1))
        beside = [(2 * i, 2 * i + 2) for i in range(layers - 1)]
        beside += [(2 * i + 3, 2 * i + 1) for i in range(layers - 1)]
        other = lax.ppermute(layer, CPG, beside)
        scores, scales = layer[:rows], layer[rows:]
        before, after = other[rows - HALO : rows], other[:HALO]
    with jax.named_scope("smooth"):
        block_len = reaches.shape[0]
        high = lax.axis_index("cpg_1")
        widened = lax.dynamic_slice_in_dim(
            jnp.concatenate([before, scores, after]), high * block_len, block_len + 2 * HALO, 0
        )
        log_scale = lax.dynamic_slice_in_dim(scales, high * block_len, block_len, 0)
        base = lax.axis_index(CPG) * block_len
        total_cpgs = block_len * lax.axis_size(CPG)
        places = lax.dynamic_slice_in_dim(
            jnp.pad(positions.astype(jnp.float32), HALO), base, block_len + 2 * HALO, 0
        )
        global_index = base - HALO + jnp.arange(block_len + 2 * HALO, dtype=jnp.int32)
        present = ((global_index >= 0) & (global_index < total_cpgs)).astype(jnp.float32)
        smoothed = smooth_block(widened, places, present, reaches)
    return (smoothed, log_scale)


def solution(mesh):
    split = Mesh(
        mesh.devices.reshape(2, 4, 2, 8, 2), ("samp_0", "samp_1", "samp_2", "cpg_0", "cpg_1")
    )
    return jax.shard_map(
        shards,
        mesh=split,
        in_specs=(P(SAMP, CPG), P(SAMP, CPG), P(CPG), P(CPG, SAMP), P(SAMP), P(), P(CPG)),
        out_specs=(P(CPG), P(CPG)),
        check_vma=False,
    )
```

```python
import functools

import jax
import jax.numpy as jnp
from jax import lax
from jax.experimental import pallas as pl
from jax.experimental.pallas import tpu as pltpu
from jax.sharding import Mesh
from jax.sharding import PartitionSpec as P

ITERS = 4
HALO = 8
SAMP = ("samp_0", "samp_1", "samp_2")
CPG = ("cpg_0", "cpg_1")
PLANE = ("cpg_1", "samp_0", "samp_1")
FLOOR = ("samp_0", "samp_1")
LAYER = ("cpg_1", "samp_0", "samp_1", "samp_2")

EPSILON = 1e-06
band_width = 1000.0


def shifted(value, axis, by):
    peers = lax.axis_size(axis)
    return lax.ppermute(value, axis, [(i, (i + by) % peers) for i in range(peers)])


EXTRA = 16


def weigh_kernel(resp_ref, weight_ref, trait_ref, values_ref, out_ref):
    trait = trait_ref[...]
    width = trait.shape[1]
    upper = lax.broadcasted_iota(jnp.int32, (8, width), 0) < 4
    for at in range(0, resp_ref.shape[0], 16):
        root = jnp.sqrt(weight_ref[at : at + 16, :].astype(jnp.float32))
        weighted = root * resp_ref[at : at + 16, :].astype(jnp.float32)
        design = root * trait
        tiles = []
        for half in (0, 8):
            a, b = weighted[half : half + 8], design[half : half + 8]
            tiles.append(jnp.where(upper, a, pltpu.roll(b, 4, 0)))
            tiles.append(jnp.where(upper, pltpu.roll(a, 4, 0), b))
        out_ref[2 * at : 2 * at + 32, :] = jnp.concatenate(tiles, axis=0).astype(jnp.bfloat16)
    rest = values_ref[...]
    row = lax.broadcasted_iota(jnp.int32, (EXTRA, width), 0)
    parts = jnp.zeros((EXTRA, width), jnp.float32)
    for k in range(3):
        part = rest.astype(jnp.bfloat16).astype(jnp.float32)
        parts = jnp.where(row == k, part, parts)
        rest = rest - part
    out_ref[out_ref.shape[0] - EXTRA :, :] = parts.astype(jnp.bfloat16)


def weigh(responses, weights, phenotype, eigvals):
    rows, width = responses.shape
    return pl.pallas_call(
        weigh_kernel,
        out_shape=jax.ShapeDtypeStruct((2 * rows + EXTRA, width), jnp.bfloat16),
    )(responses, weights, phenotype[None, :], eigvals[None, :])


def fit_kernel(slot_ref, sums_ref, values_ref, out_ref, r_ref, d_ref, w_ref):
    half, width = values_ref.shape
    lanes = 512
    upper = lax.broadcasted_iota(jnp.int32, (8, width), 0) < 4
    for i in range(0, half, 8):
        pair = sums_ref[2 * i : 2 * i + 16, :].astype(jnp.float32) + sums_ref[
            2 * (half + i) : 2 * (half + i) + 16, :
        ].astype(jnp.float32)
        a, b = pair[:8], pair[8:]
        r_ref[i : i + 8, :] = jnp.where(upper, a, pltpu.roll(b, 4, 0))
        d_ref[i : i + 8, :] = jnp.where(upper, pltpu.roll(a, 4, 0), b)
    blocks = [(i, j) for i in range(0, half, 8) for j in range(0, width, lanes)]

    def total(acc):
        acc = functools.reduce(jnp.add, [acc[:, k : k + 128] for k in range(0, lanes, 128)])
        acc = acc + pltpu.roll(acc, 4, 0)
        return jnp.broadcast_to(jnp.sum(acc, axis=1, keepdims=True), (8, 128))

    def wide(value):
        return jnp.concatenate([value] * (lanes // 128), axis=1)

    def sweep(scale, last):
        zero = jnp.zeros((8, lanes), jnp.float32)
        crossed, energy, traced, fisher = zero, zero, zero, zero
        scale = wide(scale)
        for i, j in blocks:
            at = (slice(i, i + 8), slice(j, j + lanes))
            lam, resp, design = values_ref[at], r_ref[at], d_ref[at]
            v = scale * lam + 1.0
            inv = pl.reciprocal(v, approx=True)
            inv = inv * (2.0 - v * inv)
            over = design * inv
            crossed = crossed + over * resp
            energy = energy + over * design
            if not last:
                lev = lam * inv
                traced = traced + lev
                fisher = fisher + lev * lev
                w_ref[at] = lev * inv
        return total(crossed), total(energy) + EPSILON, traced, fisher

    log_scale = jnp.zeros((8, 128), jnp.float32)
    for _ in range(ITERS):
        scale = jnp.exp(log_scale)
        crossed, energy, traced, fisher = sweep(scale, False)
        effect = wide(crossed / energy)
        spread = jnp.zeros((8, lanes), jnp.float32)
        for i, j in blocks:
            at = (slice(i, i + 8), slice(j, j + lanes))
            residual = r_ref[at] - effect * d_ref[at]
            spread = spread + w_ref[at] * residual * residual
        gradient = 0.5 * (total(spread) - total(traced))
        log_scale = log_scale + jnp.tanh(gradient / (scale * (0.5 * total(fisher))))
    crossed, energy, _, _ = sweep(jnp.exp(log_scale), True)
    score = crossed / jnp.sqrt(energy)
    lane = lax.broadcasted_iota(jnp.int32, (8, 128), 1)
    row = lax.broadcasted_iota(jnp.int32, (8, 128), 0)
    here = (row < 4) & (lane == 4 * slot_ref[0] + row)
    both = [jnp.sum(jnp.where(here, v, 0.0), axis=0, keepdims=True) for v in (score, log_scale)]
    out_ref[...] = jnp.broadcast_to(
        jnp.concatenate(both, axis=1)[None], (out_ref.shape[0], 1, 256)
    )


def fit(slot, sums, values):
    rows, width = values.shape
    vmem = pl.BlockSpec(memory_space=pltpu.VMEM)
    return pl.pallas_call(
        fit_kernel,
        out_shape=jax.ShapeDtypeStruct((32, 1, 256), jnp.float32),
        in_specs=[pl.BlockSpec(memory_space=pltpu.SMEM), vmem, vmem],
        out_specs=vmem,
        scratch_shapes=[pltpu.VMEM((rows, width), jnp.float32)] * 3,
        compiler_params=pltpu.CompilerParams(vmem_limit_bytes=16 * 1024 * 1024),
    )(slot, sums, values)


def gather_plane(own, other):
    x, y = "samp_1", "samp_0"
    left = shifted(own, x, 1)
    right = shifted(own, x, -1)
    over = shifted(own, y, 1)
    floor = lax.axis_size(x)

    def across(value, by):
        pairs = [
            (floor * v + u, floor * (1 - v) + (u + by) % floor) for v in (0, 1) for u in range(floor)
        ]
        return lax.ppermute(value, (y, x), pairs)

    over_left = shifted(left, y, 1)
    over_far = across(right, -1)
    over_right = shifted(over, x, -1)
    far = shifted(left, x, 1)
    over_right = over_right + 0 * other[: own.shape[0]]
    return jnp.stack([over_far, over_left, own, right, far, left, over, over_right])


def smooth_block(widened, places, present, reaches):
    block_len = reaches.shape[0]
    centre = places[HALO : HALO + block_len]
    total_sum = jnp.zeros((block_len,), jnp.float32)
    norm_sum = jnp.zeros((block_len,), jnp.float32)
    for offset in range(2 * HALO + 1):
        near_scores = widened[offset : offset + block_len]
        near_places = places[offset : offset + block_len]
        within = (abs(offset - HALO) <= reaches).astype(jnp.float32)
        kernel = (
            present[offset : offset + block_len]
            * within
            * jnp.exp(-jnp.abs(near_places - centre) / band_width)
        )
        total_sum = total_sum + kernel * near_scores
        norm_sum = norm_sum + kernel
    return total_sum / norm_sum


def copies(value, axes):
    peers = lax.axis_size(axes)
    return lax.all_to_all(
        jnp.broadcast_to(value[None], (peers, *value.shape)), axes, 0, 0, tiled=True
    )


def shards(responses, weights, phenotype, eigvecs, eigvals, positions, reaches):
    z, x, y = lax.axis_index("cpg_0"), lax.axis_index("samp_1"), lax.axis_index("samp_0")
    layers = lax.axis_size("cpg_0")
    with jax.named_scope("swap_eigvecs"):
        other = shifted(eigvecs, "samp_2", 1)
        vecs = (eigvecs, other)
    with jax.named_scope("weigh"):
        own = weigh(responses, weights, phenotype, eigvals)
    with jax.named_scope("gather_rows"):
        blocks = gather_plane(own, other)
    rows = own.shape[0] - EXTRA

    def place(across, along):
        return (4 * (across ^ y) + (along - x) % 4 + 2) % 8

    with jax.named_scope("gather_values"):
        here = jnp.arange(8, dtype=jnp.int32)
        kept = place(here // 4, here % 4)[:, None] == here[None, :]
        parts = blocks[:, rows : rows + 3].astype(jnp.float32)
        parts = parts[:, 0] + parts[:, 1] + parts[:, 2]
        values = jnp.sum(jnp.where(kept[:, :, None], parts[None], 0.0), axis=1)
        values = jnp.concatenate([values, shifted(values, "samp_2", 1)], axis=1)
        everywhere = jnp.repeat(values, 4, axis=0)

    def term(q, ahead):
        dest = lax.rem(z + ahead + layers, layers)
        at = place(dest // 4, lax.rem(dest, 4))
        block = lax.dynamic_index_in_dim(blocks, at, 0, keepdims=False)[:rows]
        return jnp.dot(block, vecs[q], preferred_element_type=jnp.float32)

    far = layers // 2
    sent = {}

    def onward(q, way, ahead):
        total = term(q, way * ahead)
        if (q, way) in sent:
            total = total + sent[q, way].astype(jnp.float32)
        sent[q, way] = shifted(total.astype(jnp.bfloat16), "cpg_0", way)

    def summed(q):
        total = term(q, 0)
        for way in (1, -1):
            total = total + sent[q, way].astype(jnp.float32)
        return total.astype(jnp.bfloat16)

    with jax.named_scope("sum_layers"):
        for ahead in range(far, 0, -1):
            onward(0, 1, ahead)
            onward(1, -1, ahead)
            if ahead > 1:
                onward(0, -1, ahead - 1)
                onward(1, 1, ahead - 1)
        whole = jnp.concatenate([summed(0), summed(1)], axis=1)
    with jax.named_scope("to_components"):
        sums = lax.all_to_all(whole, PLANE, 0, 0, tiled=True)
    with jax.named_scope("fit"):
        slot = lax.axis_index("samp_2") * 16 + lax.axis_index(PLANE)
        fitted = fit(slot.astype(jnp.int32)[None], sums, everywhere)
    with jax.named_scope("gather_scores"):
        layer = jnp.sum(lax.all_to_all(fitted, LAYER, 0, 0, tiled=True), axis=(0, 1))
        beside = [(2 * i, 2 * i + 2) for i in range(layers - 1)]
        beside += [(2 * i + 3, 2 * i + 1) for i in range(layers - 1)]
        other = lax.ppermute(layer, CPG, beside)
        scores, scales = layer[:rows], layer[rows:]
        before, after = other[rows - HALO : rows], other[:HALO]
    with jax.named_scope("smooth"):
        block_len = reaches.shape[0]
        high = lax.axis_index("cpg_1")
        widened = lax.dynamic_slice_in_dim(
            jnp.concatenate([before, scores, after]), high * block_len, block_len + 2 * HALO, 0
        )
        log_scale = lax.dynamic_slice_in_dim(scales, high * block_len, block_len, 0)
        base = lax.axis_index(CPG) * block_len
        total_cpgs = block_len * lax.axis_size(CPG)
        places = lax.dynamic_slice_in_dim(
            jnp.pad(positions.astype(jnp.float32), HALO), base, block_len + 2 * HALO, 0
        )
        global_index = base - HALO + jnp.arange(block_len + 2 * HALO, dtype=jnp.int32)
        present = ((global_index >= 0) & (global_index < total_cpgs)).astype(jnp.float32)
        smoothed = smooth_block(widened, places, present, reaches)
    return (smoothed, log_scale)


def solution(mesh):
    split = Mesh(
        mesh.devices.reshape(2, 4, 2, 8, 2), ("samp_0", "samp_1", "samp_2", "cpg_0", "cpg_1")
    )
    return jax.shard_map(
        shards,
        mesh=split,
        in_specs=(P(SAMP, CPG), P(SAMP, CPG), P(CPG), P(CPG, SAMP), P(SAMP), P(), P(CPG)),
        out_specs=(P(CPG), P(CPG)),
        check_vma=False,
    )
```

```python
import functools

import jax
import jax.numpy as jnp
from jax import lax
from jax.experimental import pallas as pl
from jax.experimental.pallas import tpu as pltpu
from jax.sharding import Mesh
from jax.sharding import PartitionSpec as P

ITERS = 4
HALO = 8
SAMP = ("samp_0", "samp_1", "samp_2")
CPG = ("cpg_0", "cpg_1")
PLANE = ("cpg_1", "samp_0", "samp_1")
FLOOR = ("samp_0", "samp_1")
LAYER = ("cpg_1", "samp_0", "samp_1", "samp_2")

EPSILON = 1e-06
band_width = 1000.0


def shifted(value, axis, by):
    peers = lax.axis_size(axis)
    return lax.ppermute(value, axis, [(i, (i + by) % peers) for i in range(peers)])


EXTRA = 16


def weigh_kernel(resp_ref, weight_ref, trait_ref, values_ref, out_ref):
    trait = trait_ref[...]
    width = trait.shape[1]
    upper = lax.broadcasted_iota(jnp.int32, (8, width), 0) < 4
    for at in range(0, resp_ref.shape[0], 16):
        root = jnp.sqrt(weight_ref[at : at + 16, :].astype(jnp.float32))
        weighted = root * resp_ref[at : at + 16, :].astype(jnp.float32)
        design = root * trait
        tiles = []
        for half in (0, 8):
            a, b = weighted[half : half + 8], design[half : half + 8]
            tiles.append(jnp.where(upper, a, pltpu.roll(b, 4, 0)))
            tiles.append(jnp.where(upper, pltpu.roll(a, 4, 0), b))
        out_ref[2 * at : 2 * at + 32, :] = jnp.concatenate(tiles, axis=0).astype(jnp.bfloat16)
    rest = values_ref[...]
    row = lax.broadcasted_iota(jnp.int32, (EXTRA, width), 0)
    parts = jnp.zeros((EXTRA, width), jnp.float32)
    for k in range(3):
        part = rest.astype(jnp.bfloat16).astype(jnp.float32)
        parts = jnp.where(row == k, part, parts)
        rest = rest - part
    out_ref[out_ref.shape[0] - EXTRA :, :] = parts.astype(jnp.bfloat16)


def weigh(responses, weights, phenotype, eigvals):
    rows, width = responses.shape
    return pl.pallas_call(
        weigh_kernel,
        out_shape=jax.ShapeDtypeStruct((2 * rows + EXTRA, width), jnp.bfloat16),
    )(responses, weights, phenotype[None, :], eigvals[None, :])


def fit_kernel(slot_ref, sums_ref, values_ref, out_ref, r_ref, d_ref, w_ref):
    half, width = values_ref.shape
    lanes = 512
    upper = lax.broadcasted_iota(jnp.int32, (8, width), 0) < 4
    for i in range(0, half, 8):
        pair = sums_ref[2 * i : 2 * i + 16, :].astype(jnp.float32) + sums_ref[
            2 * (half + i) : 2 * (half + i) + 16, :
        ].astype(jnp.float32)
        a, b = pair[:8], pair[8:]
        r_ref[i : i + 8, :] = jnp.where(upper, a, pltpu.roll(b, 4, 0))
        d_ref[i : i + 8, :] = jnp.where(upper, pltpu.roll(a, 4, 0), b)
    blocks = [(i, j) for i in range(0, half, 8) for j in range(0, width, lanes)]

    def total(acc):
        acc = functools.reduce(jnp.add, [acc[:, k : k + 128] for k in range(0, lanes, 128)])
        acc = acc + pltpu.roll(acc, 4, 0)
        return jnp.broadcast_to(jnp.sum(acc, axis=1, keepdims=True), (8, 128))

    def wide(value):
        return jnp.concatenate([value] * (lanes // 128), axis=1)

    def sweep(scale, last):
        zero = jnp.zeros((8, lanes), jnp.float32)
        crossed, energy, traced, fisher = zero, zero, zero, zero
        scale = wide(scale)
        for i, j in blocks:
            at = (slice(i, i + 8), slice(j, j + lanes))
            lam, resp, design = values_ref[at], r_ref[at], d_ref[at]
            v = scale * lam + 1.0
            inv = pl.reciprocal(v, approx=True)
            inv = inv * (2.0 - v * inv)
            over = design * inv
            crossed = crossed + over * resp
            energy = energy + over * design
            if not last:
                lev = lam * inv
                traced = traced + lev
                fisher = fisher + lev * lev
                w_ref[at] = lev * inv
        return total(crossed), total(energy) + EPSILON, traced, fisher

    log_scale = jnp.zeros((8, 128), jnp.float32)
    for _ in range(ITERS):
        scale = jnp.exp(log_scale)
        crossed, energy, traced, fisher = sweep(scale, False)
        effect = wide(crossed / energy)
        spread = jnp.zeros((8, lanes), jnp.float32)
        for i, j in blocks:
            at = (slice(i, i + 8), slice(j, j + lanes))
            residual = r_ref[at] - effect * d_ref[at]
            spread = spread + w_ref[at] * residual * residual
        gradient = 0.5 * (total(spread) - total(traced))
        log_scale = log_scale + jnp.tanh(gradient / (scale * (0.5 * total(fisher))))
    crossed, energy, _, _ = sweep(jnp.exp(log_scale), True)
    score = crossed / jnp.sqrt(energy)
    lane = lax.broadcasted_iota(jnp.int32, (8, 128), 1)
    row = lax.broadcasted_iota(jnp.int32, (8, 128), 0)
    here = (row < 4) & (lane == 4 * slot_ref[0] + row)
    both = [jnp.sum(jnp.where(here, v, 0.0), axis=0, keepdims=True) for v in (score, log_scale)]
    out_ref[...] = jnp.broadcast_to(
        jnp.concatenate(both, axis=1)[None], (out_ref.shape[0], 1, 256)
    )


def fit(slot, sums, values):
    rows, width = values.shape
    vmem = pl.BlockSpec(memory_space=pltpu.VMEM)
    return pl.pallas_call(
        fit_kernel,
        out_shape=jax.ShapeDtypeStruct((32, 1, 256), jnp.float32),
        in_specs=[pl.BlockSpec(memory_space=pltpu.SMEM), vmem, vmem],
        out_specs=vmem,
        scratch_shapes=[pltpu.VMEM((rows, width), jnp.float32)] * 3,
        compiler_params=pltpu.CompilerParams(vmem_limit_bytes=16 * 1024 * 1024),
    )(slot, sums, values)


def gather_plane(own, other):
    x, y = "samp_1", "samp_0"
    left = shifted(own, x, 1)
    right = shifted(own, x, -1)
    over = shifted(own, y, 1)
    floor = lax.axis_size(x)

    def across(value, by):
        pairs = [
            (floor * v + u, floor * (1 - v) + (u + by) % floor) for v in (0, 1) for u in range(floor)
        ]
        return lax.ppermute(value, (y, x), pairs)

    over_left = shifted(left, y, 1)
    over_far = across(right, -1)
    over_right = shifted(over, x, -1)
    far = shifted(left, x, 1)
    over_left = over_left + 0 * other[: own.shape[0]]
    return jnp.stack([over_far, over_right, over, left, far, right, own, over_left])


def smooth_block(widened, places, present, reaches):
    block_len = reaches.shape[0]
    centre = places[HALO : HALO + block_len]
    total_sum = jnp.zeros((block_len,), jnp.float32)
    norm_sum = jnp.zeros((block_len,), jnp.float32)
    for offset in range(2 * HALO + 1):
        near_scores = widened[offset : offset + block_len]
        near_places = places[offset : offset + block_len]
        within = (abs(offset - HALO) <= reaches).astype(jnp.float32)
        kernel = (
            present[offset : offset + block_len]
            * within
            * jnp.exp(-jnp.abs(near_places - centre) / band_width)
        )
        total_sum = total_sum + kernel * near_scores
        norm_sum = norm_sum + kernel
    return total_sum / norm_sum


def copies(value, axes):
    peers = lax.axis_size(axes)
    return lax.all_to_all(
        jnp.broadcast_to(value[None], (peers, *value.shape)), axes, 0, 0, tiled=True
    )


def shards(responses, weights, phenotype, eigvecs, eigvals, positions, reaches):
    z, x, y = lax.axis_index("cpg_0"), lax.axis_index("samp_1"), lax.axis_index("samp_0")
    layers = lax.axis_size("cpg_0")
    with jax.named_scope("swap_eigvecs"):
        other = shifted(eigvecs, "samp_2", 1)
        vecs = (eigvecs, other)
    with jax.named_scope("weigh"):
        own = weigh(responses, weights, phenotype, eigvals)
    with jax.named_scope("gather_rows"):
        blocks = gather_plane(own, other)
    rows = own.shape[0] - EXTRA

    def place(across, along):
        return (6 - 4 * (across ^ y) - (along - x) % 4) % 8

    with jax.named_scope("gather_values"):
        here = jnp.arange(8, dtype=jnp.int32)
        kept = place(here // 4, here % 4)[:, None] == here[None, :]
        parts = blocks[:, rows : rows + 3].astype(jnp.float32)
        parts = parts[:, 0] + parts[:, 1] + parts[:, 2]
        values = jnp.sum(jnp.where(kept[:, :, None], parts[None], 0.0), axis=1)
        values = jnp.concatenate([values, shifted(values, "samp_2", 1)], axis=1)
        everywhere = jnp.repeat(values, 4, axis=0)

    def term(q, ahead):
        dest = lax.rem(z + ahead + layers, layers)
        at = place(dest // 4, lax.rem(dest, 4))
        block = lax.dynamic_index_in_dim(blocks, at, 0, keepdims=False)[:rows]
        return jnp.dot(block, vecs[q], preferred_element_type=jnp.float32)

    far = layers // 2
    sent = {}

    def onward(q, way, ahead, behind=None):
        total = term(q, way * ahead)
        if (q, way) in sent:
            total = total + sent[q, way].astype(jnp.float32)
        if behind is not None:
            total = total + 0.0 * behind.astype(jnp.float32)
        total = total.astype(jnp.bfloat16)
        sent[q, way] = shifted(total, "cpg_0", way)
        return total

    def summed(q):
        total = term(q, 0)
        for way in (1, -1):
            total = total + sent[q, way].astype(jnp.float32)
        return total.astype(jnp.bfloat16)

    with jax.named_scope("sum_layers"):
        for ahead in range(far, 0, -1):
            onward(0, 1, ahead)
            behind = onward(1, -1, ahead)
            if ahead > 1:
                onward(0, -1, ahead - 1, behind)
                onward(1, 1, ahead - 1, behind)
        whole = jnp.concatenate([summed(0), summed(1)], axis=1)
    with jax.named_scope("to_components"):
        sums = lax.all_to_all(whole, PLANE, 0, 0, tiled=True)
    with jax.named_scope("fit"):
        slot = lax.axis_index("samp_2") * 16 + lax.axis_index(PLANE)
        fitted = fit(slot.astype(jnp.int32)[None], sums, everywhere)
    with jax.named_scope("gather_scores"):
        layer = jnp.sum(lax.all_to_all(fitted, LAYER, 0, 0, tiled=True), axis=(0, 1))
        beside = [(2 * i, 2 * i + 2) for i in range(layers - 1)]
        beside += [(2 * i + 3, 2 * i + 1) for i in range(layers - 1)]
        other = lax.ppermute(layer, CPG, beside)
        scores, scales = layer[:rows], layer[rows:]
        before, after = other[rows - HALO : rows], other[:HALO]
    with jax.named_scope("smooth"):
        block_len = reaches.shape[0]
        high = lax.axis_index("cpg_1")
        widened = lax.dynamic_slice_in_dim(
            jnp.concatenate([before, scores, after]), high * block_len, block_len + 2 * HALO, 0
        )
        log_scale = lax.dynamic_slice_in_dim(scales, high * block_len, block_len, 0)
        base = lax.axis_index(CPG) * block_len
        total_cpgs = block_len * lax.axis_size(CPG)
        places = lax.dynamic_slice_in_dim(
            jnp.pad(positions.astype(jnp.float32), HALO), base, block_len + 2 * HALO, 0
        )
        global_index = base - HALO + jnp.arange(block_len + 2 * HALO, dtype=jnp.int32)
        present = ((global_index >= 0) & (global_index < total_cpgs)).astype(jnp.float32)
        smoothed = smooth_block(widened, places, present, reaches)
    return (smoothed, log_scale)


def solution(mesh):
    split = Mesh(
        mesh.devices.reshape(2, 4, 2, 8, 2), ("samp_0", "samp_1", "samp_2", "cpg_0", "cpg_1")
    )
    return jax.shard_map(
        shards,
        mesh=split,
        in_specs=(P(SAMP, CPG), P(SAMP, CPG), P(CPG), P(CPG, SAMP), P(SAMP), P(), P(CPG)),
        out_specs=(P(CPG), P(CPG)),
        check_vma=False,
    )
```

```python
import functools

import jax
import jax.numpy as jnp
from jax import lax
from jax.experimental import pallas as pl
from jax.experimental.pallas import tpu as pltpu
from jax.sharding import Mesh
from jax.sharding import PartitionSpec as P

ITERS = 4
HALO = 8
SAMP = ("samp_0", "samp_1", "samp_2")
CPG = ("cpg_0", "cpg_1")
PLANE = ("cpg_1", "samp_0", "samp_1")
FLOOR = ("samp_0", "samp_1")
LAYER = ("cpg_1", "samp_0", "samp_1", "samp_2")

EPSILON = 1e-06
band_width = 1000.0


def shifted(value, axis, by):
    peers = lax.axis_size(axis)
    return lax.ppermute(value, axis, [(i, (i + by) % peers) for i in range(peers)])


EXTRA = 16


def weigh_kernel(resp_ref, weight_ref, trait_ref, values_ref, out_ref):
    trait = trait_ref[...]
    width = trait.shape[1]
    upper = lax.broadcasted_iota(jnp.int32, (8, width), 0) < 4
    for at in range(0, resp_ref.shape[0], 16):
        root = jnp.sqrt(weight_ref[at : at + 16, :].astype(jnp.float32))
        weighted = root * resp_ref[at : at + 16, :].astype(jnp.float32)
        design = root * trait
        tiles = []
        for half in (0, 8):
            a, b = weighted[half : half + 8], design[half : half + 8]
            tiles.append(jnp.where(upper, a, pltpu.roll(b, 4, 0)))
            tiles.append(jnp.where(upper, pltpu.roll(a, 4, 0), b))
        out_ref[2 * at : 2 * at + 32, :] = jnp.concatenate(tiles, axis=0).astype(jnp.bfloat16)
    rest = values_ref[...]
    row = lax.broadcasted_iota(jnp.int32, (EXTRA, width), 0)
    parts = jnp.zeros((EXTRA, width), jnp.float32)
    for k in range(3):
        part = rest.astype(jnp.bfloat16).astype(jnp.float32)
        parts = jnp.where(row == k, part, parts)
        rest = rest - part
    out_ref[out_ref.shape[0] - EXTRA :, :] = parts.astype(jnp.bfloat16)


def weigh(responses, weights, phenotype, eigvals):
    rows, width = responses.shape
    return pl.pallas_call(
        weigh_kernel,
        out_shape=pltpu.VMEM((2 * rows + EXTRA, width), jnp.bfloat16),
    )(responses, weights, phenotype[None, :], eigvals[None, :])


def fit_kernel(slot_ref, sums_ref, values_ref, out_ref, r_ref, d_ref, w_ref):
    half, width = values_ref.shape
    lanes = 512
    upper = lax.broadcasted_iota(jnp.int32, (8, width), 0) < 4
    for i in range(0, half, 8):
        pair = sums_ref[2 * i : 2 * i + 16, :].astype(jnp.float32) + sums_ref[
            2 * (half + i) : 2 * (half + i) + 16, :
        ].astype(jnp.float32)
        a, b = pair[:8], pair[8:]
        r_ref[i : i + 8, :] = jnp.where(upper, a, pltpu.roll(b, 4, 0))
        d_ref[i : i + 8, :] = jnp.where(upper, pltpu.roll(a, 4, 0), b)
    blocks = [(i, j) for i in range(0, half, 8) for j in range(0, width, lanes)]

    def total(acc):
        acc = functools.reduce(jnp.add, [acc[:, k : k + 128] for k in range(0, lanes, 128)])
        acc = acc + pltpu.roll(acc, 4, 0)
        return jnp.broadcast_to(jnp.sum(acc, axis=1, keepdims=True), (8, 128))

    def wide(value):
        return jnp.concatenate([value] * (lanes // 128), axis=1)

    def sweep(scale, last):
        zero = jnp.zeros((8, lanes), jnp.float32)
        crossed, energy, traced, fisher = zero, zero, zero, zero
        scale = wide(scale)
        for i, j in blocks:
            at = (slice(i, i + 8), slice(j, j + lanes))
            lam, resp, design = values_ref[at], r_ref[at], d_ref[at]
            v = scale * lam + 1.0
            inv = pl.reciprocal(v, approx=True)
            inv = inv * (2.0 - v * inv)
            over = design * inv
            crossed = crossed + over * resp
            energy = energy + over * design
            if not last:
                lev = lam * inv
                traced = traced + lev
                fisher = fisher + lev * lev
                w_ref[at] = lev * inv
        return total(crossed), total(energy) + EPSILON, traced, fisher

    log_scale = jnp.zeros((8, 128), jnp.float32)
    for _ in range(ITERS):
        scale = jnp.exp(log_scale)
        crossed, energy, traced, fisher = sweep(scale, False)
        effect = wide(crossed / energy)
        spread = jnp.zeros((8, lanes), jnp.float32)
        for i, j in blocks:
            at = (slice(i, i + 8), slice(j, j + lanes))
            residual = r_ref[at] - effect * d_ref[at]
            spread = spread + w_ref[at] * residual * residual
        gradient = 0.5 * (total(spread) - total(traced))
        log_scale = log_scale + jnp.tanh(gradient / (scale * (0.5 * total(fisher))))
    crossed, energy, _, _ = sweep(jnp.exp(log_scale), True)
    score = crossed / jnp.sqrt(energy)
    lane = lax.broadcasted_iota(jnp.int32, (8, 128), 1)
    row = lax.broadcasted_iota(jnp.int32, (8, 128), 0)
    here = (row < 4) & (lane == 4 * slot_ref[0] + row)
    both = [jnp.sum(jnp.where(here, v, 0.0), axis=0, keepdims=True) for v in (score, log_scale)]
    out_ref[...] = jnp.broadcast_to(
        jnp.concatenate(both, axis=1)[None], (out_ref.shape[0], 1, 256)
    )


def fit(slot, sums, values):
    rows, width = values.shape
    vmem = pl.BlockSpec(memory_space=pltpu.VMEM)
    return pl.pallas_call(
        fit_kernel,
        out_shape=jax.ShapeDtypeStruct((32, 1, 256), jnp.float32),
        in_specs=[pl.BlockSpec(memory_space=pltpu.SMEM), vmem, vmem],
        out_specs=vmem,
        scratch_shapes=[pltpu.VMEM((rows, width), jnp.float32)] * 3,
        compiler_params=pltpu.CompilerParams(vmem_limit_bytes=16 * 1024 * 1024),
    )(slot, sums, values)


def gather_plane(own, other):
    x, y = "samp_1", "samp_0"
    left = shifted(own, x, 1)
    right = shifted(own, x, -1)
    over = shifted(own, y, 1)
    floor = lax.axis_size(x)

    def across(value, by):
        pairs = [
            (floor * v + u, floor * (1 - v) + (u + by) % floor) for v in (0, 1) for u in range(floor)
        ]
        return lax.ppermute(value, (y, x), pairs)

    over_left = shifted(left, y, 1)
    over_far = across(right, -1)
    over_right = shifted(over, x, -1)
    far = shifted(left, x, 1)
    over_left = over_left + 0 * other[: own.shape[0]]
    return jnp.stack([over_far, over_right, over, left, far, right, own, over_left])


def smooth_block(widened, places, present, reaches):
    block_len = reaches.shape[0]
    centre = places[HALO : HALO + block_len]
    total_sum = jnp.zeros((block_len,), jnp.float32)
    norm_sum = jnp.zeros((block_len,), jnp.float32)
    for offset in range(2 * HALO + 1):
        near_scores = widened[offset : offset + block_len]
        near_places = places[offset : offset + block_len]
        within = (abs(offset - HALO) <= reaches).astype(jnp.float32)
        kernel = (
            present[offset : offset + block_len]
            * within
            * jnp.exp(-jnp.abs(near_places - centre) / band_width)
        )
        total_sum = total_sum + kernel * near_scores
        norm_sum = norm_sum + kernel
    return total_sum / norm_sum


def copies(value, axes):
    peers = lax.axis_size(axes)
    return lax.all_to_all(
        jnp.broadcast_to(value[None], (peers, *value.shape)), axes, 0, 0, tiled=True
    )


def shards(responses, weights, phenotype, eigvecs, eigvals, positions, reaches):
    z, x, y = lax.axis_index("cpg_0"), lax.axis_index("samp_1"), lax.axis_index("samp_0")
    layers = lax.axis_size("cpg_0")
    with jax.named_scope("swap_eigvecs"):
        other = shifted(eigvecs, "samp_2", 1)
        vecs = (eigvecs, other)
    with jax.named_scope("weigh"):
        own = weigh(responses, weights, phenotype, eigvals)
    with jax.named_scope("gather_rows"):
        blocks = gather_plane(own, other)
    rows = own.shape[0] - EXTRA

    def place(across, along):
        return (6 - 4 * (across ^ y) - (along - x) % 4) % 8

    with jax.named_scope("gather_values"):
        here = jnp.arange(8, dtype=jnp.int32)
        kept = place(here // 4, here % 4)[:, None] == here[None, :]
        parts = blocks[:, rows : rows + 3].astype(jnp.float32)
        parts = parts[:, 0] + parts[:, 1] + parts[:, 2]
        values = jnp.sum(jnp.where(kept[:, :, None], parts[None], 0.0), axis=1)
        values = jnp.concatenate([values, shifted(values, "samp_2", 1)], axis=1)
        everywhere = jnp.repeat(values, 4, axis=0)

    def term(q, ahead):
        dest = lax.rem(z + ahead + layers, layers)
        at = place(dest // 4, lax.rem(dest, 4))
        block = lax.dynamic_index_in_dim(blocks, at, 0, keepdims=False)[:rows]
        return jnp.dot(block, vecs[q], preferred_element_type=jnp.float32)

    far = layers // 2
    sent = {}

    def onward(q, way, ahead, behind=None):
        total = term(q, way * ahead)
        if (q, way) in sent:
            total = total + sent[q, way].astype(jnp.float32)
        if behind is not None:
            total = total + 0.0 * behind.astype(jnp.float32)
        total = total.astype(jnp.bfloat16)
        sent[q, way] = shifted(total, "cpg_0", way)
        return total

    def summed(q):
        total = term(q, 0)
        for way in (1, -1):
            total = total + sent[q, way].astype(jnp.float32)
        return total.astype(jnp.bfloat16)

    with jax.named_scope("sum_layers"):
        for ahead in range(far, 0, -1):
            onward(0, 1, ahead)
            behind = onward(1, -1, ahead)
            if ahead > 1:
                onward(0, -1, ahead - 1, behind)
                onward(1, 1, ahead - 1, behind)
        whole = jnp.concatenate([summed(0), summed(1)], axis=1)
    with jax.named_scope("to_components"):
        sums = lax.all_to_all(whole, PLANE, 0, 0, tiled=True)
    with jax.named_scope("fit"):
        slot = lax.axis_index("samp_2") * 16 + lax.axis_index(PLANE)
        fitted = fit(slot.astype(jnp.int32)[None], sums, everywhere)
    with jax.named_scope("gather_scores"):
        layer = jnp.sum(lax.all_to_all(fitted, LAYER, 0, 0, tiled=True), axis=(0, 1))
        beside = [(2 * i, 2 * i + 2) for i in range(layers - 1)]
        beside += [(2 * i + 3, 2 * i + 1) for i in range(layers - 1)]
        other = lax.ppermute(layer, CPG, beside)
        scores, scales = layer[:rows], layer[rows:]
        before, after = other[rows - HALO : rows], other[:HALO]
    with jax.named_scope("smooth"):
        block_len = reaches.shape[0]
        high = lax.axis_index("cpg_1")
        widened = lax.dynamic_slice_in_dim(
            jnp.concatenate([before, scores, after]), high * block_len, block_len + 2 * HALO, 0
        )
        log_scale = lax.dynamic_slice_in_dim(scales, high * block_len, block_len, 0)
        base = lax.axis_index(CPG) * block_len
        total_cpgs = block_len * lax.axis_size(CPG)
        places = lax.dynamic_slice_in_dim(
            jnp.pad(positions.astype(jnp.float32), HALO), base, block_len + 2 * HALO, 0
        )
        global_index = base - HALO + jnp.arange(block_len + 2 * HALO, dtype=jnp.int32)
        present = ((global_index >= 0) & (global_index < total_cpgs)).astype(jnp.float32)
        smoothed = smooth_block(widened, places, present, reaches)
    return (smoothed, log_scale)


def solution(mesh):
    split = Mesh(
        mesh.devices.reshape(2, 4, 2, 8, 2), ("samp_0", "samp_1", "samp_2", "cpg_0", "cpg_1")
    )
    return jax.shard_map(
        shards,
        mesh=split,
        in_specs=(P(SAMP, CPG), P(SAMP, CPG), P(CPG), P(CPG, SAMP), P(SAMP), P(), P(CPG)),
        out_specs=(P(CPG), P(CPG)),
        check_vma=False,
    )
```

```python
import functools

import jax
import jax.numpy as jnp
from jax import lax
from jax.experimental import pallas as pl
from jax.experimental.pallas import tpu as pltpu
from jax.sharding import Mesh
from jax.sharding import PartitionSpec as P

ITERS = 4
HALO = 8
SAMP = ("samp_0", "samp_1", "samp_2")
CPG = ("cpg_0", "cpg_1")
PLANE = ("cpg_1", "samp_0", "samp_1")
FLOOR = ("samp_0", "samp_1")
LAYER = ("cpg_1", "samp_0", "samp_1", "samp_2")

EPSILON = 1e-06
band_width = 1000.0


def shifted(value, axis, by):
    peers = lax.axis_size(axis)
    return lax.ppermute(value, axis, [(i, (i + by) % peers) for i in range(peers)])


EXTRA = 16


def weigh_kernel(resp_ref, weight_ref, trait_ref, values_ref, out_ref):
    trait = trait_ref[...]
    width = trait.shape[1]
    upper = lax.broadcasted_iota(jnp.int32, (8, width), 0) < 4
    for at in range(0, resp_ref.shape[0], 16):
        root = jnp.sqrt(weight_ref[at : at + 16, :].astype(jnp.float32))
        weighted = root * resp_ref[at : at + 16, :].astype(jnp.float32)
        design = root * trait
        tiles = []
        for half in (0, 8):
            a, b = weighted[half : half + 8], design[half : half + 8]
            tiles.append(jnp.where(upper, a, pltpu.roll(b, 4, 0)))
            tiles.append(jnp.where(upper, pltpu.roll(a, 4, 0), b))
        out_ref[2 * at : 2 * at + 32, :] = jnp.concatenate(tiles, axis=0).astype(jnp.bfloat16)
    rest = values_ref[...]
    row = lax.broadcasted_iota(jnp.int32, (EXTRA, width), 0)
    parts = jnp.zeros((EXTRA, width), jnp.float32)
    for k in range(3):
        part = rest.astype(jnp.bfloat16).astype(jnp.float32)
        parts = jnp.where(row == k, part, parts)
        rest = rest - part
    out_ref[out_ref.shape[0] - EXTRA :, :] = parts.astype(jnp.bfloat16)


def weigh(responses, weights, phenotype, eigvals):
    rows, width = responses.shape
    return pl.pallas_call(
        weigh_kernel,
        out_shape=pltpu.VMEM((2 * rows + EXTRA, width), jnp.bfloat16),
    )(responses, weights, phenotype[None, :], eigvals[None, :])


def fit_kernel(slot_ref, sums_ref, values_ref, out_ref, r_ref, d_ref, w_ref):
    half, width = values_ref.shape
    lanes = 512
    upper = lax.broadcasted_iota(jnp.int32, (8, width), 0) < 4
    for i in range(0, half, 8):
        pair = sums_ref[2 * i : 2 * i + 16, :].astype(jnp.float32) + sums_ref[
            2 * (half + i) : 2 * (half + i) + 16, :
        ].astype(jnp.float32)
        a, b = pair[:8], pair[8:]
        r_ref[i : i + 8, :] = jnp.where(upper, a, pltpu.roll(b, 4, 0))
        d_ref[i : i + 8, :] = jnp.where(upper, pltpu.roll(a, 4, 0), b)
    blocks = [(i, j) for i in range(0, half, 8) for j in range(0, width, lanes)]

    def total(acc):
        acc = functools.reduce(jnp.add, [acc[:, k : k + 128] for k in range(0, lanes, 128)])
        acc = acc + pltpu.roll(acc, 4, 0)
        return jnp.broadcast_to(jnp.sum(acc, axis=1, keepdims=True), (8, 128))

    def wide(value):
        return jnp.concatenate([value] * (lanes // 128), axis=1)

    def sweep(scale, last):
        zero = jnp.zeros((8, lanes), jnp.float32)
        crossed, energy, traced, fisher = zero, zero, zero, zero
        scale = wide(scale)
        for i, j in blocks:
            at = (slice(i, i + 8), slice(j, j + lanes))
            lam, resp, design = values_ref[at], r_ref[at], d_ref[at]
            v = scale * lam + 1.0
            inv = pl.reciprocal(v, approx=True)
            inv = inv * (2.0 - v * inv)
            over = design * inv
            crossed = crossed + over * resp
            energy = energy + over * design
            if not last:
                lev = lam * inv
                traced = traced + lev
                fisher = fisher + lev * lev
                w_ref[at] = lev * inv
        return total(crossed), total(energy) + EPSILON, traced, fisher

    log_scale = jnp.zeros((8, 128), jnp.float32)
    for _ in range(ITERS):
        scale = jnp.exp(log_scale)
        crossed, energy, traced, fisher = sweep(scale, False)
        effect = wide(crossed / energy)
        spread = jnp.zeros((8, lanes), jnp.float32)
        for i, j in blocks:
            at = (slice(i, i + 8), slice(j, j + lanes))
            residual = r_ref[at] - effect * d_ref[at]
            spread = spread + w_ref[at] * residual * residual
        gradient = 0.5 * (total(spread) - total(traced))
        log_scale = log_scale + jnp.tanh(gradient / (scale * (0.5 * total(fisher))))
    crossed, energy, _, _ = sweep(jnp.exp(log_scale), True)
    score = crossed / jnp.sqrt(energy)
    lane = lax.broadcasted_iota(jnp.int32, (8, 128), 1)
    row = lax.broadcasted_iota(jnp.int32, (8, 128), 0)
    here = (row < 4) & (lane == 4 * slot_ref[0] + row)
    both = [jnp.sum(jnp.where(here, v, 0.0), axis=0, keepdims=True) for v in (score, log_scale)]
    out_ref[...] = jnp.broadcast_to(
        jnp.concatenate(both, axis=1)[None], (out_ref.shape[0], 1, 256)
    )


def fit(slot, sums, values):
    rows, width = values.shape
    vmem = pl.BlockSpec(memory_space=pltpu.VMEM)
    return pl.pallas_call(
        fit_kernel,
        out_shape=jax.ShapeDtypeStruct((32, 1, 256), jnp.float32),
        in_specs=[pl.BlockSpec(memory_space=pltpu.SMEM), vmem, vmem],
        out_specs=vmem,
        scratch_shapes=[pltpu.VMEM((rows, width), jnp.float32)] * 3,
        compiler_params=pltpu.CompilerParams(vmem_limit_bytes=16 * 1024 * 1024),
    )(slot, sums, values)


def gather_plane(own, other):
    x, y = "samp_1", "samp_0"
    left = shifted(own, x, 1)
    right = shifted(own, x, -1)
    over = shifted(own, y, 1)
    floor = lax.axis_size(x)

    def across(value, by):
        pairs = [
            (floor * v + u, floor * (1 - v) + (u + by) % floor) for v in (0, 1) for u in range(floor)
        ]
        return lax.ppermute(value, (y, x), pairs)

    over_left = shifted(left, y, 1)
    over_far = across(left, 1)
    over_right = shifted(over, x, -1)
    far = shifted(right, x, -1)
    over_right = over_right + 0 * other[: own.shape[0]]
    return jnp.stack([over, left, far, right, own, over_left, over_far, over_right])


def smooth_block(widened, places, present, reaches):
    block_len = reaches.shape[0]
    centre = places[HALO : HALO + block_len]
    total_sum = jnp.zeros((block_len,), jnp.float32)
    norm_sum = jnp.zeros((block_len,), jnp.float32)
    for offset in range(2 * HALO + 1):
        near_scores = widened[offset : offset + block_len]
        near_places = places[offset : offset + block_len]
        within = (abs(offset - HALO) <= reaches).astype(jnp.float32)
        kernel = (
            present[offset : offset + block_len]
            * within
            * jnp.exp(-jnp.abs(near_places - centre) / band_width)
        )
        total_sum = total_sum + kernel * near_scores
        norm_sum = norm_sum + kernel
    return total_sum / norm_sum


def copies(value, axes):
    peers = lax.axis_size(axes)
    return lax.all_to_all(
        jnp.broadcast_to(value[None], (peers, *value.shape)), axes, 0, 0, tiled=True
    )


def shards(responses, weights, phenotype, eigvecs, eigvals, positions, reaches):
    z, x, y = lax.axis_index("cpg_0"), lax.axis_index("samp_1"), lax.axis_index("samp_0")
    layers = lax.axis_size("cpg_0")
    with jax.named_scope("swap_eigvecs"):
        other = shifted(eigvecs, "samp_2", 1)
        vecs = (eigvecs, other)
    with jax.named_scope("weigh"):
        own = weigh(responses, weights, phenotype, eigvals)
    with jax.named_scope("gather_rows"):
        blocks = gather_plane(own, other)
    rows = own.shape[0] - EXTRA

    def place(across, along):
        return (4 - 4 * (across ^ y) - (along - x) % 4) % 8

    with jax.named_scope("gather_values"):
        here = jnp.arange(8, dtype=jnp.int32)
        kept = place(here // 4, here % 4)[:, None] == here[None, :]
        parts = blocks[:, rows : rows + 3].astype(jnp.float32)
        parts = parts[:, 0] + parts[:, 1] + parts[:, 2]
        values = jnp.sum(jnp.where(kept[:, :, None], parts[None], 0.0), axis=1)
        values = jnp.concatenate([values, shifted(values, "samp_2", 1)], axis=1)
        everywhere = jnp.repeat(values, 4, axis=0)

    def term(q, ahead):
        dest = lax.rem(z + ahead + layers, layers)
        at = place(dest // 4, lax.rem(dest, 4))
        block = lax.dynamic_index_in_dim(blocks, at, 0, keepdims=False)[:rows]
        return jnp.dot(block, vecs[q], preferred_element_type=jnp.float32)

    far = layers // 2
    sent = {}

    def onward(q, way, ahead, behind=None):
        total = term(q, way * ahead)
        if (q, way) in sent:
            total = total + sent[q, way].astype(jnp.float32)
        if behind is not None:
            total = total + 0.0 * behind.astype(jnp.float32)
        total = total.astype(jnp.bfloat16)
        sent[q, way] = shifted(total, "cpg_0", way)
        return total

    def summed(q):
        total = term(q, 0)
        for way in (1, -1):
            total = total + sent[q, way].astype(jnp.float32)
        return total.astype(jnp.bfloat16)

    with jax.named_scope("sum_layers"):
        for ahead in range(far, 0, -1):
            onward(0, 1, ahead)
            behind = onward(1, -1, ahead)
            if ahead > 1:
                onward(0, -1, ahead - 1, behind)
                onward(1, 1, ahead - 1, behind)
        whole = jnp.concatenate([summed(0), summed(1)], axis=1)
    with jax.named_scope("to_components"):
        sums = lax.all_to_all(whole, PLANE, 0, 0, tiled=True)
    with jax.named_scope("fit"):
        slot = lax.axis_index("samp_2") * 16 + lax.axis_index(PLANE)
        fitted = fit(slot.astype(jnp.int32)[None], sums, everywhere)
    with jax.named_scope("gather_scores"):
        layer = jnp.sum(lax.all_to_all(fitted, LAYER, 0, 0, tiled=True), axis=(0, 1))
        beside = [(2 * i, 2 * i + 2) for i in range(layers - 1)]
        beside += [(2 * i + 3, 2 * i + 1) for i in range(layers - 1)]
        other = lax.ppermute(layer, CPG, beside)
        scores, scales = layer[:rows], layer[rows:]
        before, after = other[rows - HALO : rows], other[:HALO]
    with jax.named_scope("smooth"):
        block_len = reaches.shape[0]
        high = lax.axis_index("cpg_1")
        widened = lax.dynamic_slice_in_dim(
            jnp.concatenate([before, scores, after]), high * block_len, block_len + 2 * HALO, 0
        )
        log_scale = lax.dynamic_slice_in_dim(scales, high * block_len, block_len, 0)
        base = lax.axis_index(CPG) * block_len
        total_cpgs = block_len * lax.axis_size(CPG)
        places = lax.dynamic_slice_in_dim(
            jnp.pad(positions.astype(jnp.float32), HALO), base, block_len + 2 * HALO, 0
        )
        global_index = base - HALO + jnp.arange(block_len + 2 * HALO, dtype=jnp.int32)
        present = ((global_index >= 0) & (global_index < total_cpgs)).astype(jnp.float32)
        smoothed = smooth_block(widened, places, present, reaches)
    return (smoothed, log_scale)


def solution(mesh):
    split = Mesh(
        mesh.devices.reshape(2, 4, 2, 8, 2), ("samp_0", "samp_1", "samp_2", "cpg_0", "cpg_1")
    )
    return jax.shard_map(
        shards,
        mesh=split,
        in_specs=(P(SAMP, CPG), P(SAMP, CPG), P(CPG), P(CPG, SAMP), P(SAMP), P(), P(CPG)),
        out_specs=(P(CPG), P(CPG)),
        check_vma=False,
    )
```

```python
import functools

import jax
import jax.numpy as jnp
from jax import lax
from jax.experimental import pallas as pl
from jax.experimental.pallas import tpu as pltpu
from jax.sharding import Mesh
from jax.sharding import PartitionSpec as P

ITERS = 4
HALO = 8
SAMP = ("samp_0", "samp_1", "samp_2")
CPG = ("cpg_0", "cpg_1")
PLANE = ("cpg_1", "samp_0", "samp_1")
FLOOR = ("samp_0", "samp_1")
LAYER = ("cpg_1", "samp_0", "samp_1", "samp_2")

EPSILON = 1e-06
band_width = 1000.0


def shifted(value, axis, by):
    peers = lax.axis_size(axis)
    return lax.ppermute(value, axis, [(i, (i + by) % peers) for i in range(peers)])


EXTRA = 16


def weigh_kernel(resp_ref, weight_ref, trait_ref, values_ref, out_ref):
    trait = trait_ref[...]
    width = trait.shape[1]
    upper = lax.broadcasted_iota(jnp.int32, (8, width), 0) < 4
    for at in range(0, resp_ref.shape[0], 16):
        root = jnp.sqrt(weight_ref[at : at + 16, :].astype(jnp.float32))
        weighted = root * resp_ref[at : at + 16, :].astype(jnp.float32)
        design = root * trait
        tiles = []
        for half in (0, 8):
            a, b = weighted[half : half + 8], design[half : half + 8]
            tiles.append(jnp.where(upper, a, pltpu.roll(b, 4, 0)))
            tiles.append(jnp.where(upper, pltpu.roll(a, 4, 0), b))
        out_ref[2 * at : 2 * at + 32, :] = jnp.concatenate(tiles, axis=0).astype(jnp.bfloat16)
    rest = values_ref[...]
    row = lax.broadcasted_iota(jnp.int32, (EXTRA, width), 0)
    parts = jnp.zeros((EXTRA, width), jnp.float32)
    for k in range(3):
        part = rest.astype(jnp.bfloat16).astype(jnp.float32)
        parts = jnp.where(row == k, part, parts)
        rest = rest - part
    out_ref[out_ref.shape[0] - EXTRA :, :] = parts.astype(jnp.bfloat16)


def weigh(responses, weights, phenotype, eigvals):
    rows, width = responses.shape
    return pl.pallas_call(
        weigh_kernel,
        out_shape=pltpu.VMEM((2 * rows + EXTRA, width), jnp.bfloat16),
    )(responses, weights, phenotype[None, :], eigvals[None, :])


def fit_kernel(slot_ref, sums_ref, values_ref, out_ref, r_ref, d_ref, w_ref):
    half, width = values_ref.shape
    lanes = 512
    upper = lax.broadcasted_iota(jnp.int32, (8, width), 0) < 4
    for i in range(0, half, 8):
        pair = sums_ref[2 * i : 2 * i + 16, :].astype(jnp.float32) + sums_ref[
            2 * (half + i) : 2 * (half + i) + 16, :
        ].astype(jnp.float32)
        a, b = pair[:8], pair[8:]
        r_ref[i : i + 8, :] = jnp.where(upper, a, pltpu.roll(b, 4, 0))
        d_ref[i : i + 8, :] = jnp.where(upper, pltpu.roll(a, 4, 0), b)
    blocks = [(i, j) for i in range(0, half, 8) for j in range(0, width, lanes)]

    def total(acc):
        acc = functools.reduce(jnp.add, [acc[:, k : k + 128] for k in range(0, lanes, 128)])
        acc = acc + pltpu.roll(acc, 4, 0)
        return jnp.broadcast_to(jnp.sum(acc, axis=1, keepdims=True), (8, 128))

    def wide(value):
        return jnp.concatenate([value] * (lanes // 128), axis=1)

    def sweep(scale, last):
        zero = jnp.zeros((8, lanes), jnp.float32)
        crossed, energy, traced, fisher = zero, zero, zero, zero
        scale = wide(scale)
        for i, j in blocks:
            at = (slice(i, i + 8), slice(j, j + lanes))
            lam, resp, design = values_ref[at], r_ref[at], d_ref[at]
            v = scale * lam + 1.0
            inv = pl.reciprocal(v, approx=True)
            inv = inv * (2.0 - v * inv)
            over = design * inv
            crossed = crossed + over * resp
            energy = energy + over * design
            if not last:
                lev = lam * inv
                traced = traced + lev
                fisher = fisher + lev * lev
                w_ref[at] = lev * inv
        return total(crossed), total(energy) + EPSILON, traced, fisher

    log_scale = jnp.zeros((8, 128), jnp.float32)
    for _ in range(ITERS):
        scale = jnp.exp(log_scale)
        crossed, energy, traced, fisher = sweep(scale, False)
        effect = wide(crossed / energy)
        spread = jnp.zeros((8, lanes), jnp.float32)
        for i, j in blocks:
            at = (slice(i, i + 8), slice(j, j + lanes))
            residual = r_ref[at] - effect * d_ref[at]
            spread = spread + w_ref[at] * residual * residual
        gradient = 0.5 * (total(spread) - total(traced))
        log_scale = log_scale + jnp.tanh(gradient / (scale * (0.5 * total(fisher))))
    crossed, energy, _, _ = sweep(jnp.exp(log_scale), True)
    score = crossed / jnp.sqrt(energy)
    lane = lax.broadcasted_iota(jnp.int32, (8, 128), 1)
    row = lax.broadcasted_iota(jnp.int32, (8, 128), 0)
    here = (row < 4) & (lane == 4 * slot_ref[0] + row)
    both = [jnp.sum(jnp.where(here, v, 0.0), axis=0, keepdims=True) for v in (score, log_scale)]
    out_ref[...] = jnp.broadcast_to(
        jnp.concatenate(both, axis=1)[None], (out_ref.shape[0], 1, 256)
    )


def fit(slot, sums, values):
    rows, width = values.shape
    vmem = pl.BlockSpec(memory_space=pltpu.VMEM)
    return pl.pallas_call(
        fit_kernel,
        out_shape=jax.ShapeDtypeStruct((32, 1, 256), jnp.float32),
        in_specs=[pl.BlockSpec(memory_space=pltpu.SMEM), vmem, vmem],
        out_specs=vmem,
        scratch_shapes=[pltpu.VMEM((rows, width), jnp.float32)] * 3,
        compiler_params=pltpu.CompilerParams(vmem_limit_bytes=16 * 1024 * 1024),
    )(slot, sums, values)


def gather_plane(own, other):
    x, y = "samp_1", "samp_0"
    left = shifted(own, x, 1)
    right = shifted(own, x, -1)
    over = shifted(own, y, 1)
    floor = lax.axis_size(x)

    def across(value, by):
        pairs = [
            (floor * v + u, floor * (1 - v) + (u + by) % floor) for v in (0, 1) for u in range(floor)
        ]
        return lax.ppermute(value, (y, x), pairs)

    over_left = shifted(left, y, 1)
    over_far = across(right, -1)
    over_right = shifted(over, x, -1)
    far = shifted(left, x, 1)
    over_left = over_left + 0 * other[: own.shape[0]]
    return jnp.stack([over_far, over_right, over, left, far, right, own, over_left])


def smooth_block(widened, places, present, reaches):
    block_len = reaches.shape[0]
    centre = places[HALO : HALO + block_len]
    total_sum = jnp.zeros((block_len,), jnp.float32)
    norm_sum = jnp.zeros((block_len,), jnp.float32)
    for offset in range(2 * HALO + 1):
        near_scores = widened[offset : offset + block_len]
        near_places = places[offset : offset + block_len]
        within = (abs(offset - HALO) <= reaches).astype(jnp.float32)
        kernel = (
            present[offset : offset + block_len]
            * within
            * jnp.exp(-jnp.abs(near_places - centre) / band_width)
        )
        total_sum = total_sum + kernel * near_scores
        norm_sum = norm_sum + kernel
    return total_sum / norm_sum


def copies(value, axes):
    peers = lax.axis_size(axes)
    return lax.all_to_all(
        jnp.broadcast_to(value[None], (peers, *value.shape)), axes, 0, 0, tiled=True
    )


def shards(responses, weights, phenotype, eigvecs, eigvals, positions, reaches):
    z, x, y = lax.axis_index("cpg_0"), lax.axis_index("samp_1"), lax.axis_index("samp_0")
    layers = lax.axis_size("cpg_0")
    with jax.named_scope("swap_eigvecs"):
        other = shifted(eigvecs, "samp_2", 1)
        vecs = (eigvecs, other)
    with jax.named_scope("weigh"):
        own = weigh(responses, weights, phenotype, eigvals)
    with jax.named_scope("gather_rows"):
        blocks = gather_plane(own, other)
    rows = own.shape[0] - EXTRA

    def place(across, along):
        return (6 - 4 * (across ^ y) - (along - x) % 4) % 8

    with jax.named_scope("gather_values"):
        here = jnp.arange(8, dtype=jnp.int32)
        kept = place(here // 4, here % 4)[:, None] == here[None, :]
        parts = blocks[:, rows : rows + 3].astype(jnp.float32)
        parts = parts[:, 0] + parts[:, 1] + parts[:, 2]
        values = jnp.sum(jnp.where(kept[:, :, None], parts[None], 0.0), axis=1)
        values = jnp.concatenate([values, shifted(values, "samp_2", 1)], axis=1)
        everywhere = jnp.repeat(values, 4, axis=0)

    def term(q, ahead):
        dest = lax.rem(z + ahead + layers, layers)
        at = place(dest // 4, lax.rem(dest, 4))
        block = lax.dynamic_index_in_dim(blocks, at, 0, keepdims=False)[:rows]
        return jnp.dot(block, vecs[q], preferred_element_type=jnp.float32)

    far = layers // 2
    sent = {}

    def onward(q, way, ahead, behind=None):
        total = term(q, way * ahead)
        if (q, way) in sent:
            total = total + sent[q, way].astype(jnp.float32)
        if behind is not None:
            total = total + 0.0 * behind.astype(jnp.float32)
        total = total.astype(jnp.bfloat16)
        sent[q, way] = shifted(total, "cpg_0", way)
        return total

    with jax.named_scope("sum_layers"):
        for ahead in range(far, 0, -1):
            onward(0, 1, ahead)
            behind = onward(1, -1, ahead)
            if ahead > 1:
                onward(0, -1, ahead - 1, behind)
                onward(1, 1, ahead - 1, behind)
        def joined(first, second):
            return jnp.concatenate([first, second], axis=1).astype(jnp.float32)

        whole = joined(term(0, 0), term(1, 0))
        for way in (1, -1):
            whole = whole + joined(sent[0, way], sent[1, way])
        whole = whole.astype(jnp.bfloat16)
    with jax.named_scope("to_components"):
        sums = lax.all_to_all(whole, PLANE, 0, 0, tiled=True)
    with jax.named_scope("fit"):
        slot = lax.axis_index("samp_2") * 16 + lax.axis_index(PLANE)
        fitted = fit(slot.astype(jnp.int32)[None], sums, everywhere)
    with jax.named_scope("gather_scores"):
        layer = jnp.sum(lax.all_to_all(fitted, LAYER, 0, 0, tiled=True), axis=(0, 1))
        beside = [(2 * i, 2 * i + 2) for i in range(layers - 1)]
        beside += [(2 * i + 3, 2 * i + 1) for i in range(layers - 1)]
        other = lax.ppermute(layer, CPG, beside)
        scores, scales = layer[:rows], layer[rows:]
        before, after = other[rows - HALO : rows], other[:HALO]
    with jax.named_scope("smooth"):
        block_len = reaches.shape[0]
        high = lax.axis_index("cpg_1")
        widened = lax.dynamic_slice_in_dim(
            jnp.concatenate([before, scores, after]), high * block_len, block_len + 2 * HALO, 0
        )
        log_scale = lax.dynamic_slice_in_dim(scales, high * block_len, block_len, 0)
        base = lax.axis_index(CPG) * block_len
        total_cpgs = block_len * lax.axis_size(CPG)
        places = lax.dynamic_slice_in_dim(
            jnp.pad(positions.astype(jnp.float32), HALO), base, block_len + 2 * HALO, 0
        )
        global_index = base - HALO + jnp.arange(block_len + 2 * HALO, dtype=jnp.int32)
        present = ((global_index >= 0) & (global_index < total_cpgs)).astype(jnp.float32)
        smoothed = smooth_block(widened, places, present, reaches)
    return (smoothed, log_scale)


def solution(mesh):
    split = Mesh(
        mesh.devices.reshape(2, 4, 2, 8, 2), ("samp_0", "samp_1", "samp_2", "cpg_0", "cpg_1")
    )
    return jax.shard_map(
        shards,
        mesh=split,
        in_specs=(P(SAMP, CPG), P(SAMP, CPG), P(CPG), P(CPG, SAMP), P(SAMP), P(), P(CPG)),
        out_specs=(P(CPG), P(CPG)),
        check_vma=False,
    )
```
